32 devices in a mesh: wrap: 8 (over y, x, core), span: 4 (over z).
Axes of the slice: x: 2, y: 2, z: 4, core: 2. Of those that a mesh axis runs over, the one named last changes fastest.
Arguments:
- density: float32 [128, 16, 512], P('wrap', None, 'span'), may hold values from 0.8 to 1.2
- velocity: float32 [3, 128, 16, 512], P(None, 'wrap', None, 'span'), may hold values from -0.4 to 0.4
- pressure: float32 [128, 16, 512], P('wrap', None, 'span'), may hold values from 0.7 to 1.4
- metrics: float32 [9, 128, 16, 512], P(None, 'wrap', None, 'span'), may hold values from -0.3 to 0.3
- volume: float32 [128, 16, 512], P('wrap', None, 'span'), may hold values from 0.5 to 2
- wake_partner: int32 [128], P('wrap'), may hold values from 0 to 127, as said below
- iblank: int32 [128, 16, 512], P('wrap', None, 'span'), may hold values 0 or 1
Outputs:
- final_state: float32 [5, 128, 16, 512], P(None, 'wrap', None, 'span')
The draws below stay inside these ranges and needn't reach their ends.
Inputs may be any that keep to these rules, and one draw needn't show every extreme that they name: For i in i-slab s (rows s * 16 to (s + 1) * 16 - 1, s from 0), wake_partner[i] is one of the rows (n - 1 - s) * 16 to (n - s) * 16 - 1 with n = 8; each of those rows is named once.
All inputs are finite; a program needn't handle non-finite values. No bound on the sum of `iblank` on one device may be relied on, other than what follows from the above.
Results may differ from the reference program's by a relative error of at most 0.0003.
Values sent between devices are 32-bit elements; how exact they have to be, the bound alone decides.
No kernel may reach another device: no remote copies, remote signals or barrier semaphores. Data moves between devices by JAX's collectives and lax.ppermute only.
A program may use at most 64 MiB of HBM per device.

```python
import math
import jax
import jax.numpy as jnp
from jax import lax

CI = 16
J = 16
CK = 128
NI = 128
NK = 512


def draw_wake_partner(key, part):
    slabs = NI // CI
    slab_keys = jax.random.split(key, slabs)
    shuffled = jax.vmap(lambda one_key: jax.random.permutation(one_key, CI))(slab_keys).astype(jnp.int32)
    mirror_start = (slabs - 1 - jnp.arange(slabs, dtype=jnp.int32))[:, None] * CI
    return (mirror_start + shuffled).reshape(NI).astype(jnp.int32)


def with_ends(drawn, own_key, least, high):
    spot = [jax.random.randint(jax.random.fold_in(own_key, axis), (), 0, length) for axis, length in enumerate(drawn.shape)]
    widest = drawn.shape.index(max(drawn.shape))
    beside = spot[:widest] + [(spot[widest] + 1) % drawn.shape[widest]] + spot[widest + 1:]
    return drawn.at[tuple(spot)].set(least).at[tuple(beside)].set(high)


def block_levels(stream_key, extent, cuts, smallest, largest):
    level, own = 1.0, jax.random.fold_in(stream_key, 6)
    for dim, shards_of in cuts:
        steps = jnp.exp(jax.random.uniform(jax.random.fold_in(own, dim), (shards_of,), jnp.float32, smallest / len(cuts), largest / len(cuts)))
        level = level * jnp.repeat(steps, extent[dim] // shards_of).reshape([-1 if axis == dim else 1 for axis in range(len(extent))])
    return level


def setup_inputs(seed: int = 0) -> dict:
    keys = jax.random.split(jax.random.key(seed), 8)
    density = jnp.clip(0.8 + 0.40000004 * jax.random.uniform(keys[0], (NI, J, NK), jnp.float32) ** block_levels(keys[0], (NI, J, NK), ((0, 8), (2, 4)), -0.2, 0.2), 0.8, 1.2)
    velocity = jnp.clip(jax.random.uniform(keys[1], (3, NI, J, NK), jnp.float32, -0.4, 0.4) * block_levels(keys[1], (3, NI, J, NK), ((1, 8), (3, 4)), -0.4, 0.0), -0.4, 0.4)
    pressure = jnp.clip(0.7 + 0.7 * jax.random.uniform(keys[2], (NI, J, NK), jnp.float32) ** block_levels(keys[2], (NI, J, NK), ((0, 8), (2, 4)), -0.2, 0.2), 0.7, 1.4)
    metrics = jnp.clip(jax.random.uniform(keys[3], (9, NI, J, NK), jnp.float32, -0.3, 0.3) * block_levels(keys[3], (9, NI, J, NK), ((1, 8), (3, 4)), -0.4, 0.0), -0.3, 0.3)
    volume = jnp.clip(jnp.exp(math.log(2.0) - 1.3862944 * jax.random.uniform(keys[4], (NI, J, NK), jnp.float32) ** block_levels(keys[4], (NI, J, NK), ((0, 8), (2, 4)), -0.2, 0.2)), 0.5, 2.0)
    wake_partner = draw_wake_partner(jax.random.fold_in(keys[7], 71), 0)
    iblank = with_ends((jax.random.randint(keys[6], (NI, J, NK), 0, 8) < 7).astype(jnp.int32), jax.random.fold_in(keys[6], 1), 0, 1)
    return {"density": density, "velocity": velocity, "pressure": pressure, "metrics": metrics, "volume": volume, "wake_partner": wake_partner, "iblank": iblank}


epsilon = 1e-06
viscosity = 0.8
conduction = 1.0
time_step = 0.05

def window(array, start, length, array_dim):
    return lax.slice_in_dim(array, start, start + length, axis=array_dim)

def reconstruct(first, second, third, fourth, fifth):
    guess_left = (2.0 * first - 7.0 * second + 11.0 * third) / 6.0
    guess_mid = (-second + 5.0 * third + 2.0 * fourth) / 6.0
    guess_right = (2.0 * third + 5.0 * fourth - fifth) / 6.0
    smooth_left = 13.0 / 12.0 * (first - 2.0 * second + third) ** 2 + 0.25 * (first - 4.0 * second + 3.0 * third) ** 2
    smooth_mid = 13.0 / 12.0 * (second - 2.0 * third + fourth) ** 2 + 0.25 * (second - fourth) ** 2
    smooth_right = 13.0 / 12.0 * (third - 2.0 * fourth + fifth) ** 2 + 0.25 * (3.0 * third - 4.0 * fourth + fifth) ** 2
    weight_left = 0.1 / (epsilon + smooth_left) ** 2
    weight_mid = 0.6 / (epsilon + smooth_mid) ** 2
    weight_right = 0.3 / (epsilon + smooth_right) ** 2
    return (weight_left * guess_left + weight_mid * guess_mid + weight_right * guess_right) / (weight_left + weight_mid + weight_right)

def divergence(state, metric_row, array_dim):
    cells = state.shape[array_dim] - 6
    faces = cells + 1
    density = state[0:1]
    velocity = state[1:4] / density
    speed_sq = lax.optimization_barrier(jnp.sum(velocity * velocity, axis=0, keepdims=True))
    pressure = 0.4 * (state[4:5] - 0.5 * density * speed_sq)
    contra = lax.optimization_barrier(jnp.sum(metric_row * velocity, axis=0, keepdims=True))
    metric_sq = lax.optimization_barrier(jnp.sum(metric_row * metric_row, axis=0, keepdims=True))
    wave_speed = jnp.abs(contra) + jnp.sqrt(1.4 * pressure / density * metric_sq)
    fluxes = jnp.concatenate([density * contra, state[1:4] * contra + metric_row * pressure, (state[4:5] + pressure) * contra], axis=0)
    split_plus = 0.5 * (fluxes + wave_speed * state)
    split_minus = 0.5 * (fluxes - wave_speed * state)
    inviscid = reconstruct(window(split_plus, 0, faces, array_dim), window(split_plus, 1, faces, array_dim), window(split_plus, 2, faces, array_dim), window(split_plus, 3, faces, array_dim), window(split_plus, 4, faces, array_dim))
    inviscid = inviscid + reconstruct(window(split_minus, 5, faces, array_dim), window(split_minus, 4, faces, array_dim), window(split_minus, 3, faces, array_dim), window(split_minus, 2, faces, array_dim), window(split_minus, 1, faces, array_dim))
    heat = 0.5 * speed_sq + conduction * pressure / density
    diffused = jnp.concatenate([velocity, heat], axis=0)
    face_metric = 0.5 * (window(metric_sq, 2, faces, array_dim) + window(metric_sq, 3, faces, array_dim))
    viscous = viscosity * face_metric * (window(diffused, 3, faces, array_dim) - window(diffused, 2, faces, array_dim))
    net_flux = jnp.concatenate([-inviscid[0:1], viscous - inviscid[1:5]], axis=0)
    return window(net_flux, 1, cells, array_dim) - window(net_flux, 0, cells, array_dim)

def identity_row(which):
    return jnp.eye(3, dtype=jnp.float32)[which][:, None, None, None]

def conserved(density, velocity, pressure):
    speed_sq = lax.optimization_barrier(jnp.sum(velocity * velocity, axis=0))
    return jnp.concatenate([density[None], density[None] * velocity, (pressure / 0.4 + 0.5 * density * speed_sq)[None]], axis=0)

def pad_normal(state, partner):
    wake_rows = state[:, :, 1:4, :]
    below = jnp.take(wake_rows, partner, axis=1)[:, :, ::-1, :]
    above = jnp.broadcast_to(state[:, :, -1:, :], below.shape)
    return jnp.concatenate([below, state, above], axis=2)

def span_wrap(array):
    return jnp.concatenate([array[..., -3:], array, array[..., :3]], axis=-1)

def edge_pad(array, array_dim):
    widths = [(0, 0)] * array.ndim
    widths[array_dim] = (3, 3)
    return jnp.pad(array, widths, mode='edge')

def reference(density, velocity, pressure, metrics, volume, wake_partner, iblank):
    state0 = conserved(density, velocity, pressure)
    row_chord = span_wrap(metrics[0:3] + identity_row(0))
    row_normal = span_wrap(metrics[3:6] + identity_row(1))
    row_span = span_wrap(metrics[6:9] + identity_row(2))
    mask = iblank.astype(jnp.float32)[None]
    blocks = NK // CK

    def full_rhs(state):
        wrapped = span_wrap(state)

        def block_rhs(block_id):
            start = (block_id * CK).astype(jnp.int32)
            piece = lax.dynamic_slice_in_dim(wrapped, start, CK + 6, 3)
            center = piece[..., 3:-3]
            padded_chord = edge_pad(center, 1)
            padded_normal = pad_normal(center, wake_partner)
            metric_chord = edge_pad(lax.dynamic_slice_in_dim(row_chord, start, CK + 6, 3)[..., 3:-3], 1)
            metric_normal = edge_pad(lax.dynamic_slice_in_dim(row_normal, start, CK + 6, 3)[..., 3:-3], 2)
            metric_span = lax.dynamic_slice_in_dim(row_span, start, CK + 6, 3)
            cell_volume = lax.dynamic_slice_in_dim(volume, start, CK, 2)
            total = divergence(padded_chord, metric_chord, 1) + divergence(padded_normal, metric_normal, 2) + divergence(piece, metric_span, 3)
            return total / cell_volume[None]
        stacked = lax.map(block_rhs, jnp.arange(blocks, dtype=jnp.int32))
        return jnp.transpose(stacked, (1, 2, 3, 0, 4)).reshape(5, NI, J, NK)
    state1 = state0 + time_step * mask * full_rhs(state0)
    return 0.5 * state0 + 0.5 * (state1 + time_step * mask * full_rhs(state1))
```

```python
import functools

import jax
import jax.numpy as jnp
from jax import lax
from jax.experimental import pallas as pl
from jax.experimental.pallas import tpu as pltpu
from jax.sharding import PartitionSpec as P

epsilon = 1e-06
viscosity = 0.8
conduction = 1.0
time_step = 0.05
H = 3
F32 = jnp.float32


def point_fluxes(state, row):
    rho, m0, m1, m2, energy = state
    x0, x1, x2 = row
    inverse = 1.0 / rho
    u0, u1, u2 = m0 * inverse, m1 * inverse, m2 * inverse
    speed_sq = u0 * u0 + u1 * u1 + u2 * u2
    pressure = 0.4 * (energy - 0.5 * rho * speed_sq)
    ratio = pressure * inverse
    contra = x0 * u0 + x1 * u1 + x2 * u2
    metric_sq = x0 * x0 + x1 * x1 + x2 * x2
    sound_sq = 1.4 * ratio * metric_sq
    speed = jnp.abs(contra) + sound_sq * lax.rsqrt(jnp.maximum(sound_sq, 1e-30))
    fluxes = (
        rho * contra,
        m0 * contra + x0 * pressure,
        m1 * contra + x1 * pressure,
        m2 * contra + x2 * pressure,
        (energy + pressure) * contra,
    )
    waves = [speed * one for one in state]
    plus = [a + b for a, b in zip(fluxes, waves)]
    minus = [a - b for a, b in zip(fluxes, waves)]
    diffused = (u0, u1, u2, 0.5 * speed_sq + conduction * ratio)
    return plus, minus, diffused, metric_sq


class Split:
    def __init__(self, load):
        self.load, self.memo = load, {}

    def get(self, name, n):
        if (name, n) not in self.memo:
            self.memo[name, n] = getattr(self, "make_" + name)(n)
        return self.memo[name, n]

    def make_v(self, n):
        return self.load(n)

    def make_d(self, n):
        return self.get("v", n + 1) - self.get("v", n)

    def make_e(self, n):
        return self.get("d", n) - self.get("d", n - 1)

    def make_t(self, n):
        return self.get("e", n + 1) - self.get("e", n)

    def make_t2(self, n):
        return self.get("t", n) + self.get("t", n)

    def make_smooth(self, n):
        high, low, bend = self.get("d", n), self.get("d", n - 1), self.get("e", n)
        twice = bend + bend
        a, b = high * twice, low * twice
        centre = (a - b) * (2.0 / 3.0) + (high * low + 16.0 * epsilon / 3.0)
        return centre + a, centre, centre - b

    def correction(self, outer, middle, inner, near, far):
        left = middle * pl.reciprocal(outer, approx=True)
        right = middle * pl.reciprocal(inner, approx=True)
        weight_left = left * left * (1.0 / 3.0)
        weight_right = right * right
        total = (weight_left + weight_right) + 2.0
        return (weight_left * near + weight_right * far) * pl.reciprocal(total, approx=True)


def sweep(load_plus, load_minus, load_diffused, load_metric, store, first, last):
    plus, minus = Split(load_plus), Split(load_minus)
    central, diffused, metric = {}, {}, {}

    def flux_centre(n):
        if n not in central:
            both = plus.get("v", n) + minus.get("v", n)
            central[n] = 6.0 * both - (plus.get("e", n) + minus.get("e", n))
        return central[n]

    def cached(table, load, n):
        if n not in table:
            table[n] = load(n)
        return table[n]

    before = None
    for n in range(first, last + 1):
        up = plus.correction(
            plus.get("smooth", n - 1)[0],
            plus.get("smooth", n)[1],
            plus.get("smooth", n + 1)[2],
            plus.get("t2", n - 1),
            plus.get("t", n),
        )
        down = minus.correction(
            minus.get("smooth", n + 2)[2],
            minus.get("smooth", n + 1)[1],
            minus.get("smooth", n)[0],
            minus.get("t2", n + 1),
            minus.get("t", n),
        )
        correction = down - up
        flux = flux_centre(n) + flux_centre(n + 1) + (plus.get("t", n) - minus.get("t", n))
        flux = flux + (correction + correction)
        face_metric = cached(metric, load_metric, n) + cached(metric, load_metric, n + 1)
        jump = cached(diffused, load_diffused, n + 1) - cached(diffused, load_diffused, n)
        net = face_metric * jump - flux
        if before is not None:
            store(n, net - before)
        before = net


class Lines:
    def __init__(self, plus, minus, diffused, metric, width):
        self.refs, self.width = (plus, minus, diffused, metric), width

    def rows(self, n, count):
        return pl.ds(pl.multiple_of((n + H) * self.width, 8), count)

    def put(self, n, count, state, row):
        plus_ref, minus_ref, diffused_ref, metric_ref = self.refs
        plus, minus, diffused, metric_sq = point_fluxes(state, row)
        rows = self.rows(n, count)
        for f in range(5):
            plus_ref[f, rows, :] = plus[f]
            minus_ref[f, rows, :] = minus[f]
        for m in range(4):
            diffused_ref[1 + m, rows, :] = diffused[m]
        metric_ref[rows, :] = metric_sq * (24.0 * viscosity * 0.5)

    def copy(self, n, source):
        plus_ref, minus_ref, diffused_ref, metric_ref = self.refs
        to, origin = self.rows(n, self.width), self.rows(source, self.width)
        for ref in (plus_ref, minus_ref, diffused_ref):
            ref[:, to, :] = ref[:, origin, :]
        metric_ref[to, :] = metric_ref[origin, :]

    def zero_diffused(self):
        self.refs[2][0] = jnp.zeros(self.refs[2].shape[1:], F32)

    def sweep(self, f, tile, store, first, last):
        def loader(ref, lead):
            return lambda n: ref[lead + (pl.ds(pl.multiple_of((n + H) * self.width + tile * 8, 8), 8), slice(None))]

        plus_ref, minus_ref, diffused_ref, metric_ref = self.refs
        sweep(
            loader(plus_ref, (f,)),
            loader(minus_ref, (f,)),
            loader(diffused_ref, (f,)),
            loader(metric_ref, ()),
            store,
            first,
            last,
        )


def to_span(value, put, height):
    for half in range(2):
        turned = value[half * 128 : (half + 1) * 128].T
        for q in range(4):
            put(q * 2 + half, turned[q * height : (q + 1) * height])


def send_parts(state_ref, span_ref, fields, outs, dims):
    rows_i, height = dims
    low_ref, high_ref, wake_ref, span_low_ref, span_high_ref = outs
    total = rows_i * rows_i
    for f in range(5):
        low_ref[f] = state_ref[f, 0 : H * rows_i, :]
        high_ref[f] = state_ref[f, total - H * rows_i : total, :]
        for r in range(H):
            wake_ref[pl.ds(f * H + r, rows_i, stride=16), :] = state_ref[f, pl.ds(r + 1, rows_i, stride=rows_i), :]
    for f in range(fields):
        for r in range(H):
            span_low_ref[f, 2 * r : 2 * r + 2, :] = span_ref[f, r * 8 : r * 8 + 2, :]
            top = (height - H + r) * 8
            span_high_ref[f, 2 * r : 2 * r + 2, :] = span_ref[f, top + 6 : top + 8, :]


def prepare_kernel(dims, rho_ref, vel_ref, pre_ref, met_ref, state_ref, span_ref, *outs):
    rows_i, height = dims
    total = rows_i * rows_i
    rho, pressure = rho_ref[...], pre_ref[...]
    u = [vel_ref[m] for m in range(3)]
    speed_sq = u[0] * u[0] + u[1] * u[1] + u[2] * u[2]
    state_ref[0] = rho
    for m in range(3):
        state_ref[1 + m] = rho * u[m]
    state_ref[4] = pressure * (1.0 / 0.4) + 0.5 * rho * speed_sq
    low_ref, high_ref = outs[:2]
    for m in range(3):
        low_ref[5 + m] = met_ref[m, 0 : H * rows_i, :]
        high_ref[5 + m] = met_ref[m, total - H * rows_i : total, :]
    for f in range(8):
        value = state_ref[f] if f < 5 else met_ref[6 + f - 5]

        def put(start, block, f=f):
            span_ref[f, pl.ds(start, height, stride=8), :] = block

        to_span(value, put, height)
    send_parts(state_ref, span_ref, 8, outs, dims)


def unit(which, m, value):
    return value + 1.0 if which == m else value


def stage_kernel(dims, final, *refs):
    rows_i, height = dims
    total = rows_i * rows_i
    size_in = 13
    (state_ref, span_ref, span_met_ref, met_ref, vol_ref, blank_ref, partner_ref,
     low_ref, high_ref, met_low_ref, met_high_ref, wake_ref, span_low_ref, span_high_ref) = refs[:14]
    refs = refs[14:]
    if final:
        start_ref, out_ref = refs[:2]
        refs = refs[2:]
    else:
        out_ref, out_span_ref = refs[:2]
        outs = refs[2:7]
        refs = refs[7:]
    acc_ref, acc_span_ref, plus_ref, minus_ref, diffused_ref, metric_ref, ghost_ref, pad_ref, pad_met_ref = refs

    position, count = lax.axis_index("wrap"), lax.axis_size("wrap")
    is_first, is_last = position == 0, position == count - 1

    lines = Lines(plus_ref, minus_ref, diffused_ref, metric_ref, 8)
    lines.zero_diffused()
    def interior_span(step, carry):
        rows = pl.ds(pl.multiple_of(step * 16, 16), 16)
        lines.put(2 * step, 16, [span_ref[f, rows, :] for f in range(5)],
                  [unit(2, m, span_met_ref[5 + m, rows, :]) for m in range(3)])
        return carry

    lax.fori_loop(0, height // 2, interior_span, 0)
    sublane = lax.broadcasted_iota(jnp.int32, (8, 128), 0)
    for r in range(H):
        for f in range(8):
            pad_ref[f, r * 8 : r * 8 + 2, :] = (span_low_ref[f, 2 * r : 2 * r + 2, :])
            pad_ref[f, (H + r) * 8 + 6 : (H + r) * 8 + 8, :] = span_high_ref[f, 2 * r : 2 * r + 2, :]
    for r in range(H):
        def joined(low):
            values = []
            for f in range(8):
                ref = span_ref if f < 5 else span_met_ref
                if low:
                    own = pltpu.roll(ref[f, (height - H + r) * 8 : (height - H + r) * 8 + 8, :], 2, 0)
                    values.append(jnp.where(sublane < 2, pad_ref[f, r * 8 : r * 8 + 8, :], own))
                else:
                    own = pltpu.roll(ref[f, r * 8 : r * 8 + 8, :], 6, 0)
                    values.append(jnp.where(sublane >= 6, pad_ref[f, (H + r) * 8 : (H + r) * 8 + 8, :], own))
            return values[:5], [unit(2, m, values[5 + m]) for m in range(3)]

        lines.put(r - H, 8, *joined(True))
        lines.put(height + r, 8, *joined(False))

    def span_sweep(f, carry):
        def store(n, value):
            acc_span_ref[f, n * 8 : n * 8 + 8, :] = value

        lines.sweep(f, 0, store, -1, height - 1)
        return carry

    lax.fori_loop(0, 5, span_sweep, 0)
    for f in range(5):
        for half in range(2):
            parts = [acc_span_ref[f, pl.ds(q * 2 + half, height, stride=8), :] for q in range(4)]
            acc_ref[f, half * 128 : (half + 1) * 128, :] = jnp.concatenate(parts, axis=0).T

    lines = Lines(plus_ref, minus_ref, diffused_ref, metric_ref, rows_i)

    def interior_chord(n, carry):
        rows = pl.ds(pl.multiple_of(n * rows_i, 16), rows_i)
        lines.put(n, rows_i, [state_ref[f, rows, :] for f in range(5)],
                  [unit(0, m, met_ref[m, rows, :]) for m in range(3)])
        return carry

    lax.fori_loop(0, rows_i, interior_chord, 0)
    for r in range(H):
        rows = slice(r * rows_i, (r + 1) * rows_i)
        edge = slice(0, rows_i)
        lines.put(
            r - H, rows_i,
            [jnp.where(is_first, state_ref[f, edge, :], low_ref[f, rows, :]) for f in range(5)],
            [unit(0, m, jnp.where(is_first, met_ref[m, edge, :], met_low_ref[5 + m, rows, :])) for m in range(3)],
        )
        edge = slice(total - rows_i, total)
        lines.put(
            rows_i + r, rows_i,
            [jnp.where(is_last, state_ref[f, edge, :], high_ref[f, rows, :]) for f in range(5)],
            [unit(0, m, jnp.where(is_last, met_ref[m, edge, :], met_high_ref[5 + m, rows, :])) for m in range(3)],
        )

    def chord_sweep(step, carry):
        f, tile = step // 2, step % 2

        def store(n, value):
            rows = pl.ds(pl.multiple_of(n * rows_i + tile * 8, 8), 8)
            acc_ref[f, rows, :] = acc_ref[f, rows, :] + value

        lines.sweep(f, tile, store, -1, rows_i - 1)
        return carry

    lax.fori_loop(0, 10, chord_sweep, 0)

    def interior_normal(n, carry):
        rows = pl.ds(n, rows_i, stride=rows_i)
        lines.put(n, rows_i, [state_ref[f, rows, :] for f in range(5)],
                  [unit(1, m, met_ref[3 + m, rows, :]) for m in range(3)])
        return carry

    lax.fori_loop(0, rows_i, interior_normal, 0)
    base = (count - 1 - position) * rows_i
    for i in range(rows_i):
        ghost_ref[i * 16 : i * 16 + 16, :] = wake_ref[pl.ds(pl.multiple_of((partner_ref[i] - base) * 16, 16), 16), :]
    wall = pl.ds(0, rows_i, stride=rows_i)
    for r in range(H):
        lines.put(-1 - r, rows_i, [ghost_ref[pl.ds(f * H + r, rows_i, stride=16), :] for f in range(5)],
                  [unit(1, m, met_ref[3 + m, wall, :]) for m in range(3)])
        lines.copy(rows_i + r, rows_i - 1)

    def normal_sweep(step, carry):
        f, tile = step // 2, step % 2

        def store(n, value):
            rows = pl.ds(tile * 8 * rows_i + n, 8, stride=rows_i)
            acc_ref[f, rows, :] = acc_ref[f, rows, :] + value

        lines.sweep(f, tile, store, -1, rows_i - 1)
        return carry

    lax.fori_loop(0, 10, normal_sweep, 0)

    scale = (time_step / 24.0) * blank_ref[...].astype(F32) / vol_ref[...]
    for f in range(5):
        moved = state_ref[f] + scale * acc_ref[f]
        out_ref[f] = 0.5 * start_ref[f] + 0.5 * moved if final else moved
    if not final:
        for f in range(5):
            def put(start, block, f=f):
                out_span_ref[f, pl.ds(start, height, stride=8), :] = block

            to_span(out_ref[f], put, height)
        send_parts(out_ref, out_span_ref, 5, outs, dims)


def shape(*sizes):
    return jax.ShapeDtypeStruct(sizes, F32)


def body(density, velocity, pressure, metrics, volume, wake_partner, iblank):
    rows_i, rows_j, lanes = density.shape
    total, height = rows_i * rows_j, lanes // 4
    dims = (rows_i, height)
    metrics = metrics.reshape(9, total, lanes)
    volume, blank = volume.reshape(total, lanes), iblank.reshape(total, lanes)
    whole = pl.BlockSpec(memory_space=pltpu.VMEM)
    params = pltpu.CompilerParams(vmem_limit_bytes=40 * 2**20)

    def parts(fields):
        edge = H * rows_j
        return [shape(fields, edge, lanes), shape(fields, edge, lanes), shape(rows_i * 16, lanes),
                shape(fields, 8, lanes), shape(fields, 8, lanes)]

    def exchange(sent):
        low, high, wake, span_low, span_high = sent
        n, s = lax.axis_size("wrap"), lax.axis_size("span")
        up = [(i, i + 1) for i in range(n - 1)]
        down = [(i + 1, i) for i in range(n - 1)]
        mirror = [(i, n - 1 - i) for i in range(n)]
        ring_up = [(i, (i + 1) % s) for i in range(s)]
        ring_down = [((i + 1) % s, i) for i in range(s)]
        return (lax.ppermute(high, "wrap", up), lax.ppermute(low, "wrap", down), lax.ppermute(wake, "wrap", mirror),
                lax.ppermute(span_high, "span", ring_up), lax.ppermute(span_low, "span", ring_down))

    state, span, *sent = pl.pallas_call(
        functools.partial(prepare_kernel, dims),
        out_shape=[shape(5, total, lanes), shape(8, total, lanes)] + parts(8),
        in_specs=[whole] * 4,
        out_specs=[whole] * 7,
        compiler_params=params,
        name="prepare",
    )(density.reshape(total, lanes), velocity.reshape(3, total, lanes), pressure.reshape(total, lanes), metrics)
    below, above, wake, span_below, span_above = exchange(sent)

    points = (rows_i + 2 * H) * rows_i
    scratch = [pltpu.VMEM((5, total, lanes), F32), pltpu.VMEM((5, total, lanes), F32)]
    scratch += [pltpu.VMEM((5, points, lanes), F32)] * 3 + [pltpu.VMEM((points, lanes), F32)]
    scratch += [pltpu.VMEM((rows_i * 16, lanes), F32), pltpu.VMEM((8, 6 * 8, lanes), F32), pltpu.VMEM((8, 128), F32)]
    smem = pl.BlockSpec(memory_space=pltpu.SMEM)
    in_specs = [whole] * 6 + [smem] + [whole] * 7

    moved, moved_span, *sent = pl.pallas_call(
        functools.partial(stage_kernel, dims, False),
        out_shape=[shape(5, total, lanes), shape(5, total, lanes)] + parts(5),
        in_specs=in_specs,
        out_specs=[whole] * 7,
        scratch_shapes=scratch,
        compiler_params=params,
        name="first_section",
    )(state, span, span, metrics, volume, blank, wake_partner, below, above, below, above, wake, span_below, span_above)
    below2, above2, wake, span_below2, span_above2 = exchange(sent)
    grow = lambda new, old: jnp.concatenate([new, old[5:]], axis=0)
    (result,) = pl.pallas_call(
        functools.partial(stage_kernel, dims, True),
        out_shape=[shape(5, total, lanes)],
        in_specs=in_specs + [whole],
        out_specs=[whole],
        scratch_shapes=scratch,
        compiler_params=params,
        name="second_section",
    )(moved, moved_span, span, metrics, volume, blank, wake_partner, below2, above2, below, above, wake,
      grow(span_below2, span_below), grow(span_above2, span_above), state)
    return result.reshape(5, rows_i, rows_j, lanes)


def solution(mesh):
    placed = (
        P("wrap", None, "span"),
        P(None, "wrap", None, "span"),
        P("wrap", None, "span"),
        P(None, "wrap", None, "span"),
        P("wrap", None, "span"),
        P("wrap"),
        P("wrap", None, "span"),
    )
    return jax.shard_map(
        body, mesh=mesh, in_specs=placed, out_specs=P(None, "wrap", None, "span"), check_vma=False
    )
```

```python
import functools

import jax
import jax.numpy as jnp
from jax import lax
from jax.experimental import pallas as pl
from jax.experimental.pallas import tpu as pltpu
from jax.sharding import PartitionSpec as P

epsilon = 1e-06
viscosity = 0.8
conduction = 1.0
time_step = 0.05
H = 3
F32 = jnp.float32


def primitives(state):
    rho, m0, m1, m2, energy = state
    inverse = 1.0 / rho
    velocity = (m0 * inverse, m1 * inverse, m2 * inverse)
    speed_sq = velocity[0] * velocity[0] + velocity[1] * velocity[1] + velocity[2] * velocity[2]
    pressure = 0.4 * (energy - 0.5 * rho * speed_sq)
    ratio = pressure * inverse
    heat = 0.5 * speed_sq + conduction * ratio
    return velocity, pressure, energy + pressure, 1.4 * ratio, heat


def point_fluxes(state, prims, row):
    rho, m0, m1, m2, _ = state
    (u0, u1, u2), pressure, enthalpy, sound_sq, _ = prims
    x0, x1, x2 = row
    contra = x0 * u0 + x1 * u1 + x2 * u2
    metric_sq = x0 * x0 + x1 * x1 + x2 * x2
    square = sound_sq * metric_sq
    speed = jnp.abs(contra) + square * lax.rsqrt(jnp.maximum(square, 1e-30))
    fluxes = (
        rho * contra,
        m0 * contra + x0 * pressure,
        m1 * contra + x1 * pressure,
        m2 * contra + x2 * pressure,
        enthalpy * contra,
    )
    waves = [speed * one for one in state]
    plus = [a + b for a, b in zip(fluxes, waves)]
    minus = [a - b for a, b in zip(fluxes, waves)]
    return plus, minus, metric_sq * (24.0 * viscosity * 0.5)


class Split:
    def __init__(self, load):
        self.load, self.memo = load, {}

    def get(self, name, n):
        if (name, n) not in self.memo:
            self.memo[name, n] = getattr(self, "make_" + name)(n)
        return self.memo[name, n]

    def make_v(self, n):
        return self.load(n)

    def make_d(self, n):
        return self.get("v", n + 1) - self.get("v", n)

    def make_e(self, n):
        return self.get("d", n) - self.get("d", n - 1)

    def make_t(self, n):
        return self.get("e", n + 1) - self.get("e", n)

    def make_t2(self, n):
        return self.get("t", n) + self.get("t", n)

    def make_smooth(self, n):
        high, low, bend = self.get("d", n), self.get("d", n - 1), self.get("e", n)
        twice = bend + bend
        a, b = high * twice, low * twice
        centre = (a - b) * (2.0 / 3.0) + (high * low + 16.0 * epsilon / 3.0)
        return centre + a, centre, centre - b

    def correction(self, outer, middle, inner, near, far):
        left = middle * pl.reciprocal(outer, approx=True)
        right = middle * pl.reciprocal(inner, approx=True)
        weight_left = left * left * (1.0 / 3.0)
        weight_right = right * right
        total = (weight_left + weight_right) + 2.0
        return (weight_left * near + weight_right * far) * pl.reciprocal(total, approx=True)


def sweep(load_plus, load_minus, load_diffused, load_metric, store, first, last, open_low=False, open_high=False):
    plus, minus = Split(load_plus), Split(load_minus)
    central, diffused, metric = {}, {}, {}

    def flux_centre(n):
        if n not in central:
            both = plus.get("v", n) + minus.get("v", n)
            central[n] = 6.0 * both - (plus.get("e", n) + minus.get("e", n))
        return central[n]

    def cached(table, load, n):
        if n not in table:
            table[n] = load(n)
        return table[n]

    before = None
    for n in range(first, last + 1):
        up = plus.correction(
            plus.get("smooth", n - 1)[0],
            plus.get("smooth", n)[1],
            plus.get("smooth", n + 1)[2],
            plus.get("t2", n - 1),
            plus.get("t", n),
        )
        down = minus.correction(
            minus.get("smooth", n + 2)[2],
            minus.get("smooth", n + 1)[1],
            minus.get("smooth", n)[0],
            minus.get("t2", n + 1),
            minus.get("t", n),
        )
        correction = down - up
        flux = flux_centre(n) + flux_centre(n + 1) + (plus.get("t", n) - minus.get("t", n))
        flux = flux + (correction + correction)
        face_metric = cached(metric, load_metric, n) + cached(metric, load_metric, n + 1)
        jump = cached(diffused, load_diffused, n + 1) - cached(diffused, load_diffused, n)
        net = face_metric * jump - flux
        if before is not None:
            store(n, net - before)
        elif open_low:
            store(n, net)
        before = net
    if open_high:
        store(last + 1, -before)


def put(refs, rows, plus, minus, metric=None):
    plus_ref, minus_ref, metric_ref = refs
    for f in range(5):
        plus_ref[f, rows, :] = plus[f]
        minus_ref[f, rows, :] = minus[f]
    if metric is not None:
        metric_ref[rows, :] = metric


def put_diffused(ref, rows, prims):
    for m in range(3):
        ref[1 + m, rows, :] = prims[0][m]
    ref[4, rows, :] = prims[4]


def aligned(start, count):
    return pl.ds(pl.multiple_of(start, 8), count)


def unit(which, m, value):
    return value + 1.0 if which == m else value


def to_span(value, store, height):
    for half in range(2):
        turned = value[half * 128 : (half + 1) * 128].T
        for q in range(4):
            store(q * 2 + half, turned[q * height : (q + 1) * height])


def send_parts(state_ref, span_ref, fields, outs, dims):
    rows_i, height = dims
    total = rows_i * rows_i
    core_ref, chip_ref, wake_ref, span_low_ref, span_high_ref = outs
    even = lax.rem(lax.axis_index("wrap"), 2) == 0
    edge = H * rows_i
    to_core, to_chip = jnp.where(even, total - edge, 0), jnp.where(even, 0, total - edge)
    for f in range(5):
        core_ref[f] = state_ref[f, aligned(to_core, edge), :]
        chip_ref[f] = state_ref[f, aligned(to_chip, edge), :]
        for r in range(H):
            wake_ref[pl.ds(f * H + r, rows_i, stride=16), :] = state_ref[f, pl.ds(r + 1, rows_i, stride=rows_i), :]
    for f in range(fields):
        for r in range(H):
            span_low_ref[f, 2 * r : 2 * r + 2, :] = span_ref[f, r * 8 : r * 8 + 2, :]
            top = (height - H + r) * 8
            span_high_ref[f, 2 * r : 2 * r + 2, :] = span_ref[f, top + 6 : top + 8, :]


def prepare_kernel(dims, rho_hbm, vel_hbm, pre_hbm, met_hbm, state_ref, span_ref, met_ref, *refs):
    outs, (rho_ref, vel_ref, pre_ref, sems) = refs[:5], refs[5:]
    rows_i, height = dims
    total = rows_i * rows_i
    pairs = [(rho_hbm, rho_ref), (vel_hbm, vel_ref), (pre_hbm, pre_ref)]
    pairs += [(met_hbm.at[pl.ds(3 * d, 3)], met_ref.at[pl.ds(3 * d, 3)]) for d in (2, 0, 1)]
    copies = [pltpu.make_async_copy(a, b, sems.at[n]) for n, (a, b) in enumerate(pairs)]
    for copy in copies:
        copy.start()
    for copy in copies[:3]:
        copy.wait()
    rho, pressure = rho_ref[...], pre_ref[...]
    u = [vel_ref[m] for m in range(3)]
    speed_sq = u[0] * u[0] + u[1] * u[1] + u[2] * u[2]
    state_ref[0] = rho
    for m in range(3):
        state_ref[1 + m] = rho * u[m]
    state_ref[4] = pressure * (1.0 / 0.4) + 0.5 * rho * speed_sq
    core_ref, chip_ref = outs[:2]
    for f in range(8):
        if f == 5:
            copies[3].wait()
        value = state_ref[f] if f < 5 else met_ref[6 + f - 5]

        def store(start, block, f=f):
            span_ref[f, pl.ds(start, height, stride=8), :] = block

        to_span(value, store, height)
    send_parts(state_ref, span_ref, 8, outs, dims)
    copies[4].wait()
    even = lax.rem(lax.axis_index("wrap"), 2) == 0
    edge = H * rows_i
    to_core, to_chip = jnp.where(even, total - edge, 0), jnp.where(even, 0, total - edge)
    for m in range(3):
        core_ref[5 + m] = met_ref[m, aligned(to_core, edge), :]
        chip_ref[5 + m] = met_ref[m, aligned(to_chip, edge), :]
    copies[5].wait()


def early_kernel(dims, state_ref, span_ref, span_met_ref, met_ref, acc_ref, plus_i, minus_i, metric_i, plus_j, minus_j,
                 metric_j, diffused_ref, plus_k, minus_k, metric_k, diffused_k):
    rows_i, height = dims
    diffused_ref[0] = jnp.zeros(diffused_ref.shape[1:], F32)
    diffused_k[0] = jnp.zeros(diffused_k.shape[1:], F32)

    def planes(n, carry):
        rows = aligned(n * rows_i, rows_i)
        state = [state_ref[f, rows, :] for f in range(5)]
        prims = primitives(state)
        put_diffused(diffused_ref, rows, prims)
        put((plus_i, minus_i, metric_i), rows,
            *point_fluxes(state, prims, [unit(0, m, met_ref[m, rows, :]) for m in range(3)]))
        put((plus_j, minus_j, metric_j), rows,
            *point_fluxes(state, prims, [unit(1, m, met_ref[3 + m, rows, :]) for m in range(3)]))
        return carry

    lax.fori_loop(0, rows_i, planes, 0, unroll=2)

    def spans(n, carry):
        rows = aligned(n * 16, 16)
        state = [span_ref[f, rows, :] for f in range(5)]
        prims = primitives(state)
        put_diffused(diffused_k, rows, prims)
        put((plus_k, minus_k, metric_k), rows,
            *point_fluxes(state, prims, [unit(2, m, span_met_ref[5 + m, rows, :]) for m in range(3)]))
        return carry

    lax.fori_loop(0, height // 2, spans, 0, unroll=2)

    def normal(step, carry):
        f, tile = step // 2, step % 2

        def rows(n):
            return pl.ds(tile * 8 * rows_i + min(n, rows_i - 1), 8, stride=rows_i)

        def store(n, value):
            acc_ref[f, rows(n), :] = value

        for n in range(2):
            store(n, jnp.zeros((8, 128), F32))
        sweep(lambda n: plus_j[f, rows(n), :], lambda n: minus_j[f, rows(n), :], lambda n: diffused_ref[f, rows(n), :],
              lambda n: metric_j[rows(n), :], store, 2, rows_i - 1, open_low=True)
        return carry

    lax.fori_loop(0, 10, normal, 0)


def span_kernel(dims, span_ref, span_met_ref, span_low_ref, span_high_ref, met_low_ref, met_high_ref,
                plus_k, minus_k, metric_k, diffused_k, out_ref,
                acc_ref, halo_plus, halo_minus, halo_metric, halo_diffused, pad_ref):
    rows_i, height = dims
    sublane = lax.broadcasted_iota(jnp.int32, (8, 128), 0)
    halo_diffused[0] = jnp.zeros(halo_diffused.shape[1:], F32)
    for r in range(H):
        for f in range(8):
            low, high = (span_low_ref, span_high_ref) if f < 5 else (met_low_ref, met_high_ref)
            pad_ref[f, r * 8 : r * 8 + 2, :] = low[f, 2 * r : 2 * r + 2, :]
            pad_ref[f, (H + r) * 8 + 6 : (H + r) * 8 + 8, :] = high[f, 2 * r : 2 * r + 2, :]
    for r in range(2 * H):
        rows = slice(r * 8, r * 8 + 8)
        values = []
        for f in range(8):
            ref = span_ref if f < 5 else span_met_ref
            if r < H:
                own = pltpu.roll(ref[f, (height - H + r) * 8 : (height - H + r) * 8 + 8, :], 2, 0)
                values.append(jnp.where(sublane < 2, pad_ref[f, rows, :], own))
            else:
                own = pltpu.roll(ref[f, (r - H) * 8 : (r - H) * 8 + 8, :], 6, 0)
                values.append(jnp.where(sublane >= 6, pad_ref[f, rows, :], own))
        prims = primitives(values[:5])
        put_diffused(halo_diffused, rows, prims)
        put((halo_plus, halo_minus, halo_metric), rows,
            *point_fluxes(values[:5], prims, [unit(2, m, values[5 + m]) for m in range(3)]))

    def sweep_span(f, carry):
        def loader(ref, halo, lead):
            def load(n):
                if 0 <= n < height:
                    return ref[lead + (slice(n * 8, n * 8 + 8),)]
                r = n + H if n < 0 else n - height + H
                return halo[lead + (slice(r * 8, r * 8 + 8),)]

            return load

        def store(n, value):
            acc_ref[f, n * 8 : n * 8 + 8, :] = value

        sweep(loader(plus_k, halo_plus, (f,)), loader(minus_k, halo_minus, (f,)), loader(diffused_k, halo_diffused, (f,)),
              loader(metric_k, halo_metric, ()), store, -1, height - 1)
        return carry

    lax.fori_loop(0, 5, sweep_span, 0)
    for f in range(5):
        for half in range(2):
            parts = [acc_ref[f, pl.ds(q * 2 + half, height, stride=8), :] for q in range(4)]
            out_ref[f, half * 128 : (half + 1) * 128, :] = jnp.concatenate(parts, axis=0).T


def late_kernel(dims, final, *refs):
    rows_i, height = dims
    total = rows_i * rows_i
    (state_ref, met_ref, vol_ref, blank_ref, partner_ref, core_ref, chip_ref, met_core_ref, met_chip_ref, wake_ref,
     normal_ref, span_acc_ref, plus_i, minus_i, metric_i, plus_j, minus_j, metric_j, diffused_ref) = refs[:19]
    refs = refs[19:]
    if final:
        start_ref, out_ref = refs[:2]
        refs = refs[2:]
    else:
        out_ref, out_span_ref = refs[:2]
        outs, refs = refs[2:7], refs[7:]
    acc_ref, halo_plus, halo_minus, halo_metric, halo_diffused, ghost_ref = refs
    position, count = lax.axis_index("wrap"), lax.axis_size("wrap")
    even = lax.rem(position, 2) == 0
    at_end = (position == 0) | (position == count - 1)
    halo_diffused[0] = jnp.zeros(halo_diffused.shape[1:], F32)

    core_rows, chip_rows = jnp.where(even, H, 0), jnp.where(even, 0, H)
    own = jnp.where(even, 0, total - rows_i)
    for r in range(H):
        rows = slice(r * rows_i, (r + 1) * rows_i)
        state = [core_ref[f, rows, :] for f in range(5)]
        prims = primitives(state)
        to = aligned((core_rows + r) * rows_i, rows_i)
        put_diffused(halo_diffused, to, prims)
        put((halo_plus, halo_minus, halo_metric), to,
            *point_fluxes(state, prims, [unit(0, m, met_core_ref[5 + m, rows, :]) for m in range(3)]))
        edge = aligned(own, rows_i)
        state = [jnp.where(at_end, state_ref[f, edge, :], chip_ref[f, rows, :]) for f in range(5)]
        row = [jnp.where(at_end, met_ref[m, edge, :], met_chip_ref[5 + m, rows, :]) for m in range(3)]
        prims = primitives(state)
        to = aligned((chip_rows + r) * rows_i, rows_i)
        put_diffused(halo_diffused, to, prims)
        put((halo_plus, halo_minus, halo_metric), to,
            *point_fluxes(state, prims, [unit(0, m, row[m]) for m in range(3)]))

    def chord(step, carry):
        f, tile = step // 2, step % 2

        def loader(ref, halo, lead):
            def load(n):
                if 0 <= n < rows_i:
                    return ref[lead + (aligned(n * rows_i + tile * 8, 8),)]
                r = n + H if n < 0 else n - rows_i + H
                return halo[lead + (aligned(r * rows_i + tile * 8, 8),)]

            return load

        def store(n, value):
            rows = aligned(n * rows_i + tile * 8, 8)
            acc_ref[f, rows, :] = value + (normal_ref[f, rows, :] + span_acc_ref[f, rows, :])

        sweep(loader(plus_i, halo_plus, (f,)), loader(minus_i, halo_minus, (f,)), loader(diffused_ref, halo_diffused, (f,)),
              loader(metric_i, halo_metric, ()), store, -1, rows_i - 1)
        return carry

    lax.fori_loop(0, 10, chord, 0)

    base = (count - 1 - position) * rows_i
    for i in range(rows_i):
        ghost_ref[i * 16 : i * 16 + 16, :] = wake_ref[aligned((partner_ref[i] - base) * 16, 16), :]
    wall = pl.ds(0, rows_i, stride=rows_i)
    for r in range(H):
        state = [ghost_ref[pl.ds(f * H + r, rows_i, stride=16), :] for f in range(5)]
        prims = primitives(state)
        to = slice(r * rows_i, (r + 1) * rows_i)
        put_diffused(halo_diffused, to, prims)
        put((halo_plus, halo_minus, halo_metric), to,
            *point_fluxes(state, prims, [unit(1, m, met_ref[3 + m, wall, :]) for m in range(3)]))

    def normal(step, carry):
        f, tile = step // 2, step % 2

        def rows(n):
            return pl.ds(tile * 8 * rows_i + n, 8, stride=rows_i)

        def loader(ref, halo, lead):
            def load(n):
                if n >= 0:
                    return ref[lead + (rows(n),)]
                return halo[lead + (aligned((-1 - n) * rows_i + tile * 8, 8),)]

            return load

        def store(n, value):
            acc_ref[f, rows(n), :] = acc_ref[f, rows(n), :] + value

        sweep(loader(plus_j, halo_plus, (f,)), loader(minus_j, halo_minus, (f,)), loader(diffused_ref, halo_diffused, (f,)),
              lambda n: metric_j[rows(max(n, 0)), :], store, -1, 1, open_high=True)
        return carry

    lax.fori_loop(0, 10, normal, 0)

    scale = (time_step / 24.0) * blank_ref[...].astype(F32) / vol_ref[...]
    for f in range(5):
        moved = state_ref[f] + scale * acc_ref[f]
        out_ref[f] = 0.5 * start_ref[f] + 0.5 * moved if final else moved
    if not final:
        for f in range(5):
            def store(start, block, f=f):
                out_span_ref[f, pl.ds(start, height, stride=8), :] = block

            to_span(out_ref[f], store, height)
        send_parts(out_ref, out_span_ref, 5, outs, dims)


def shape(*sizes):
    return jax.ShapeDtypeStruct(sizes, F32)


def exchange(sent):
    core, chip, wake, span_low, span_high = sent
    n, s = lax.axis_size("wrap"), lax.axis_size("span")
    cores = [(i, i ^ 1) for i in range(n)]
    chips = [pair for i in range(1, n - 1, 2) for pair in ((i, i + 1), (i + 1, i))]
    mirror = [(i, n - 1 - i) for i in range(n)]
    ring_up = [(i, (i + 1) % s) for i in range(s)]
    ring_down = [((i + 1) % s, i) for i in range(s)]
    return (lax.ppermute(core, "wrap", cores), lax.ppermute(chip, "wrap", chips), lax.ppermute(wake, "wrap", mirror),
            lax.ppermute(span_high, "span", ring_up), lax.ppermute(span_low, "span", ring_down))


def body(density, velocity, pressure, metrics, volume, wake_partner, iblank):
    rows_i, rows_j, lanes = density.shape
    total, height = rows_i * rows_j, lanes // 4
    dims = (rows_i, height)
    volume, blank = volume.reshape(total, lanes), iblank.reshape(total, lanes)
    whole = pl.BlockSpec(memory_space=pltpu.VMEM)
    far = pl.BlockSpec(memory_space=pltpu.HBM)
    smem = pl.BlockSpec(memory_space=pltpu.SMEM)
    params = pltpu.CompilerParams(vmem_limit_bytes=16 * 2**20)

    def call(kernel, name, ins, outs, scratch, specs=None, cost=0):
        return pl.pallas_call(
            kernel,
            out_shape=outs,
            in_specs=specs or [whole] * len(ins),
            out_specs=[whole] * len(outs),
            scratch_shapes=scratch,
            compiler_params=params,
            cost_estimate=pl.CostEstimate(flops=cost, bytes_accessed=cost // 4, transcendentals=0),
            name=name,
        )(*ins)

    def parts(fields):
        edge = H * rows_j
        return [shape(fields, edge, lanes), shape(fields, edge, lanes), shape(rows_i * 16, lanes),
                shape(fields, 8, lanes), shape(fields, 8, lanes)]

    field, span_rows, halo = shape(5, total, lanes), height * 8, 2 * H * rows_i
    state, span, met, *sent = call(
        functools.partial(prepare_kernel, dims), "prepare",
        (density.reshape(total, lanes), velocity.reshape(3, total, lanes), pressure.reshape(total, lanes),
         metrics.reshape(9, total, lanes)),
        [field, shape(8, total, lanes), shape(9, total, lanes)] + parts(8),
        [pltpu.VMEM((total, lanes), F32), pltpu.VMEM((3, total, lanes), F32), pltpu.VMEM((total, lanes), F32),
         pltpu.SemaphoreType.DMA((6,))],
        [far] * 4,
    )
    span_met = span

    def halo_scratch(rows):
        return [pltpu.VMEM((5, rows, lanes), F32), pltpu.VMEM((5, rows, lanes), F32), pltpu.VMEM((rows, lanes), F32),
                pltpu.VMEM((5, rows, lanes), F32)]

    metric_halo = None
    start = state
    for final in (False, True):
        core, chip, wake, span_low, span_high = exchange(sent)
        if metric_halo is None:
            metric_halo = core, chip, span_low, span_high
        line, span_line = shape(5, total, lanes), shape(5, span_rows, lanes)
        normal, *lines = call(
            functools.partial(early_kernel, dims), "early", (state, span, span_met, met),
            [field, line, line, shape(total, lanes), line, line, shape(total, lanes), line,
             span_line, span_line, shape(span_rows, lanes), span_line],
            [], cost=10**8,
        )
        plus_i, minus_i, metric_i, plus_j, minus_j, metric_j, diffused = lines[:7]
        (span_acc,) = call(
            functools.partial(span_kernel, dims), "span",
            (span, span_met, span_low, span_high, metric_halo[2], metric_halo[3], *lines[7:]),
            [field],
            [pltpu.VMEM((5, span_rows, lanes), F32)] + halo_scratch(2 * H * 8) + [pltpu.VMEM((8, 2 * H * 8, lanes), F32)],
            cost=10**8,
        )
        ins = (state, met, volume, blank, wake_partner, core, chip, metric_halo[0], metric_halo[1], wake, normal, span_acc,
               plus_i, minus_i, metric_i, plus_j, minus_j, metric_j, diffused)
        ins += (start,) if final else ()
        state, *rest = call(
            functools.partial(late_kernel, dims, final), "late", ins,
            [field] if final else [field, field] + parts(5),
            [pltpu.VMEM((5, total, lanes), F32)] + halo_scratch(halo) + [pltpu.VMEM((rows_i * 16, lanes), F32)],
            [whole] * 4 + [smem] + [whole] * (len(ins) - 5),
            cost=10**8,
        )
        if not final:
            span, *sent = rest
    return state.reshape(5, rows_i, rows_j, lanes)


def solution(mesh):
    placed = (
        P("wrap", None, "span"),
        P(None, "wrap", None, "span"),
        P("wrap", None, "span"),
        P(None, "wrap", None, "span"),
        P("wrap", None, "span"),
        P("wrap"),
        P("wrap", None, "span"),
    )
    return jax.shard_map(
        body, mesh=mesh, in_specs=placed, out_specs=P(None, "wrap", None, "span"), check_vma=False
    )
```

```python
import functools

import jax
import jax.numpy as jnp
from jax import lax
from jax.experimental import pallas as pl
from jax.experimental.pallas import tpu as pltpu
from jax.sharding import PartitionSpec as P

epsilon = 1e-06
viscosity = 0.8
conduction = 1.0
time_step = 0.05
H = 3
F32 = jnp.float32


def primitives(state):
    rho, m0, m1, m2, energy = state
    inverse = 1.0 / rho
    velocity = (m0 * inverse, m1 * inverse, m2 * inverse)
    speed_sq = velocity[0] * velocity[0] + velocity[1] * velocity[1] + velocity[2] * velocity[2]
    pressure = 0.4 * (energy - 0.5 * rho * speed_sq)
    ratio = pressure * inverse
    heat = 0.5 * speed_sq + conduction * ratio
    return velocity, pressure, energy + pressure, 1.4 * ratio, heat


def point_fluxes(state, prims, row):
    rho, m0, m1, m2, _ = state
    (u0, u1, u2), pressure, enthalpy, sound_sq, _ = prims
    x0, x1, x2 = row
    contra = x0 * u0 + x1 * u1 + x2 * u2
    metric_sq = x0 * x0 + x1 * x1 + x2 * x2
    square = sound_sq * metric_sq
    speed = jnp.abs(contra) + square * lax.rsqrt(jnp.maximum(square, 1e-30))
    fluxes = (
        rho * contra,
        m0 * contra + x0 * pressure,
        m1 * contra + x1 * pressure,
        m2 * contra + x2 * pressure,
        enthalpy * contra,
    )
    waves = [speed * one for one in state]
    plus = [a + b for a, b in zip(fluxes, waves)]
    minus = [a - b for a, b in zip(fluxes, waves)]
    return plus, minus, metric_sq * (12.0 * viscosity * 0.5)


def RCP(x):
    return pl.reciprocal(x, approx=True)


class Split:
    def __init__(self, load, kind):
        self.load, self.memo, self.kind = load, {}, kind

    def get(self, name, n):
        if (name, n) not in self.memo:
            self.memo[name, n] = getattr(self, "make_" + name)(n)
        return self.memo[name, n]

    def make_v(self, n):
        return self.load(n)

    def make_d(self, n):
        return self.get("v", n + 1) - self.get("v", n)

    def make_e(self, n):
        return self.get("d", n) - self.get("d", n - 1)

    def make_t(self, n):
        return self.get("e", n + 1) - self.get("e", n)

    def make_near(self, n):
        return self.get("t", n).astype(self.kind)

    def make_near2(self, n):
        return self.get("near", n) + self.get("near", n)

    def make_low(self, n):
        return self.get("d", n).astype(self.kind)

    def make_smooth(self, n):
        high, low = self.get("low", n), self.get("low", n - 1)
        bend = self.get("e", n).astype(self.kind)
        twice = bend + bend
        a, b = high * twice, low * twice
        centre = (a - b) * self.kind(2.0 / 3.0) + (high * low + self.kind(16.0 * epsilon / 3.0))
        return centre + a, centre, centre - b

    def correction(self, outer, middle, inner, near, far):
        left = middle * RCP(outer)
        right = middle * RCP(inner)
        weight_left = left * left * self.kind(1.0 / 3.0)
        weight_right = right * right
        total = (weight_left + weight_right) + self.kind(2.0)
        return (weight_left * near + weight_right * far) * RCP(total)


def sweep(kind, load_plus, load_minus, load_diffused, load_metric, store, first, last, open_low=False, open_high=False):
    plus, minus = Split(load_plus, kind), Split(load_minus, kind)
    central, diffused, metric = {}, {}, {}

    def tripled(n):
        if n not in central:
            central[n] = 3.0 * (plus.get("v", n) + minus.get("v", n))
        return central[n]

    def cached(table, load, n):
        if n not in table:
            table[n] = load(n)
        return table[n]

    before = None
    for n in range(first, last + 1):
        up = plus.correction(
            plus.get("smooth", n - 1)[0],
            plus.get("smooth", n)[1],
            plus.get("smooth", n + 1)[2],
            plus.get("near2", n - 1),
            plus.get("near", n),
        )
        down = minus.correction(
            minus.get("smooth", n + 2)[2],
            minus.get("smooth", n + 1)[1],
            minus.get("smooth", n)[0],
            minus.get("near2", n + 1),
            minus.get("near", n),
        )
        flux = (tripled(n) + tripled(n + 1)) - (plus.get("e", n) + minus.get("e", n + 1)) + (down - up).astype(F32)
        face_metric = cached(metric, load_metric, n) + cached(metric, load_metric, n + 1)
        jump = cached(diffused, load_diffused, n + 1) - cached(diffused, load_diffused, n)
        net = face_metric * jump - flux
        if before is not None:
            store(n, net - before)
        elif open_low:
            store(n, net)
        before = net
    if open_high:
        store(last + 1, -before)


def put(refs, rows, plus, minus, metric=None):
    plus_ref, minus_ref, metric_ref = refs
    for f in range(5):
        plus_ref[f, rows, :] = plus[f]
        minus_ref[f, rows, :] = minus[f]
    if metric is not None:
        metric_ref[rows, :] = metric


def put_diffused(ref, rows, prims):
    for m in range(3):
        ref[1 + m, rows, :] = prims[0][m]
    ref[4, rows, :] = prims[4]


def aligned(start, count):
    return pl.ds(pl.multiple_of(start, 8), count)


def unit(which, m, value):
    return value + 1.0 if which == m else value


def to_span(value, store, height):
    for half in range(2):
        turned = value[half * 128 : (half + 1) * 128].T
        for q in range(4):
            store(q * 2 + half, turned[q * height : (q + 1) * height])


def send_parts(state_ref, span_ref, fields, outs, dims):
    rows_i, height = dims
    total = rows_i * rows_i
    core_ref, chip_ref, wake_ref, span_low_ref, span_high_ref = outs
    even = lax.rem(lax.axis_index("wrap"), 2) == 0
    edge = H * rows_i
    to_core, to_chip = jnp.where(even, total - edge, 0), jnp.where(even, 0, total - edge)
    for f in range(5):
        core_ref[f] = state_ref[f, aligned(to_core, edge), :]
        chip_ref[f] = state_ref[f, aligned(to_chip, edge), :]
        for r in range(H):
            wake_ref[pl.ds(f * H + r, rows_i, stride=16), :] = state_ref[f, pl.ds(r + 1, rows_i, stride=rows_i), :]
    for f in range(fields):
        for r in range(H):
            span_low_ref[f, 2 * r : 2 * r + 2, :] = span_ref[f, r * 8 : r * 8 + 2, :]
            top = (height - H + r) * 8
            span_high_ref[f, 2 * r : 2 * r + 2, :] = span_ref[f, top + 6 : top + 8, :]


def prepare_kernel(dims, rho_hbm, vel_hbm, pre_hbm, met_hbm, state_ref, span_ref, met_ref, *refs):
    outs, (rho_ref, vel_ref, pre_ref, sems) = refs[:5], refs[5:]
    rows_i, height = dims
    total = rows_i * rows_i
    pairs = [(rho_hbm, rho_ref), (vel_hbm, vel_ref), (pre_hbm, pre_ref)]
    pairs += [(met_hbm.at[pl.ds(3 * d, 3)], met_ref.at[pl.ds(3 * d, 3)]) for d in (2, 0, 1)]
    copies = [pltpu.make_async_copy(a, b, sems.at[n]) for n, (a, b) in enumerate(pairs)]
    for copy in copies:
        copy.start()
    for copy in copies[:3]:
        copy.wait()
    rho, pressure = rho_ref[...], pre_ref[...]
    u = [vel_ref[m] for m in range(3)]
    speed_sq = u[0] * u[0] + u[1] * u[1] + u[2] * u[2]
    state_ref[0] = rho
    for m in range(3):
        state_ref[1 + m] = rho * u[m]
    state_ref[4] = pressure * (1.0 / 0.4) + 0.5 * rho * speed_sq
    core_ref, chip_ref = outs[:2]
    for f in range(8):
        if f == 5:
            copies[3].wait()
        value = state_ref[f] if f < 5 else met_ref[6 + f - 5]

        def store(start, block, f=f):
            span_ref[f, pl.ds(start, height, stride=8), :] = block

        to_span(value, store, height)
    send_parts(state_ref, span_ref, 8, outs, dims)
    copies[4].wait()
    even = lax.rem(lax.axis_index("wrap"), 2) == 0
    edge = H * rows_i
    to_core, to_chip = jnp.where(even, total - edge, 0), jnp.where(even, 0, total - edge)
    for m in range(3):
        core_ref[5 + m] = met_ref[m, aligned(to_core, edge), :]
        chip_ref[5 + m] = met_ref[m, aligned(to_chip, edge), :]
    copies[5].wait()


def early_kernel(dims, kind, state_ref, span_ref, span_met_ref, met_ref, acc_ref, plus_i, minus_i, metric_i, plus_j, minus_j,
                 metric_j, diffused_ref, plus_k, minus_k, metric_k, diffused_k):
    rows_i, height = dims
    diffused_ref[0] = jnp.zeros(diffused_ref.shape[1:], F32)
    diffused_k[0] = jnp.zeros(diffused_k.shape[1:], F32)

    def planes(n, carry):
        rows = aligned(n * rows_i, rows_i)
        state = [state_ref[f, rows, :] for f in range(5)]
        prims = primitives(state)
        put_diffused(diffused_ref, rows, prims)
        put((plus_i, minus_i, metric_i), rows,
            *point_fluxes(state, prims, [unit(0, m, met_ref[m, rows, :]) for m in range(3)]))
        put((plus_j, minus_j, metric_j), rows,
            *point_fluxes(state, prims, [unit(1, m, met_ref[3 + m, rows, :]) for m in range(3)]))
        return carry

    lax.fori_loop(0, rows_i, planes, 0, unroll=2)

    def spans(n, carry):
        rows = aligned(n * 16, 16)
        state = [span_ref[f, rows, :] for f in range(5)]
        prims = primitives(state)
        put_diffused(diffused_k, rows, prims)
        put((plus_k, minus_k, metric_k), rows,
            *point_fluxes(state, prims, [unit(2, m, span_met_ref[5 + m, rows, :]) for m in range(3)]))
        return carry

    lax.fori_loop(0, height // 2, spans, 0, unroll=2)

    def normal(f, carry):
        def rows(n):
            return pl.ds(min(n, rows_i - 1), rows_i, stride=rows_i)

        def store(n, value):
            acc_ref[f, rows(n), :] = value

        for n in range(2):
            store(n, jnp.zeros((rows_i, 128), F32))
        sweep(kind, lambda n: plus_j[f, rows(n), :], lambda n: minus_j[f, rows(n), :], lambda n: diffused_ref[f, rows(n), :],
              lambda n: metric_j[rows(n), :], store, 2, rows_i - 1, open_low=True)
        return carry

    lax.fori_loop(0, 5, normal, 0)


def span_kernel(dims, kind, span_ref, span_met_ref, span_low_ref, span_high_ref, met_low_ref, met_high_ref,
                plus_k, minus_k, metric_k, diffused_k, out_ref,
                acc_ref, halo_plus, halo_minus, halo_metric, halo_diffused, pad_ref):
    rows_i, height = dims
    sublane = lax.broadcasted_iota(jnp.int32, (8, 128), 0)
    halo_diffused[0] = jnp.zeros(halo_diffused.shape[1:], F32)
    for r in range(H):
        for f in range(8):
            low, high = (span_low_ref, span_high_ref) if f < 5 else (met_low_ref, met_high_ref)
            pad_ref[f, r * 8 : r * 8 + 2, :] = low[f, 2 * r : 2 * r + 2, :]
            pad_ref[f, (H + r) * 8 + 6 : (H + r) * 8 + 8, :] = high[f, 2 * r : 2 * r + 2, :]
    for r in range(2 * H):
        rows = slice(r * 8, r * 8 + 8)
        values = []
        for f in range(8):
            ref = span_ref if f < 5 else span_met_ref
            if r < H:
                own = pltpu.roll(ref[f, (height - H + r) * 8 : (height - H + r) * 8 + 8, :], 2, 0)
                values.append(jnp.where(sublane < 2, pad_ref[f, rows, :], own))
            else:
                own = pltpu.roll(ref[f, (r - H) * 8 : (r - H) * 8 + 8, :], 6, 0)
                values.append(jnp.where(sublane >= 6, pad_ref[f, rows, :], own))
        prims = primitives(values[:5])
        put_diffused(halo_diffused, rows, prims)
        put((halo_plus, halo_minus, halo_metric), rows,
            *point_fluxes(values[:5], prims, [unit(2, m, values[5 + m]) for m in range(3)]))

    def sweep_span(f, carry):
        def loader(ref, halo, lead):
            def one(n):
                if 0 <= n < height:
                    return ref[lead + (slice(n * 8, n * 8 + 8),)]
                r = n + H if n < 0 else n - height + H
                return halo[lead + (slice(r * 8, r * 8 + 8),)]

            return lambda n: jnp.concatenate([one(n), one(n + height // 2)], axis=0)

        def store(n, value):
            acc_ref[f, n * 8 : n * 8 + 8, :] = value[:8]
            m = n + height // 2
            acc_ref[f, m * 8 : m * 8 + 8, :] = value[8:]

        sweep(kind, loader(plus_k, halo_plus, (f,)), loader(minus_k, halo_minus, (f,)), loader(diffused_k, halo_diffused, (f,)),
              loader(metric_k, halo_metric, ()), store, -1, height // 2 - 1)
        return carry

    lax.fori_loop(0, 5, sweep_span, 0)
    for f in range(5):
        for half in range(2):
            parts = [acc_ref[f, pl.ds(q * 2 + half, height, stride=8), :] for q in range(4)]
            out_ref[f, half * 128 : (half + 1) * 128, :] = jnp.concatenate(parts, axis=0).T


def late_kernel(dims, kind, final, *refs):
    rows_i, height = dims
    total = rows_i * rows_i
    (state_ref, met_ref, vol_ref, blank_ref, partner_ref, core_ref, chip_ref, met_core_ref, met_chip_ref, wake_ref,
     normal_ref, span_acc_ref, plus_i, minus_i, metric_i, plus_j, minus_j, metric_j, diffused_ref) = refs[:19]
    refs = refs[19:]
    if final:
        start_ref, out_ref = refs[:2]
        refs = refs[2:]
    else:
        out_ref, out_span_ref = refs[:2]
        outs, refs = refs[2:7], refs[7:]
    acc_ref, halo_plus, halo_minus, halo_metric, halo_diffused, ghost_ref = refs
    position, count = lax.axis_index("wrap"), lax.axis_size("wrap")
    even = lax.rem(position, 2) == 0
    at_end = (position == 0) | (position == count - 1)
    halo_diffused[0] = jnp.zeros(halo_diffused.shape[1:], F32)

    core_rows, chip_rows = jnp.where(even, H, 0), jnp.where(even, 0, H)
    own = jnp.where(even, 0, total - rows_i)
    for r in range(H):
        rows = slice(r * rows_i, (r + 1) * rows_i)
        state = [core_ref[f, rows, :] for f in range(5)]
        prims = primitives(state)
        to = aligned((core_rows + r) * rows_i, rows_i)
        put_diffused(halo_diffused, to, prims)
        put((halo_plus, halo_minus, halo_metric), to,
            *point_fluxes(state, prims, [unit(0, m, met_core_ref[5 + m, rows, :]) for m in range(3)]))
        edge = aligned(own, rows_i)
        state = [jnp.where(at_end, state_ref[f, edge, :], chip_ref[f, rows, :]) for f in range(5)]
        row = [jnp.where(at_end, met_ref[m, edge, :], met_chip_ref[5 + m, rows, :]) for m in range(3)]
        prims = primitives(state)
        to = aligned((chip_rows + r) * rows_i, rows_i)
        put_diffused(halo_diffused, to, prims)
        put((halo_plus, halo_minus, halo_metric), to,
            *point_fluxes(state, prims, [unit(0, m, row[m]) for m in range(3)]))

    def chord(f, carry):
        def loader(ref, halo, lead):
            def load(n):
                if 0 <= n < rows_i:
                    return ref[lead + (aligned(n * rows_i, rows_i),)]
                r = n + H if n < 0 else n - rows_i + H
                return halo[lead + (aligned(r * rows_i, rows_i),)]

            return load

        def store(n, value):
            rows = aligned(n * rows_i, rows_i)
            acc_ref[f, rows, :] = value + (normal_ref[f, rows, :] + span_acc_ref[f, rows, :])

        sweep(kind, loader(plus_i, halo_plus, (f,)), loader(minus_i, halo_minus, (f,)), loader(diffused_ref, halo_diffused, (f,)),
              loader(metric_i, halo_metric, ()), store, -1, rows_i - 1)
        return carry

    lax.fori_loop(0, 5, chord, 0)

    base = (count - 1 - position) * rows_i
    for i in range(rows_i):
        ghost_ref[i * 16 : i * 16 + 16, :] = wake_ref[aligned((partner_ref[i] - base) * 16, 16), :]
    wall = pl.ds(0, rows_i, stride=rows_i)
    for r in range(H):
        state = [ghost_ref[pl.ds(f * H + r, rows_i, stride=16), :] for f in range(5)]
        prims = primitives(state)
        to = slice(r * rows_i, (r + 1) * rows_i)
        put_diffused(halo_diffused, to, prims)
        put((halo_plus, halo_minus, halo_metric), to,
            *point_fluxes(state, prims, [unit(1, m, met_ref[3 + m, wall, :]) for m in range(3)]))

    def normal(f, carry):
        def rows(n):
            return pl.ds(n, rows_i, stride=rows_i)

        def loader(ref, halo, lead):
            def load(n):
                if n >= 0:
                    return ref[lead + (rows(n),)]
                return halo[lead + (aligned((-1 - n) * rows_i, rows_i),)]

            return load

        def store(n, value):
            acc_ref[f, rows(n), :] = acc_ref[f, rows(n), :] + value

        sweep(kind, loader(plus_j, halo_plus, (f,)), loader(minus_j, halo_minus, (f,)), loader(diffused_ref, halo_diffused, (f,)),
              lambda n: metric_j[rows(max(n, 0)), :], store, -1, 1, open_high=True)
        return carry

    lax.fori_loop(0, 5, normal, 0)

    scale = (time_step / 12.0) * blank_ref[...].astype(F32) / vol_ref[...]
    for f in range(5):
        moved = state_ref[f] + scale * acc_ref[f]
        out_ref[f] = 0.5 * start_ref[f] + 0.5 * moved if final else moved
    if not final:
        for f in range(5):
            def store(start, block, f=f):
                out_span_ref[f, pl.ds(start, height, stride=8), :] = block

            to_span(out_ref[f], store, height)
        send_parts(out_ref, out_span_ref, 5, outs, dims)


def shape(*sizes):
    return jax.ShapeDtypeStruct(sizes, F32)


def exchange(sent):
    core, chip, wake, span_low, span_high = sent
    n, s = lax.axis_size("wrap"), lax.axis_size("span")
    cores = [(i, i ^ 1) for i in range(n)]
    chips = [pair for i in range(1, n - 1, 2) for pair in ((i, i + 1), (i + 1, i))]
    mirror = [(i, n - 1 - i) for i in range(n)]
    ring_up = [(i, (i + 1) % s) for i in range(s)]
    ring_down = [((i + 1) % s, i) for i in range(s)]
    return (lax.ppermute(core, "wrap", cores), lax.ppermute(chip, "wrap", chips), lax.ppermute(wake, "wrap", mirror),
            lax.ppermute(span_high, "span", ring_up), lax.ppermute(span_low, "span", ring_down))


def body(density, velocity, pressure, metrics, volume, wake_partner, iblank):
    rows_i, rows_j, lanes = density.shape
    total, height = rows_i * rows_j, lanes // 4
    dims = (rows_i, height)
    volume, blank = volume.reshape(total, lanes), iblank.reshape(total, lanes)
    whole = pl.BlockSpec(memory_space=pltpu.VMEM)
    far = pl.BlockSpec(memory_space=pltpu.HBM)
    smem = pl.BlockSpec(memory_space=pltpu.SMEM)
    params = pltpu.CompilerParams(vmem_limit_bytes=16 * 2**20)

    def call(kernel, name, ins, outs, scratch, specs=None, cost=0):
        return pl.pallas_call(
            kernel,
            out_shape=outs,
            in_specs=specs or [whole] * len(ins),
            out_specs=[whole] * len(outs),
            scratch_shapes=scratch,
            compiler_params=params,
            cost_estimate=pl.CostEstimate(flops=cost, bytes_accessed=cost // 4, transcendentals=0),
            name=name,
        )(*ins)

    def parts(fields):
        edge = H * rows_j
        return [shape(fields, edge, lanes), shape(fields, edge, lanes), shape(rows_i * 16, lanes),
                shape(fields, 8, lanes), shape(fields, 8, lanes)]

    field, span_rows, halo = shape(5, total, lanes), height * 8, 2 * H * rows_i
    state, span, met, *sent = call(
        functools.partial(prepare_kernel, dims), "prepare",
        [pltpu.with_memory_space_constraint(one, pltpu.HBM) for one in (
            density.reshape(total, lanes), velocity.reshape(3, total, lanes), pressure.reshape(total, lanes),
            metrics.reshape(9, total, lanes))],
        [field, shape(8, total, lanes), shape(9, total, lanes)] + parts(8),
        [pltpu.VMEM((total, lanes), F32), pltpu.VMEM((3, total, lanes), F32), pltpu.VMEM((total, lanes), F32),
         pltpu.SemaphoreType.DMA((6,))],
        [far] * 4,
    )
    span_met = span

    def halo_scratch(rows):
        return [pltpu.VMEM((5, rows, lanes), F32), pltpu.VMEM((5, rows, lanes), F32), pltpu.VMEM((rows, lanes), F32),
                pltpu.VMEM((5, rows, lanes), F32)]

    metric_halo = None
    start = state
    for final in (False, True):
        kind = jnp.bfloat16 if final else F32
        core, chip, wake, span_low, span_high = exchange(sent)
        if metric_halo is None:
            metric_halo = core, chip, span_low, span_high
        line, span_line = shape(5, total, lanes), shape(5, span_rows, lanes)
        normal, *lines = call(
            functools.partial(early_kernel, dims, kind), "early", (state, span, span_met, met),
            [field, line, line, shape(total, lanes), line, line, shape(total, lanes), line,
             span_line, span_line, shape(span_rows, lanes), span_line],
            [], cost=10**8,
        )
        plus_i, minus_i, metric_i, plus_j, minus_j, metric_j, diffused = lines[:7]
        (span_acc,) = call(
            functools.partial(span_kernel, dims, kind), "span",
            (span, span_met, span_low, span_high, metric_halo[2], metric_halo[3], *lines[7:]),
            [field],
            [pltpu.VMEM((5, span_rows, lanes), F32)] + halo_scratch(2 * H * 8) + [pltpu.VMEM((8, 2 * H * 8, lanes), F32)],
            cost=10**8,
        )
        ins = (state, met, volume, blank, wake_partner, core, chip, metric_halo[0], metric_halo[1], wake, normal, span_acc,
               plus_i, minus_i, metric_i, plus_j, minus_j, metric_j, diffused)
        ins += (start,) if final else ()
        state, *rest = call(
            functools.partial(late_kernel, dims, kind, final), "late", ins,
            [field] if final else [field, field] + parts(5),
            [pltpu.VMEM((5, total, lanes), F32)] + halo_scratch(halo) + [pltpu.VMEM((rows_i * 16, lanes), F32)],
            [whole] * 4 + [smem] + [whole] * (len(ins) - 5),
            cost=10**8,
        )
        if not final:
            span, *sent = rest
    return state.reshape(5, rows_i, rows_j, lanes)


def solution(mesh):
    placed = (
        P("wrap", None, "span"),
        P(None, "wrap", None, "span"),
        P("wrap", None, "span"),
        P(None, "wrap", None, "span"),
        P("wrap", None, "span"),
        P("wrap"),
        P("wrap", None, "span"),
    )
    return jax.shard_map(
        body, mesh=mesh, in_specs=placed, out_specs=P(None, "wrap", None, "span"), check_vma=False
    )
```

```python
import functools

import jax
import jax.numpy as jnp
from jax import lax
from jax.experimental import pallas as pl
from jax.experimental.pallas import tpu as pltpu
from jax.sharding import PartitionSpec as P

epsilon = 1e-06
viscosity = 0.8
conduction = 1.0
time_step = 0.05
H = 3
F32 = jnp.float32


def primitives(state):
    rho, m0, m1, m2, energy = state
    inverse = 1.0 / rho
    velocity = (m0 * inverse, m1 * inverse, m2 * inverse)
    speed_sq = velocity[0] * velocity[0] + velocity[1] * velocity[1] + velocity[2] * velocity[2]
    pressure = 0.4 * (energy - 0.5 * rho * speed_sq)
    ratio = pressure * inverse
    heat = 0.5 * speed_sq + conduction * ratio
    return velocity, pressure, energy + pressure, 1.4 * ratio, heat


def point_fluxes(state, prims, row):
    rho, m0, m1, m2, _ = state
    (u0, u1, u2), pressure, enthalpy, sound_sq, _ = prims
    x0, x1, x2 = row
    contra = x0 * u0 + x1 * u1 + x2 * u2
    metric_sq = x0 * x0 + x1 * x1 + x2 * x2
    square = sound_sq * metric_sq
    speed = jnp.abs(contra) + square * lax.rsqrt(jnp.maximum(square, 1e-30))
    fluxes = (
        rho * contra,
        m0 * contra + x0 * pressure,
        m1 * contra + x1 * pressure,
        m2 * contra + x2 * pressure,
        enthalpy * contra,
    )
    waves = [speed * one for one in state]
    plus = [a + b for a, b in zip(fluxes, waves)]
    minus = [a - b for a, b in zip(fluxes, waves)]
    return plus, minus, metric_sq * (12.0 * viscosity * 0.5)


def RCP(x):
    return pl.reciprocal(x, approx=True)


class Split:
    def __init__(self, load, kind):
        self.load, self.memo, self.kind = load, {}, kind

    def get(self, name, n):
        if (name, n) not in self.memo:
            self.memo[name, n] = getattr(self, "make_" + name)(n)
        return self.memo[name, n]

    def make_v(self, n):
        return self.load(n)

    def make_d(self, n):
        return self.get("v", n + 1) - self.get("v", n)

    def make_e(self, n):
        return self.get("d", n) - self.get("d", n - 1)

    def make_t(self, n):
        return self.get("e", n + 1) - self.get("e", n)

    def make_near(self, n):
        return self.get("t", n).astype(self.kind)

    def make_near2(self, n):
        return self.get("near", n) + self.get("near", n)

    def make_low(self, n):
        return self.get("d", n).astype(self.kind)

    def make_smooth(self, n):
        high, low = self.get("low", n), self.get("low", n - 1)
        bend = self.get("e", n).astype(self.kind)
        twice = bend + bend
        a, b = high * twice, low * twice
        centre = (a - b) * self.kind(2.0 / 3.0) + (high * low + self.kind(16.0 * epsilon / 3.0))
        return centre + a, centre, centre - b

    def correction(self, outer, middle, inner, near, far):
        left = middle * RCP(outer)
        right = middle * RCP(inner)
        weight_left = left * left * self.kind(1.0 / 3.0)
        weight_right = right * right
        total = (weight_left + weight_right) + self.kind(2.0)
        return (weight_left * near + weight_right * far) * RCP(total)


def sweep(kind, load_plus, load_minus, load_diffused, load_metric, store, first, last, open_low=False, open_high=False):
    plus, minus = Split(load_plus, kind), Split(load_minus, kind)
    central, diffused, metric = {}, {}, {}

    def tripled(n):
        if n not in central:
            central[n] = 3.0 * (plus.get("v", n) + minus.get("v", n))
        return central[n]

    def cached(table, load, n):
        if n not in table:
            table[n] = load(n)
        return table[n]

    before = None
    for n in range(first, last + 1):
        up = plus.correction(
            plus.get("smooth", n - 1)[0],
            plus.get("smooth", n)[1],
            plus.get("smooth", n + 1)[2],
            plus.get("near2", n - 1),
            plus.get("near", n),
        )
        down = minus.correction(
            minus.get("smooth", n + 2)[2],
            minus.get("smooth", n + 1)[1],
            minus.get("smooth", n)[0],
            minus.get("near2", n + 1),
            minus.get("near", n),
        )
        flux = (tripled(n) + tripled(n + 1)) - (plus.get("e", n) + minus.get("e", n + 1)) + (down - up).astype(F32)
        face_metric = cached(metric, load_metric, n) + cached(metric, load_metric, n + 1)
        jump = cached(diffused, load_diffused, n + 1) - cached(diffused, load_diffused, n)
        net = face_metric * jump - flux
        if before is not None:
            store(n, net - before)
        elif open_low:
            store(n, net)
        before = net
    if open_high:
        store(last + 1, -before)


def put(refs, rows, plus, minus, metric=None):
    plus_ref, minus_ref, metric_ref = refs
    for f in range(5):
        plus_ref[f, rows, :] = plus[f]
        minus_ref[f, rows, :] = minus[f]
    if metric is not None:
        metric_ref[rows, :] = metric


def put_diffused(ref, rows, prims):
    for m in range(3):
        ref[1 + m, rows, :] = prims[0][m]
    ref[4, rows, :] = prims[4]


def aligned(start, count):
    return pl.ds(pl.multiple_of(start, 8), count)


def unit(which, m, value):
    return value + 1.0 if which == m else value


def to_span(value, store, height):
    for half in range(2):
        turned = value[half * 128 : (half + 1) * 128].T
        for q in range(4):
            store(q * 2 + half, turned[q * height : (q + 1) * height])


def send_parts(state_ref, span_ref, fields, outs, dims):
    rows_i, height = dims
    total = rows_i * rows_i
    core_ref, chip_ref, wake_ref, span_low_ref, span_high_ref = outs
    even = lax.rem(lax.axis_index("wrap"), 2) == 0
    edge = H * rows_i
    to_core, to_chip = jnp.where(even, total - edge, 0), jnp.where(even, 0, total - edge)
    for f in range(5):
        core_ref[f] = state_ref[f, aligned(to_core, edge), :]
        chip_ref[f] = state_ref[f, aligned(to_chip, edge), :]
        for r in range(H):
            wake_ref[pl.ds(f * H + r, rows_i, stride=16), :] = state_ref[f, pl.ds(r + 1, rows_i, stride=rows_i), :]
    for f in range(fields):
        for r in range(H):
            span_low_ref[f, 2 * r : 2 * r + 2, :] = span_ref[f, r * 8 : r * 8 + 2, :]
            top = (height - H + r) * 8
            span_high_ref[f, 2 * r : 2 * r + 2, :] = span_ref[f, top + 6 : top + 8, :]


def prepare_kernel(dims, rho_hbm, vel_hbm, pre_hbm, met_hbm, state_ref, span_ref, met_ref, *refs):
    outs, (rho_ref, vel_ref, pre_ref, sems) = refs[:5], refs[5:]
    rows_i, height = dims
    total = rows_i * rows_i
    pairs = [(rho_hbm, rho_ref), (vel_hbm, vel_ref), (pre_hbm, pre_ref)]
    pairs += [(met_hbm.at[pl.ds(3 * d, 3)], met_ref.at[pl.ds(3 * d, 3)]) for d in (2, 0, 1)]
    copies = [pltpu.make_async_copy(a, b, sems.at[n]) for n, (a, b) in enumerate(pairs)]
    for copy in copies:
        copy.start()
    for copy in copies[:3]:
        copy.wait()
    rho, pressure = rho_ref[...], pre_ref[...]
    u = [vel_ref[m] for m in range(3)]
    speed_sq = u[0] * u[0] + u[1] * u[1] + u[2] * u[2]
    state_ref[0] = rho
    for m in range(3):
        state_ref[1 + m] = rho * u[m]
    state_ref[4] = pressure * (1.0 / 0.4) + 0.5 * rho * speed_sq
    core_ref, chip_ref = outs[:2]
    for f in range(8):
        if f == 5:
            copies[3].wait()
        value = state_ref[f] if f < 5 else met_ref[6 + f - 5]

        def store(start, block, f=f):
            span_ref[f, pl.ds(start, height, stride=8), :] = block

        to_span(value, store, height)
    send_parts(state_ref, span_ref, 8, outs, dims)
    copies[4].wait()
    even = lax.rem(lax.axis_index("wrap"), 2) == 0
    edge = H * rows_i
    to_core, to_chip = jnp.where(even, total - edge, 0), jnp.where(even, 0, total - edge)
    for m in range(3):
        core_ref[5 + m] = met_ref[m, aligned(to_core, edge), :]
        chip_ref[5 + m] = met_ref[m, aligned(to_chip, edge), :]
    copies[5].wait()


def early_kernel(dims, kind, state_ref, span_ref, span_met_ref, met_ref, acc_ref, plus_i, minus_i, metric_i, plus_j, minus_j,
                 metric_j, diffused_ref, plus_k, minus_k, metric_k, diffused_k):
    rows_i, height = dims
    diffused_ref[0] = jnp.zeros(diffused_ref.shape[1:], F32)
    diffused_k[0] = jnp.zeros(diffused_k.shape[1:], F32)

    def planes(n, carry):
        rows = aligned(n * rows_i, rows_i)
        state = [state_ref[f, rows, :] for f in range(5)]
        prims = primitives(state)
        put_diffused(diffused_ref, rows, prims)
        put((plus_i, minus_i, metric_i), rows,
            *point_fluxes(state, prims, [unit(0, m, met_ref[m, rows, :]) for m in range(3)]))
        put((plus_j, minus_j, metric_j), rows,
            *point_fluxes(state, prims, [unit(1, m, met_ref[3 + m, rows, :]) for m in range(3)]))
        return carry

    lax.fori_loop(0, rows_i, planes, 0, unroll=2)

    def spans(n, carry):
        rows = aligned(n * 16, 16)
        state = [span_ref[f, rows, :] for f in range(5)]
        prims = primitives(state)
        put_diffused(diffused_k, rows, prims)
        put((plus_k, minus_k, metric_k), rows,
            *point_fluxes(state, prims, [unit(2, m, span_met_ref[5 + m, rows, :]) for m in range(3)]))
        return carry

    lax.fori_loop(0, height // 2, spans, 0, unroll=2)

    def normal(f, carry):
        def rows(n):
            return pl.ds(min(n, rows_i - 1), rows_i, stride=rows_i)

        def store(n, value):
            acc_ref[f, rows(n), :] = value

        for n in range(2):
            store(n, jnp.zeros((rows_i, 128), F32))
        sweep(kind, lambda n: plus_j[f, rows(n), :], lambda n: minus_j[f, rows(n), :], lambda n: diffused_ref[f, rows(n), :],
              lambda n: metric_j[rows(n), :], store, 2, rows_i - 1, open_low=True)
        return carry

    lax.fori_loop(0, 5, normal, 0)


def span_kernel(dims, kind, span_ref, span_met_ref, span_low_ref, span_high_ref, met_low_ref, met_high_ref,
                plus_k, minus_k, metric_k, diffused_k, out_ref,
                acc_ref, halo_plus, halo_minus, halo_metric, halo_diffused, pad_ref):
    rows_i, height = dims
    sublane = lax.broadcasted_iota(jnp.int32, (8, 128), 0)
    halo_diffused[0] = jnp.zeros(halo_diffused.shape[1:], F32)
    for r in range(H):
        for f in range(8):
            low, high = (span_low_ref, span_high_ref) if f < 5 else (met_low_ref, met_high_ref)
            pad_ref[f, r * 8 : r * 8 + 2, :] = low[f, 2 * r : 2 * r + 2, :]
            pad_ref[f, (H + r) * 8 + 6 : (H + r) * 8 + 8, :] = high[f, 2 * r : 2 * r + 2, :]
    for r in range(2 * H):
        rows = slice(r * 8, r * 8 + 8)
        values = []
        for f in range(8):
            ref = span_ref if f < 5 else span_met_ref
            if r < H:
                own = pltpu.roll(ref[f, (height - H + r) * 8 : (height - H + r) * 8 + 8, :], 2, 0)
                values.append(jnp.where(sublane < 2, pad_ref[f, rows, :], own))
            else:
                own = pltpu.roll(ref[f, (r - H) * 8 : (r - H) * 8 + 8, :], 6, 0)
                values.append(jnp.where(sublane >= 6, pad_ref[f, rows, :], own))
        prims = primitives(values[:5])
        put_diffused(halo_diffused, rows, prims)
        put((halo_plus, halo_minus, halo_metric), rows,
            *point_fluxes(values[:5], prims, [unit(2, m, values[5 + m]) for m in range(3)]))

    def sweep_span(f, carry):
        def loader(ref, halo, lead):
            def one(n):
                if 0 <= n < height:
                    return ref[lead + (slice(n * 8, n * 8 + 8),)]
                r = n + H if n < 0 else n - height + H
                return halo[lead + (slice(r * 8, r * 8 + 8),)]

            return lambda n: jnp.concatenate([one(n), one(n + height // 2)], axis=0)

        def store(n, value):
            acc_ref[f, n * 8 : n * 8 + 8, :] = value[:8]
            m = n + height // 2
            acc_ref[f, m * 8 : m * 8 + 8, :] = value[8:]

        sweep(kind, loader(plus_k, halo_plus, (f,)), loader(minus_k, halo_minus, (f,)), loader(diffused_k, halo_diffused, (f,)),
              loader(metric_k, halo_metric, ()), store, -1, height // 2 - 1)
        return carry

    lax.fori_loop(0, 5, sweep_span, 0)
    for f in range(5):
        for half in range(2):
            parts = [acc_ref[f, pl.ds(q * 2 + half, height, stride=8), :] for q in range(4)]
            out_ref[f, half * 128 : (half + 1) * 128, :] = jnp.concatenate(parts, axis=0).T


def late_kernel(dims, kind, final, *refs):
    rows_i, height = dims
    total = rows_i * rows_i
    (state_ref, met_ref, vol_ref, blank_ref, partner_hbm, core_ref, chip_ref, met_core_ref, met_chip_ref, wake_ref,
     normal_ref, span_acc_ref, plus_i, minus_i, metric_i, plus_j, minus_j, metric_j, diffused_ref) = refs[:19]
    refs = refs[19:]
    if final:
        start_ref, out_ref = refs[:2]
        refs = refs[2:]
    else:
        out_ref, out_span_ref = refs[:2]
        outs, refs = refs[2:7], refs[7:]
    acc_ref, halo_plus, halo_minus, halo_metric, halo_diffused, ghost_ref, partner_ref, sem = refs
    fetch = pltpu.make_async_copy(partner_hbm, partner_ref, sem)
    fetch.start()
    position, count = lax.axis_index("wrap"), lax.axis_size("wrap")
    even = lax.rem(position, 2) == 0
    at_end = (position == 0) | (position == count - 1)
    halo_diffused[0] = jnp.zeros(halo_diffused.shape[1:], F32)

    core_rows, chip_rows = jnp.where(even, H, 0), jnp.where(even, 0, H)
    own = jnp.where(even, 0, total - rows_i)
    for r in range(H):
        rows = slice(r * rows_i, (r + 1) * rows_i)
        state = [core_ref[f, rows, :] for f in range(5)]
        prims = primitives(state)
        to = aligned((core_rows + r) * rows_i, rows_i)
        put_diffused(halo_diffused, to, prims)
        put((halo_plus, halo_minus, halo_metric), to,
            *point_fluxes(state, prims, [unit(0, m, met_core_ref[5 + m, rows, :]) for m in range(3)]))
        edge = aligned(own, rows_i)
        state = [jnp.where(at_end, state_ref[f, edge, :], chip_ref[f, rows, :]) for f in range(5)]
        row = [jnp.where(at_end, met_ref[m, edge, :], met_chip_ref[5 + m, rows, :]) for m in range(3)]
        prims = primitives(state)
        to = aligned((chip_rows + r) * rows_i, rows_i)
        put_diffused(halo_diffused, to, prims)
        put((halo_plus, halo_minus, halo_metric), to,
            *point_fluxes(state, prims, [unit(0, m, row[m]) for m in range(3)]))

    def chord(f, carry):
        def loader(ref, halo, lead):
            def load(n):
                if 0 <= n < rows_i:
                    return ref[lead + (aligned(n * rows_i, rows_i),)]
                r = n + H if n < 0 else n - rows_i + H
                return halo[lead + (aligned(r * rows_i, rows_i),)]

            return load

        def store(n, value):
            rows = aligned(n * rows_i, rows_i)
            acc_ref[f, rows, :] = value + (normal_ref[f, rows, :] + span_acc_ref[f, rows, :])

        sweep(kind, loader(plus_i, halo_plus, (f,)), loader(minus_i, halo_minus, (f,)), loader(diffused_ref, halo_diffused, (f,)),
              loader(metric_i, halo_metric, ()), store, -1, rows_i - 1)
        return carry

    lax.fori_loop(0, 5, chord, 0)

    fetch.wait()
    base = (count - 1 - position) * rows_i
    for i in range(rows_i):
        ghost_ref[i * 16 : i * 16 + 16, :] = wake_ref[aligned((partner_ref[i] - base) * 16, 16), :]
    wall = pl.ds(0, rows_i, stride=rows_i)
    for r in range(H):
        state = [ghost_ref[pl.ds(f * H + r, rows_i, stride=16), :] for f in range(5)]
        prims = primitives(state)
        to = slice(r * rows_i, (r + 1) * rows_i)
        put_diffused(halo_diffused, to, prims)
        put((halo_plus, halo_minus, halo_metric), to,
            *point_fluxes(state, prims, [unit(1, m, met_ref[3 + m, wall, :]) for m in range(3)]))

    def normal(f, carry):
        def rows(n):
            return pl.ds(n, rows_i, stride=rows_i)

        def loader(ref, halo, lead):
            def load(n):
                if n >= 0:
                    return ref[lead + (rows(n),)]
                return halo[lead + (aligned((-1 - n) * rows_i, rows_i),)]

            return load

        def store(n, value):
            acc_ref[f, rows(n), :] = acc_ref[f, rows(n), :] + value

        sweep(kind, loader(plus_j, halo_plus, (f,)), loader(minus_j, halo_minus, (f,)), loader(diffused_ref, halo_diffused, (f,)),
              lambda n: metric_j[rows(max(n, 0)), :], store, -1, 1, open_high=True)
        return carry

    lax.fori_loop(0, 5, normal, 0)

    scale = (time_step / 12.0) * blank_ref[...].astype(F32) / vol_ref[...]
    for f in range(5):
        moved = state_ref[f] + scale * acc_ref[f]
        out_ref[f] = 0.5 * start_ref[f] + 0.5 * moved if final else moved
    if not final:
        for f in range(5):
            def store(start, block, f=f):
                out_span_ref[f, pl.ds(start, height, stride=8), :] = block

            to_span(out_ref[f], store, height)
        send_parts(out_ref, out_span_ref, 5, outs, dims)


def shape(*sizes):
    return jax.ShapeDtypeStruct(sizes, F32)


def exchange(sent):
    core, chip, wake, span_low, span_high = sent
    n, s = lax.axis_size("wrap"), lax.axis_size("span")
    cores = [(i, i ^ 1) for i in range(n)]
    chips = [pair for i in range(1, n - 1, 2) for pair in ((i, i + 1), (i + 1, i))]
    mirror = [(i, n - 1 - i) for i in range(n)]
    ring_up = [(i, (i + 1) % s) for i in range(s)]
    ring_down = [((i + 1) % s, i) for i in range(s)]
    return (lax.ppermute(core, "wrap", cores), lax.ppermute(chip, "wrap", chips), lax.ppermute(wake, "wrap", mirror),
            lax.ppermute(span_high, "span", ring_up), lax.ppermute(span_low, "span", ring_down))


def body(density, velocity, pressure, metrics, volume, wake_partner, iblank):
    rows_i, rows_j, lanes = density.shape
    total, height = rows_i * rows_j, lanes // 4
    dims = (rows_i, height)
    volume, blank = volume.reshape(total, lanes), iblank.reshape(total, lanes)
    whole = pl.BlockSpec(memory_space=pltpu.VMEM)
    far = pl.BlockSpec(memory_space=pltpu.HBM)
    wake_partner = pltpu.with_memory_space_constraint(wake_partner, pltpu.HBM)
    params = pltpu.CompilerParams(vmem_limit_bytes=16 * 2**20)

    def call(kernel, name, ins, outs, scratch, specs=None, cost=0):
        return pl.pallas_call(
            kernel,
            out_shape=outs,
            in_specs=specs or [whole] * len(ins),
            out_specs=[whole] * len(outs),
            scratch_shapes=scratch,
            compiler_params=params,
            cost_estimate=pl.CostEstimate(flops=cost, bytes_accessed=cost // 4, transcendentals=0),
            name=name,
        )(*ins)

    def parts(fields):
        edge = H * rows_j
        return [shape(fields, edge, lanes), shape(fields, edge, lanes), shape(rows_i * 16, lanes),
                shape(fields, 8, lanes), shape(fields, 8, lanes)]

    field, span_rows, halo = shape(5, total, lanes), height * 8, 2 * H * rows_i
    state, span, met, *sent = call(
        functools.partial(prepare_kernel, dims), "prepare",
        [pltpu.with_memory_space_constraint(one, pltpu.HBM) for one in (
            density.reshape(total, lanes), velocity.reshape(3, total, lanes), pressure.reshape(total, lanes),
            metrics.reshape(9, total, lanes))],
        [field, shape(8, total, lanes), shape(9, total, lanes)] + parts(8),
        [pltpu.VMEM((total, lanes), F32), pltpu.VMEM((3, total, lanes), F32), pltpu.VMEM((total, lanes), F32),
         pltpu.SemaphoreType.DMA((6,))],
        [far] * 4,
    )
    span_met = span

    def halo_scratch(rows):
        return [pltpu.VMEM((5, rows, lanes), F32), pltpu.VMEM((5, rows, lanes), F32), pltpu.VMEM((rows, lanes), F32),
                pltpu.VMEM((5, rows, lanes), F32)]

    metric_halo = None
    start = state
    for final in (False, True):
        kind = jnp.bfloat16 if final else F32
        core, chip, wake, span_low, span_high = exchange(sent)
        if metric_halo is None:
            metric_halo = core, chip, span_low, span_high
        line, span_line = shape(5, total, lanes), shape(5, span_rows, lanes)
        normal, *lines = call(
            functools.partial(early_kernel, dims, kind), "early", (state, span, span_met, met),
            [field, line, line, shape(total, lanes), line, line, shape(total, lanes), line,
             span_line, span_line, shape(span_rows, lanes), span_line],
            [], cost=10**8,
        )
        plus_i, minus_i, metric_i, plus_j, minus_j, metric_j, diffused = lines[:7]
        (span_acc,) = call(
            functools.partial(span_kernel, dims, kind), "span",
            (span, span_met, span_low, span_high, metric_halo[2], metric_halo[3], *lines[7:]),
            [field],
            [pltpu.VMEM((5, span_rows, lanes), F32)] + halo_scratch(2 * H * 8) + [pltpu.VMEM((8, 2 * H * 8, lanes), F32)],
            cost=10**8,
        )
        ins = (state, met, volume, blank, wake_partner, core, chip, metric_halo[0], metric_halo[1], wake, normal, span_acc,
               plus_i, minus_i, metric_i, plus_j, minus_j, metric_j, diffused)
        ins += (start,) if final else ()
        state, *rest = call(
            functools.partial(late_kernel, dims, kind, final), "late", ins,
            [field] if final else [field, field] + parts(5),
            [pltpu.VMEM((5, total, lanes), F32)] + halo_scratch(halo) + [pltpu.VMEM((rows_i * 16, lanes), F32)]
            + [pltpu.SMEM((rows_i,), jnp.int32), pltpu.SemaphoreType.DMA],
            [whole] * 4 + [far] + [whole] * (len(ins) - 5),
            cost=10**8,
        )
        if not final:
            span, *sent = rest
    return state.reshape(5, rows_i, rows_j, lanes)


def solution(mesh):
    placed = (
        P("wrap", None, "span"),
        P(None, "wrap", None, "span"),
        P("wrap", None, "span"),
        P(None, "wrap", None, "span"),
        P("wrap", None, "span"),
        P("wrap"),
        P("wrap", None, "span"),
    )
    return jax.shard_map(
        body, mesh=mesh, in_specs=placed, out_specs=P(None, "wrap", None, "span"), check_vma=False
    )
```

```python
import functools

import jax
import jax.numpy as jnp
from jax import lax
from jax.experimental import pallas as pl
from jax.experimental.pallas import tpu as pltpu
from jax.sharding import PartitionSpec as P

epsilon = 1e-06
viscosity = 0.8
conduction = 1.0
time_step = 0.05
H = 3
F32 = jnp.float32


def primitives(state):
    rho, m0, m1, m2, energy = state
    inverse = 1.0 / rho
    velocity = (m0 * inverse, m1 * inverse, m2 * inverse)
    speed_sq = velocity[0] * velocity[0] + velocity[1] * velocity[1] + velocity[2] * velocity[2]
    pressure = 0.4 * (energy - 0.5 * rho * speed_sq)
    ratio = pressure * inverse
    heat = 0.5 * speed_sq + conduction * ratio
    return velocity, pressure, energy + pressure, 1.4 * ratio, heat


def point_fluxes(state, prims, row):
    rho, m0, m1, m2, _ = state
    (u0, u1, u2), pressure, enthalpy, sound_sq, _ = prims
    x0, x1, x2 = row
    contra = x0 * u0 + x1 * u1 + x2 * u2
    metric_sq = x0 * x0 + x1 * x1 + x2 * x2
    square = sound_sq * metric_sq
    speed = jnp.abs(contra) + square * lax.rsqrt(jnp.maximum(square, 1e-30))
    fluxes = (
        rho * contra,
        m0 * contra + x0 * pressure,
        m1 * contra + x1 * pressure,
        m2 * contra + x2 * pressure,
        enthalpy * contra,
    )
    waves = [speed * one for one in state]
    plus = [a + b for a, b in zip(fluxes, waves)]
    minus = [a - b for a, b in zip(fluxes, waves)]
    return plus, minus, metric_sq * (12.0 * viscosity * 0.5)


def RCP(x):
    return pl.reciprocal(x, approx=True)


class Split:
    def __init__(self, load, kind):
        self.load, self.memo, self.kind = load, {}, kind

    def get(self, name, n):
        if (name, n) not in self.memo:
            self.memo[name, n] = getattr(self, "make_" + name)(n)
        return self.memo[name, n]

    def make_v(self, n):
        return self.load(n)

    def make_d(self, n):
        return self.get("v", n + 1) - self.get("v", n)

    def make_e(self, n):
        return self.get("d", n) - self.get("d", n - 1)

    def make_t(self, n):
        return self.get("e", n + 1) - self.get("e", n)

    def make_near(self, n):
        return self.get("t", n).astype(self.kind)

    def make_near2(self, n):
        return self.get("near", n) + self.get("near", n)

    def make_low(self, n):
        return self.get("d", n).astype(self.kind)

    def make_smooth(self, n):
        high, low = self.get("low", n), self.get("low", n - 1)
        bend = self.get("e", n).astype(self.kind)
        twice = bend + bend
        a, b = high * twice, low * twice
        centre = (a - b) * self.kind(2.0 / 3.0) + (high * low + self.kind(16.0 * epsilon / 3.0))
        return centre + a, centre, centre - b

    def correction(self, outer, middle, inner, near, far):
        left = middle * RCP(outer)
        right = middle * RCP(inner)
        weight_left = left * left * self.kind(1.0 / 3.0)
        weight_right = right * right
        total = (weight_left + weight_right) + self.kind(2.0)
        return (weight_left * near + weight_right * far) * RCP(total)


def sweep(kind, load_plus, load_minus, load_diffused, load_metric, store, first, last, open_low=False, open_high=False):
    plus, minus = Split(load_plus, kind), Split(load_minus, kind)
    central, diffused, metric = {}, {}, {}

    def tripled(n):
        if n not in central:
            central[n] = 3.0 * (plus.get("v", n) + minus.get("v", n))
        return central[n]

    def cached(table, load, n):
        if n not in table:
            table[n] = load(n)
        return table[n]

    before = None
    for n in range(first, last + 1):
        up = plus.correction(
            plus.get("smooth", n - 1)[0],
            plus.get("smooth", n)[1],
            plus.get("smooth", n + 1)[2],
            plus.get("near2", n - 1),
            plus.get("near", n),
        )
        down = minus.correction(
            minus.get("smooth", n + 2)[2],
            minus.get("smooth", n + 1)[1],
            minus.get("smooth", n)[0],
            minus.get("near2", n + 1),
            minus.get("near", n),
        )
        flux = (tripled(n) + tripled(n + 1)) - (plus.get("e", n) + minus.get("e", n + 1)) + (down - up).astype(F32)
        face_metric = cached(metric, load_metric, n) + cached(metric, load_metric, n + 1)
        jump = cached(diffused, load_diffused, n + 1) - cached(diffused, load_diffused, n)
        net = face_metric * jump - flux
        if before is not None:
            store(n, net - before)
        elif open_low:
            store(n, net)
        before = net
    if open_high:
        store(last + 1, -before)


def put(refs, rows, plus, minus, metric=None):
    plus_ref, minus_ref, metric_ref = refs
    for f in range(5):
        plus_ref[f, rows, :] = plus[f]
        minus_ref[f, rows, :] = minus[f]
    if metric is not None:
        metric_ref[rows, :] = metric


def put_diffused(ref, rows, prims):
    for m in range(3):
        ref[1 + m, rows, :] = prims[0][m]
    ref[4, rows, :] = prims[4]


def aligned(start, count):
    return pl.ds(pl.multiple_of(start, 8), count)


def unit(which, m, value):
    return value + 1.0 if which == m else value


def to_span(value, store, height):
    for half in range(2):
        turned = value[half * 128 : (half + 1) * 128].T
        for q in range(4):
            store(q * 2 + half, turned[q * height : (q + 1) * height])


def send_parts(state_ref, span_ref, fields, outs, dims):
    rows_i, height = dims
    total = rows_i * rows_i
    core_ref, chip_ref, wake_ref, span_low_ref, span_high_ref = outs
    even = lax.rem(lax.axis_index("wrap"), 2) == 0
    edge = H * rows_i
    to_core, to_chip = jnp.where(even, total - edge, 0), jnp.where(even, 0, total - edge)
    for f in range(5):
        core_ref[f] = state_ref[f, aligned(to_core, edge), :]
        chip_ref[f] = state_ref[f, aligned(to_chip, edge), :]
        for r in range(H):
            wake_ref[pl.ds(f * H + r, rows_i, stride=16), :] = state_ref[f, pl.ds(r + 1, rows_i, stride=rows_i), :]
    for f in range(fields):
        for r in range(H):
            span_low_ref[f, 2 * r : 2 * r + 2, :] = span_ref[f, r * 8 : r * 8 + 2, :]
            top = (height - H + r) * 8
            span_high_ref[f, 2 * r : 2 * r + 2, :] = span_ref[f, top + 6 : top + 8, :]


def prepare_kernel(dims, rho_hbm, vel_hbm, pre_hbm, met_hbm, state_ref, span_ref, met_ref, *refs):
    outs, (rho_ref, vel_ref, pre_ref, sems) = refs[:5], refs[5:]
    rows_i, height = dims
    total = rows_i * rows_i
    pairs = [(rho_hbm, rho_ref), (vel_hbm, vel_ref), (pre_hbm, pre_ref)]
    pairs += [(met_hbm.at[pl.ds(3 * d, 3)], met_ref.at[pl.ds(3 * d, 3)]) for d in (2, 0, 1)]
    copies = [pltpu.make_async_copy(a, b, sems.at[n]) for n, (a, b) in enumerate(pairs)]
    for copy in copies:
        copy.start()
    for copy in copies[:3]:
        copy.wait()
    rho, pressure = rho_ref[...], pre_ref[...]
    u = [vel_ref[m] for m in range(3)]
    speed_sq = u[0] * u[0] + u[1] * u[1] + u[2] * u[2]
    state_ref[0] = rho
    for m in range(3):
        state_ref[1 + m] = rho * u[m]
    state_ref[4] = pressure * (1.0 / 0.4) + 0.5 * rho * speed_sq
    core_ref, chip_ref = outs[:2]
    for f in range(8):
        if f == 5:
            copies[3].wait()
        value = state_ref[f] if f < 5 else met_ref[6 + f - 5]

        def store(start, block, f=f):
            span_ref[f, pl.ds(start, height, stride=8), :] = block

        to_span(value, store, height)
    send_parts(state_ref, span_ref, 8, outs, dims)
    copies[4].wait()
    even = lax.rem(lax.axis_index("wrap"), 2) == 0
    edge = H * rows_i
    to_core, to_chip = jnp.where(even, total - edge, 0), jnp.where(even, 0, total - edge)
    for m in range(3):
        core_ref[5 + m] = met_ref[m, aligned(to_core, edge), :]
        chip_ref[5 + m] = met_ref[m, aligned(to_chip, edge), :]
    copies[5].wait()


def early_kernel(dims, kind, state_ref, span_ref, span_met_ref, met_ref, acc_ref, plus_i, minus_i, metric_i, plus_j, minus_j,
                 metric_j, diffused_ref, plus_k, minus_k, metric_k, diffused_k):
    rows_i, height = dims
    diffused_ref[0] = jnp.zeros(diffused_ref.shape[1:], F32)
    diffused_k[0] = jnp.zeros(diffused_k.shape[1:], F32)

    def planes(n, carry):
        rows = aligned(n * rows_i, rows_i)
        state = [state_ref[f, rows, :] for f in range(5)]
        prims = primitives(state)
        put_diffused(diffused_ref, rows, prims)
        put((plus_i, minus_i, metric_i), rows,
            *point_fluxes(state, prims, [unit(0, m, met_ref[m, rows, :]) for m in range(3)]))
        put((plus_j, minus_j, metric_j), rows,
            *point_fluxes(state, prims, [unit(1, m, met_ref[3 + m, rows, :]) for m in range(3)]))
        return carry

    lax.fori_loop(0, rows_i, planes, 0, unroll=2)

    def spans(n, carry):
        rows = aligned(n * 16, 16)
        state = [span_ref[f, rows, :] for f in range(5)]
        prims = primitives(state)
        put_diffused(diffused_k, rows, prims)
        put((plus_k, minus_k, metric_k), rows,
            *point_fluxes(state, prims, [unit(2, m, span_met_ref[5 + m, rows, :]) for m in range(3)]))
        return carry

    lax.fori_loop(0, height // 2, spans, 0, unroll=2)

    def normal(f, carry):
        def rows(n):
            return pl.ds(min(n, rows_i - 1), rows_i, stride=rows_i)

        def store(n, value):
            acc_ref[f, rows(n), :] = value

        for n in range(2):
            store(n, jnp.zeros((rows_i, 128), F32))
        sweep(kind, lambda n: plus_j[f, rows(n), :], lambda n: minus_j[f, rows(n), :], lambda n: diffused_ref[f, rows(n), :],
              lambda n: metric_j[rows(n), :], store, 2, rows_i - 1, open_low=True)
        return carry

    lax.fori_loop(0, 5, normal, 0)


def span_kernel(dims, kind, span_ref, span_met_ref, span_low_ref, span_high_ref, met_low_ref, met_high_ref,
                plus_k, minus_k, metric_k, diffused_k, out_ref,
                acc_ref, halo_plus, halo_minus, halo_metric, halo_diffused, pad_ref):
    rows_i, height = dims
    sublane = lax.broadcasted_iota(jnp.int32, (8, 128), 0)
    halo_diffused[0] = jnp.zeros(halo_diffused.shape[1:], F32)
    for r in range(H):
        for f in range(8):
            low, high = (span_low_ref, span_high_ref) if f < 5 else (met_low_ref, met_high_ref)
            pad_ref[f, r * 8 : r * 8 + 2, :] = low[f, 2 * r : 2 * r + 2, :]
            pad_ref[f, (H + r) * 8 + 6 : (H + r) * 8 + 8, :] = high[f, 2 * r : 2 * r + 2, :]
    for r in range(2 * H):
        rows = slice(r * 8, r * 8 + 8)
        values = []
        for f in range(8):
            ref = span_ref if f < 5 else span_met_ref
            if r < H:
                own = pltpu.roll(ref[f, (height - H + r) * 8 : (height - H + r) * 8 + 8, :], 2, 0)
                values.append(jnp.where(sublane < 2, pad_ref[f, rows, :], own))
            else:
                own = pltpu.roll(ref[f, (r - H) * 8 : (r - H) * 8 + 8, :], 6, 0)
                values.append(jnp.where(sublane >= 6, pad_ref[f, rows, :], own))
        prims = primitives(values[:5])
        put_diffused(halo_diffused, rows, prims)
        put((halo_plus, halo_minus, halo_metric), rows,
            *point_fluxes(values[:5], prims, [unit(2, m, values[5 + m]) for m in range(3)]))

    def sweep_span(f, carry):
        def loader(ref, halo, lead):
            def one(n):
                if 0 <= n < height:
                    return ref[lead + (slice(n * 8, n * 8 + 8),)]
                r = n + H if n < 0 else n - height + H
                return halo[lead + (slice(r * 8, r * 8 + 8),)]

            return lambda n: jnp.concatenate([one(n), one(n + height // 2)], axis=0)

        def store(n, value):
            acc_ref[f, n * 8 : n * 8 + 8, :] = value[:8]
            m = n + height // 2
            acc_ref[f, m * 8 : m * 8 + 8, :] = value[8:]

        sweep(kind, loader(plus_k, halo_plus, (f,)), loader(minus_k, halo_minus, (f,)), loader(diffused_k, halo_diffused, (f,)),
              loader(metric_k, halo_metric, ()), store, -1, height // 2 - 1)
        return carry

    lax.fori_loop(0, 5, sweep_span, 0)
    for f in range(5):
        for half in range(2):
            parts = [acc_ref[f, pl.ds(q * 2 + half, height, stride=8), :] for q in range(4)]
            out_ref[f, half * 128 : (half + 1) * 128, :] = jnp.concatenate(parts, axis=0).T


def late_kernel(dims, kind, final, *refs):
    rows_i, height = dims
    total = rows_i * rows_i
    (state_ref, met_ref, vol_ref, blank_ref, partner_hbm, core_ref, chip_ref, met_core_ref, met_chip_ref, wake_ref,
     normal_ref, span_acc_ref, plus_i, minus_i, metric_i, plus_j, minus_j, metric_j, diffused_ref) = refs[:19]
    refs = refs[19:]
    if final:
        start_ref, out_ref = refs[:2]
        refs = refs[2:]
    else:
        out_ref, out_span_ref = refs[:2]
        outs, refs = refs[2:7], refs[7:]
    acc_ref, halo_plus, halo_minus, halo_metric, halo_diffused, ghost_ref, partner_ref, sem = refs
    fetch = pltpu.make_async_copy(partner_hbm, partner_ref, sem)
    fetch.start()
    position, count = lax.axis_index("wrap"), lax.axis_size("wrap")
    even = lax.rem(position, 2) == 0
    at_end = (position == 0) | (position == count - 1)
    halo_diffused[0] = jnp.zeros(halo_diffused.shape[1:], F32)

    core_rows, chip_rows = jnp.where(even, H, 0), jnp.where(even, 0, H)
    own = jnp.where(even, 0, total - rows_i)
    for r in range(H):
        rows = slice(r * rows_i, (r + 1) * rows_i)
        state = [core_ref[f, rows, :] for f in range(5)]
        prims = primitives(state)
        to = aligned((core_rows + r) * rows_i, rows_i)
        put_diffused(halo_diffused, to, prims)
        put((halo_plus, halo_minus, halo_metric), to,
            *point_fluxes(state, prims, [unit(0, m, met_core_ref[5 + m, rows, :]) for m in range(3)]))
        edge = aligned(own, rows_i)
        state = [jnp.where(at_end, state_ref[f, edge, :], chip_ref[f, rows, :]) for f in range(5)]
        row = [jnp.where(at_end, met_ref[m, edge, :], met_chip_ref[5 + m, rows, :]) for m in range(3)]
        prims = primitives(state)
        to = aligned((chip_rows + r) * rows_i, rows_i)
        put_diffused(halo_diffused, to, prims)
        put((halo_plus, halo_minus, halo_metric), to,
            *point_fluxes(state, prims, [unit(0, m, row[m]) for m in range(3)]))

    def chord(f, carry):
        def loader(ref, halo, lead):
            def load(n):
                if 0 <= n < rows_i:
                    return ref[lead + (aligned(n * rows_i, rows_i),)]
                r = n + H if n < 0 else n - rows_i + H
                return halo[lead + (aligned(r * rows_i, rows_i),)]

            return load

        def store(n, value):
            rows = aligned(n * rows_i, rows_i)
            acc_ref[f, rows, :] = value + (normal_ref[f, rows, :] + span_acc_ref[f, rows, :])

        sweep(kind, loader(plus_i, halo_plus, (f,)), loader(minus_i, halo_minus, (f,)), loader(diffused_ref, halo_diffused, (f,)),
              loader(metric_i, halo_metric, ()), store, -1, rows_i - 1)
        return carry

    lax.fori_loop(0, 5, chord, 0)

    fetch.wait()
    base = (count - 1 - position) * rows_i
    for i in range(rows_i):
        ghost_ref[i * 16 : i * 16 + 16, :] = wake_ref[aligned((partner_ref[i] - base) * 16, 16), :]
    wall = pl.ds(0, rows_i, stride=rows_i)
    for r in range(H):
        state = [ghost_ref[pl.ds(f * H + r, rows_i, stride=16), :] for f in range(5)]
        prims = primitives(state)
        to = slice(r * rows_i, (r + 1) * rows_i)
        put_diffused(halo_diffused, to, prims)
        put((halo_plus, halo_minus, halo_metric), to,
            *point_fluxes(state, prims, [unit(1, m, met_ref[3 + m, wall, :]) for m in range(3)]))

    def normal(f, carry):
        def rows(n):
            return pl.ds(n, rows_i, stride=rows_i)

        def loader(ref, halo, lead):
            def load(n):
                if n >= 0:
                    return ref[lead + (rows(n),)]
                return halo[lead + (aligned((-1 - n) * rows_i, rows_i),)]

            return load

        def store(n, value):
            acc_ref[f, rows(n), :] = acc_ref[f, rows(n), :] + value

        sweep(kind, loader(plus_j, halo_plus, (f,)), loader(minus_j, halo_minus, (f,)), loader(diffused_ref, halo_diffused, (f,)),
              lambda n: metric_j[rows(max(n, 0)), :], store, -1, 1, open_high=True)
        return carry

    lax.fori_loop(0, 5, normal, 0)

    scale = (time_step / 12.0) * blank_ref[...].astype(F32) / vol_ref[...]
    for f in range(5):
        moved = state_ref[f] + scale * acc_ref[f]
        out_ref[f] = 0.5 * start_ref[f] + 0.5 * moved if final else moved
    if not final:
        for f in range(5):
            def store(start, block, f=f):
                out_span_ref[f, pl.ds(start, height, stride=8), :] = block

            to_span(out_ref[f], store, height)
        send_parts(out_ref, out_span_ref, 5, outs, dims)


def shape(*sizes):
    return jax.ShapeDtypeStruct(sizes, F32)


def exchange(sent):
    core, chip, wake, span_low, span_high = sent
    n, s = lax.axis_size("wrap"), lax.axis_size("span")
    cores = [(i, i ^ 1) for i in range(n)]
    chips = [pair for i in range(1, n, 2) for pair in ((i, (i + 1) % n), ((i + 1) % n, i))]
    mirror = [(i, n - 1 - i) for i in range(n)]
    ring_up = [(i, (i + 1) % s) for i in range(s)]
    ring_down = [((i + 1) % s, i) for i in range(s)]
    return (lax.ppermute(core, "wrap", cores), lax.ppermute(chip, "wrap", chips), lax.ppermute(wake, "wrap", mirror),
            lax.ppermute(span_high, "span", ring_up), lax.ppermute(span_low, "span", ring_down))


def body(density, velocity, pressure, metrics, volume, wake_partner, iblank):
    rows_i, rows_j, lanes = density.shape
    total, height = rows_i * rows_j, lanes // 4
    dims = (rows_i, height)
    volume, blank = volume.reshape(total, lanes), iblank.reshape(total, lanes)
    whole = pl.BlockSpec(memory_space=pltpu.VMEM)
    far = pl.BlockSpec(memory_space=pltpu.HBM)
    wake_partner = pltpu.with_memory_space_constraint(wake_partner, pltpu.HBM)
    params = pltpu.CompilerParams(vmem_limit_bytes=16 * 2**20)

    def call(kernel, name, ins, outs, scratch, specs=None, cost=0):
        return pl.pallas_call(
            kernel,
            out_shape=outs,
            in_specs=specs or [whole] * len(ins),
            out_specs=[whole] * len(outs),
            scratch_shapes=scratch,
            compiler_params=params,
            cost_estimate=pl.CostEstimate(flops=cost, bytes_accessed=cost // 4, transcendentals=0),
            name=name,
        )(*ins)

    def parts(fields):
        edge = H * rows_j
        return [shape(fields, edge, lanes), shape(fields, edge, lanes), shape(rows_i * 16, lanes),
                shape(fields, 8, lanes), shape(fields, 8, lanes)]

    field, span_rows, halo = shape(5, total, lanes), height * 8, 2 * H * rows_i
    state, span, met, *sent = call(
        functools.partial(prepare_kernel, dims), "prepare",
        [pltpu.with_memory_space_constraint(one, pltpu.HBM) for one in (
            density.reshape(total, lanes), velocity.reshape(3, total, lanes), pressure.reshape(total, lanes),
            metrics.reshape(9, total, lanes))],
        [field, shape(8, total, lanes), shape(9, total, lanes)] + parts(8),
        [pltpu.VMEM((total, lanes), F32), pltpu.VMEM((3, total, lanes), F32), pltpu.VMEM((total, lanes), F32),
         pltpu.SemaphoreType.DMA((6,))],
        [far] * 4,
    )
    span_met = span

    def halo_scratch(rows):
        return [pltpu.VMEM((5, rows, lanes), F32), pltpu.VMEM((5, rows, lanes), F32), pltpu.VMEM((rows, lanes), F32),
                pltpu.VMEM((5, rows, lanes), F32)]

    metric_halo = None
    start = state
    for final in (False, True):
        kind = jnp.bfloat16 if final else F32
        core, chip, wake, span_low, span_high = exchange(sent)
        if metric_halo is None:
            metric_halo = core, chip, span_low, span_high
        line, span_line = shape(5, total, lanes), shape(5, span_rows, lanes)
        normal, *lines = call(
            functools.partial(early_kernel, dims, kind), "early", (state, span, span_met, met),
            [field, line, line, shape(total, lanes), line, line, shape(total, lanes), line,
             span_line, span_line, shape(span_rows, lanes), span_line],
            [], cost=10**8,
        )
        plus_i, minus_i, metric_i, plus_j, minus_j, metric_j, diffused = lines[:7]
        (span_acc,) = call(
            functools.partial(span_kernel, dims, kind), "span",
            (span, span_met, span_low, span_high, metric_halo[2], metric_halo[3], *lines[7:]),
            [field],
            [pltpu.VMEM((5, span_rows, lanes), F32)] + halo_scratch(2 * H * 8) + [pltpu.VMEM((8, 2 * H * 8, lanes), F32)],
            cost=10**8,
        )
        ins = (state, met, volume, blank, wake_partner, core, chip, metric_halo[0], metric_halo[1], wake, normal, span_acc,
               plus_i, minus_i, metric_i, plus_j, minus_j, metric_j, diffused)
        ins += (start,) if final else ()
        state, *rest = call(
            functools.partial(late_kernel, dims, kind, final), "late", ins,
            [field] if final else [field, field] + parts(5),
            [pltpu.VMEM((5, total, lanes), F32)] + halo_scratch(halo) + [pltpu.VMEM((rows_i * 16, lanes), F32)]
            + [pltpu.SMEM((rows_i,), jnp.int32), pltpu.SemaphoreType.DMA],
            [whole] * 4 + [far] + [whole] * (len(ins) - 5),
            cost=10**8,
        )
        if not final:
            span, *sent = rest
    return state.reshape(5, rows_i, rows_j, lanes)


def solution(mesh):
    placed = (
        P("wrap", None, "span"),
        P(None, "wrap", None, "span"),
        P("wrap", None, "span"),
        P(None, "wrap", None, "span"),
        P("wrap", None, "span"),
        P("wrap"),
        P("wrap", None, "span"),
    )
    return jax.shard_map(
        body, mesh=mesh, in_specs=placed, out_specs=P(None, "wrap", None, "span"), check_vma=False
    )
```

```python
import functools

import jax
import jax.numpy as jnp
from jax import lax
from jax.experimental import pallas as pl
from jax.experimental.pallas import tpu as pltpu
from jax.sharding import PartitionSpec as P

epsilon = 1e-06
viscosity = 0.8
conduction = 1.0
time_step = 0.05
H = 3
F32 = jnp.float32


def primitives(state):
    rho, m0, m1, m2, energy = state
    inverse = 1.0 / rho
    velocity = (m0 * inverse, m1 * inverse, m2 * inverse)
    speed_sq = velocity[0] * velocity[0] + velocity[1] * velocity[1] + velocity[2] * velocity[2]
    pressure = 0.4 * (energy - 0.5 * rho * speed_sq)
    ratio = pressure * inverse
    heat = 0.5 * speed_sq + conduction * ratio
    return velocity, pressure, energy + pressure, 1.4 * ratio, heat


def point_fluxes(state, prims, row):
    rho, m0, m1, m2, _ = state
    (u0, u1, u2), pressure, enthalpy, sound_sq, _ = prims
    x0, x1, x2 = row
    contra = x0 * u0 + x1 * u1 + x2 * u2
    metric_sq = x0 * x0 + x1 * x1 + x2 * x2
    square = sound_sq * metric_sq
    speed = jnp.abs(contra) + square * lax.rsqrt(jnp.maximum(square, 1e-30))
    fluxes = (
        rho * contra,
        m0 * contra + x0 * pressure,
        m1 * contra + x1 * pressure,
        m2 * contra + x2 * pressure,
        enthalpy * contra,
    )
    waves = [speed * one for one in state]
    plus = [a + b for a, b in zip(fluxes, waves)]
    minus = [a - b for a, b in zip(fluxes, waves)]
    return plus, minus, metric_sq * (12.0 * viscosity * 0.5)


def RCP(x):
    return pl.reciprocal(x, approx=True)


class Split:
    def __init__(self, load, kind):
        self.load, self.memo, self.kind = load, {}, kind

    def get(self, name, n):
        if (name, n) not in self.memo:
            self.memo[name, n] = getattr(self, "make_" + name)(n)
        return self.memo[name, n]

    def make_v(self, n):
        return self.load(n)

    def make_d(self, n):
        return self.get("v", n + 1) - self.get("v", n)

    def make_e(self, n):
        return self.get("d", n) - self.get("d", n - 1)

    def make_t(self, n):
        return self.get("e", n + 1) - self.get("e", n)

    def make_near(self, n):
        return self.get("t", n).astype(self.kind)

    def make_near2(self, n):
        return self.get("near", n) + self.get("near", n)

    def make_low(self, n):
        return self.get("d", n).astype(self.kind)

    def make_smooth(self, n):
        high, low = self.get("low", n), self.get("low", n - 1)
        bend = self.get("e", n).astype(self.kind)
        twice = bend + bend
        a, b = high * twice, low * twice
        centre = (a - b) * self.kind(2.0 / 3.0) + (high * low + self.kind(16.0 * epsilon / 3.0))
        return centre + a, centre, centre - b

    def correction(self, outer, middle, inner, near, far):
        left = middle * RCP(outer)
        right = middle * RCP(inner)
        weight_left = left * left * self.kind(1.0 / 3.0)
        weight_right = right * right
        total = (weight_left + weight_right) + self.kind(2.0)
        return (weight_left * near + weight_right * far) * RCP(total)


def sweep(kind, load_plus, load_minus, load_diffused, load_metric, store, first, last, open_low=False, open_high=False):
    plus, minus = Split(load_plus, kind), Split(load_minus, kind)
    central, diffused, metric = {}, {}, {}

    def tripled(n):
        if n not in central:
            central[n] = 3.0 * (plus.get("v", n) + minus.get("v", n))
        return central[n]

    def cached(table, load, n):
        if n not in table:
            table[n] = load(n)
        return table[n]

    before = None
    for n in range(first, last + 1):
        up = plus.correction(
            plus.get("smooth", n - 1)[0],
            plus.get("smooth", n)[1],
            plus.get("smooth", n + 1)[2],
            plus.get("near2", n - 1),
            plus.get("near", n),
        )
        down = minus.correction(
            minus.get("smooth", n + 2)[2],
            minus.get("smooth", n + 1)[1],
            minus.get("smooth", n)[0],
            minus.get("near2", n + 1),
            minus.get("near", n),
        )
        flux = (tripled(n) + tripled(n + 1)) - (plus.get("e", n) + minus.get("e", n + 1)) + (down - up).astype(F32)
        face_metric = cached(metric, load_metric, n) + cached(metric, load_metric, n + 1)
        jump = cached(diffused, load_diffused, n + 1) - cached(diffused, load_diffused, n)
        net = face_metric * jump - flux
        if before is not None:
            store(n, net - before)
        elif open_low:
            store(n, net)
        before = net
    if open_high:
        store(last + 1, -before)


def put(refs, rows, plus, minus, metric=None):
    plus_ref, minus_ref, metric_ref = refs
    for f in range(5):
        plus_ref[f, rows, :] = plus[f]
        minus_ref[f, rows, :] = minus[f]
    if metric is not None:
        metric_ref[rows, :] = metric


def put_diffused(ref, rows, prims):
    for m in range(3):
        ref[1 + m, rows, :] = prims[0][m]
    ref[4, rows, :] = prims[4]


def aligned(start, count):
    return pl.ds(pl.multiple_of(start, 8), count)


def unit(which, m, value):
    return value + 1.0 if which == m else value


def to_span(value, store, height):
    for half in range(2):
        turned = value[half * 128 : (half + 1) * 128].T
        for q in range(4):
            store(q * 2 + half, turned[q * height : (q + 1) * height])


def send_parts(state_ref, span_ref, fields, outs, dims):
    rows_i, height = dims
    total = rows_i * rows_i
    core_ref, chip_ref, wake_ref, span_near_ref, span_far_ref = outs
    even = lax.rem(lax.axis_index("wrap"), 2) == 0
    edge = H * rows_i
    to_core, to_chip = jnp.where(even, total - edge, 0), jnp.where(even, 0, total - edge)
    for f in range(5):
        core_ref[f] = state_ref[f, aligned(to_core, edge), :]
        chip_ref[f] = state_ref[f, aligned(to_chip, edge), :]
        for r in range(H):
            wake_ref[pl.ds(f * H + r, rows_i, stride=16), :] = state_ref[f, pl.ds(r + 1, rows_i, stride=rows_i), :]
    even = lax.rem(lax.axis_index("span"), 2) == 0
    for f in range(fields):
        for r in range(H):
            top = (height - H + r) * 8
            low, high = span_ref[f, r * 8 : r * 8 + 2, :], span_ref[f, top + 6 : top + 8, :]
            span_near_ref[f, 2 * r : 2 * r + 2, :] = jnp.where(even, high, low)
            span_far_ref[f, 2 * r : 2 * r + 2, :] = jnp.where(even, low, high)


def prepare_kernel(dims, rho_hbm, vel_hbm, pre_hbm, met_hbm, state_ref, span_ref, met_ref, *refs):
    outs, (rho_ref, vel_ref, pre_ref, sems) = refs[:5], refs[5:]
    rows_i, height = dims
    total = rows_i * rows_i
    pairs = [(rho_hbm, rho_ref), (vel_hbm, vel_ref), (pre_hbm, pre_ref)]
    pairs += [(met_hbm.at[pl.ds(3 * d, 3)], met_ref.at[pl.ds(3 * d, 3)]) for d in (2, 0, 1)]
    copies = [pltpu.make_async_copy(a, b, sems.at[n]) for n, (a, b) in enumerate(pairs)]
    for copy in copies:
        copy.start()
    for copy in copies[:3]:
        copy.wait()
    rho, pressure = rho_ref[...], pre_ref[...]
    u = [vel_ref[m] for m in range(3)]
    speed_sq = u[0] * u[0] + u[1] * u[1] + u[2] * u[2]
    state_ref[0] = rho
    for m in range(3):
        state_ref[1 + m] = rho * u[m]
    state_ref[4] = pressure * (1.0 / 0.4) + 0.5 * rho * speed_sq
    core_ref, chip_ref = outs[:2]
    for f in range(8):
        if f == 5:
            copies[3].wait()
        value = state_ref[f] if f < 5 else met_ref[6 + f - 5]

        def store(start, block, f=f):
            span_ref[f, pl.ds(start, height, stride=8), :] = block

        to_span(value, store, height)
    send_parts(state_ref, span_ref, 8, outs, dims)
    copies[4].wait()
    even = lax.rem(lax.axis_index("wrap"), 2) == 0
    edge = H * rows_i
    to_core, to_chip = jnp.where(even, total - edge, 0), jnp.where(even, 0, total - edge)
    for m in range(3):
        core_ref[5 + m] = met_ref[m, aligned(to_core, edge), :]
        chip_ref[5 + m] = met_ref[m, aligned(to_chip, edge), :]
    copies[5].wait()


def early_kernel(dims, kind, state_ref, span_ref, span_met_ref, met_ref, acc_ref, plus_i, minus_i, metric_i, plus_j, minus_j,
                 metric_j, diffused_ref, plus_k, minus_k, metric_k, diffused_k):
    rows_i, height = dims
    diffused_ref[0] = jnp.zeros(diffused_ref.shape[1:], F32)
    diffused_k[0] = jnp.zeros(diffused_k.shape[1:], F32)

    def planes(n, carry):
        rows = aligned(n * rows_i, rows_i)
        state = [state_ref[f, rows, :] for f in range(5)]
        prims = primitives(state)
        put_diffused(diffused_ref, rows, prims)
        put((plus_i, minus_i, metric_i), rows,
            *point_fluxes(state, prims, [unit(0, m, met_ref[m, rows, :]) for m in range(3)]))
        put((plus_j, minus_j, metric_j), rows,
            *point_fluxes(state, prims, [unit(1, m, met_ref[3 + m, rows, :]) for m in range(3)]))
        return carry

    lax.fori_loop(0, rows_i, planes, 0, unroll=2)

    def spans(n, carry):
        rows = aligned(n * 16, 16)
        state = [span_ref[f, rows, :] for f in range(5)]
        prims = primitives(state)
        put_diffused(diffused_k, rows, prims)
        put((plus_k, minus_k, metric_k), rows,
            *point_fluxes(state, prims, [unit(2, m, span_met_ref[5 + m, rows, :]) for m in range(3)]))
        return carry

    lax.fori_loop(0, height // 2, spans, 0, unroll=2)

    def normal(f, carry):
        def rows(n):
            return pl.ds(min(n, rows_i - 1), rows_i, stride=rows_i)

        def store(n, value):
            acc_ref[f, rows(n), :] = value

        for n in range(2):
            store(n, jnp.zeros((rows_i, 128), F32))
        sweep(kind, lambda n: plus_j[f, rows(n), :], lambda n: minus_j[f, rows(n), :], lambda n: diffused_ref[f, rows(n), :],
              lambda n: metric_j[rows(n), :], store, 2, rows_i - 1, open_low=True)
        return carry

    lax.fori_loop(0, 5, normal, 0)


def chord_kernel(dims, kind, state_ref, met_ref, core_ref, chip_ref, met_core_ref, met_chip_ref, normal_ref,
                 plus_i, minus_i, metric_i, diffused_ref, acc_ref, halo_plus, halo_minus, halo_metric, halo_diffused):
    rows_i, height = dims
    total = rows_i * rows_i
    position, count = lax.axis_index("wrap"), lax.axis_size("wrap")
    even = lax.rem(position, 2) == 0
    at_end = (position == 0) | (position == count - 1)
    halo_diffused[0] = jnp.zeros(halo_diffused.shape[1:], F32)

    core_rows, chip_rows = jnp.where(even, H, 0), jnp.where(even, 0, H)
    own = jnp.where(even, 0, total - rows_i)
    for r in range(H):
        rows = slice(r * rows_i, (r + 1) * rows_i)
        state = [core_ref[f, rows, :] for f in range(5)]
        prims = primitives(state)
        to = aligned((core_rows + r) * rows_i, rows_i)
        put_diffused(halo_diffused, to, prims)
        put((halo_plus, halo_minus, halo_metric), to,
            *point_fluxes(state, prims, [unit(0, m, met_core_ref[5 + m, rows, :]) for m in range(3)]))
        edge = aligned(own, rows_i)
        state = [jnp.where(at_end, state_ref[f, edge, :], chip_ref[f, rows, :]) for f in range(5)]
        row = [jnp.where(at_end, met_ref[m, edge, :], met_chip_ref[5 + m, rows, :]) for m in range(3)]
        prims = primitives(state)
        to = aligned((chip_rows + r) * rows_i, rows_i)
        put_diffused(halo_diffused, to, prims)
        put((halo_plus, halo_minus, halo_metric), to,
            *point_fluxes(state, prims, [unit(0, m, row[m]) for m in range(3)]))

    def chord(f, carry):
        def loader(ref, halo, lead):
            def load(n):
                if 0 <= n < rows_i:
                    return ref[lead + (aligned(n * rows_i, rows_i),)]
                r = n + H if n < 0 else n - rows_i + H
                return halo[lead + (aligned(r * rows_i, rows_i),)]

            return load

        def store(n, value):
            rows = aligned(n * rows_i, rows_i)
            acc_ref[f, rows, :] = value + normal_ref[f, rows, :]

        sweep(kind, loader(plus_i, halo_plus, (f,)), loader(minus_i, halo_minus, (f,)), loader(diffused_ref, halo_diffused, (f,)),
              loader(metric_i, halo_metric, ()), store, -1, rows_i - 1)
        return carry

    lax.fori_loop(0, 5, chord, 0)


def span_kernel(dims, kind, final, *refs):
    rows_i, height = dims
    (span_ref, span_met_ref, span_near_ref, span_far_ref, met_near_ref, met_far_ref, plus_k, minus_k, metric_k, diffused_k,
     partner_hbm, state_ref, met_ref, vol_ref, blank_ref, wake_ref, plane_ref, plus_j, minus_j, metric_j,
     diffused_ref) = refs[:21]
    refs = refs[21:]
    if final:
        start_ref, out_ref = refs[:2]
        refs = refs[2:]
    else:
        out_ref, out_span_ref = refs[:2]
        outs, refs = refs[2:7], refs[7:]
    (acc_ref, halo_plus, halo_minus, halo_metric, halo_diffused, pad_ref, wall_ref, sum_ref,
     ghost_plus, ghost_minus, ghost_metric, ghost_diffused, ghost_ref, partner_ref, sem) = refs[:15]
    if final:
        staged_ref, out_sems = refs[15:]
    fetch = pltpu.make_async_copy(partner_hbm, partner_ref, sem)
    fetch.start()
    position, count = lax.axis_index("wrap"), lax.axis_size("wrap")
    ghost_diffused[0] = jnp.zeros(ghost_diffused.shape[1:], F32)
    even = lax.rem(lax.axis_index("span"), 2) == 0
    sublane = lax.broadcasted_iota(jnp.int32, (8, 128), 0)
    halo_diffused[0] = jnp.zeros(halo_diffused.shape[1:], F32)
    for r in range(H):
        for f in range(8):
            near_ref, far_ref = (span_near_ref, span_far_ref) if f < 5 else (met_near_ref, met_far_ref)
            near, far = near_ref[f, 2 * r : 2 * r + 2, :], far_ref[f, 2 * r : 2 * r + 2, :]
            pad_ref[f, r * 8 : r * 8 + 2, :] = jnp.where(even, far, near)
            pad_ref[f, (H + r) * 8 + 6 : (H + r) * 8 + 8, :] = jnp.where(even, near, far)
    for r in range(2 * H):
        rows = slice(r * 8, r * 8 + 8)
        values = []
        for f in range(8):
            ref = span_ref if f < 5 else span_met_ref
            if r < H:
                own = pltpu.roll(ref[f, (height - H + r) * 8 : (height - H + r) * 8 + 8, :], 2, 0)
                values.append(jnp.where(sublane < 2, pad_ref[f, rows, :], own))
            else:
                own = pltpu.roll(ref[f, (r - H) * 8 : (r - H) * 8 + 8, :], 6, 0)
                values.append(jnp.where(sublane >= 6, pad_ref[f, rows, :], own))
        prims = primitives(values[:5])
        put_diffused(halo_diffused, rows, prims)
        put((halo_plus, halo_minus, halo_metric), rows,
            *point_fluxes(values[:5], prims, [unit(2, m, values[5 + m]) for m in range(3)]))

    def sweep_span(f, carry):
        def loader(ref, halo, lead):
            def one(n):
                if 0 <= n < height:
                    return ref[lead + (slice(n * 8, n * 8 + 8),)]
                r = n + H if n < 0 else n - height + H
                return halo[lead + (slice(r * 8, r * 8 + 8),)]

            return lambda n: jnp.concatenate([one(n), one(n + height // 2)], axis=0)

        def store(n, value):
            acc_ref[f, n * 8 : n * 8 + 8, :] = value[:8]
            m = n + height // 2
            acc_ref[f, m * 8 : m * 8 + 8, :] = value[8:]

        sweep(kind, loader(plus_k, halo_plus, (f,)), loader(minus_k, halo_minus, (f,)), loader(diffused_k, halo_diffused, (f,)),
              loader(metric_k, halo_metric, ()), store, -1, height // 2 - 1)
        return carry

    lax.fori_loop(0, 5, sweep_span, 0)

    fetch.wait()
    base = (count - 1 - position) * rows_i
    for i in range(rows_i):
        ghost_ref[i * 16 : i * 16 + 16, :] = wake_ref[aligned((partner_ref[i] - base) * 16, 16), :]
    wall = pl.ds(0, rows_i, stride=rows_i)
    for r in range(H):
        state = [ghost_ref[pl.ds(f * H + r, rows_i, stride=16), :] for f in range(5)]
        prims = primitives(state)
        to = slice(r * rows_i, (r + 1) * rows_i)
        put_diffused(ghost_diffused, to, prims)
        put((ghost_plus, ghost_minus, ghost_metric), to,
            *point_fluxes(state, prims, [unit(1, m, met_ref[3 + m, wall, :]) for m in range(3)]))

    def normal(f, carry):
        def rows(n):
            return pl.ds(n, rows_i, stride=rows_i)

        def loader(ref, halo, lead):
            def load(n):
                if n >= 0:
                    return ref[lead + (rows(n),)]
                return halo[lead + (aligned((-1 - n) * rows_i, rows_i),)]

            return load

        def store(n, value):
            wall_ref[f, n * rows_i : (n + 1) * rows_i, :] = value

        sweep(kind, loader(plus_j, ghost_plus, (f,)), loader(minus_j, ghost_minus, (f,)), loader(diffused_ref, ghost_diffused, (f,)),
              lambda n: metric_j[rows(max(n, 0)), :], store, -1, 1, open_high=True)
        return carry

    lax.fori_loop(0, 5, normal, 0)

    scale = (time_step / 12.0) * blank_ref[...].astype(F32) / vol_ref[...]
    for f in range(5):
        for half in range(2):
            parts = [acc_ref[f, pl.ds(q * 2 + half, height, stride=8), :] for q in range(4)]
            rows = slice(half * 128, (half + 1) * 128)
            sum_ref[f, rows, :] = plane_ref[f, rows, :] + jnp.concatenate(parts, axis=0).T
        for n in range(H):
            rows = pl.ds(n, rows_i, stride=rows_i)
            sum_ref[f, rows, :] = sum_ref[f, rows, :] + wall_ref[f, n * rows_i : (n + 1) * rows_i, :]
        moved = state_ref[f] + scale * sum_ref[f]
        if final:
            staged_ref[f] = 0.5 * start_ref[f] + 0.5 * moved
            pltpu.make_async_copy(staged_ref.at[f], out_ref.at[f], out_sems.at[f]).start()
        else:
            out_ref[f] = moved
    if final:
        for f in range(5):
            pltpu.make_async_copy(staged_ref.at[f], out_ref.at[f], out_sems.at[f]).wait()
    if not final:
        for f in range(5):
            def store(start, block, f=f):
                out_span_ref[f, pl.ds(start, height, stride=8), :] = block

            to_span(out_ref[f], store, height)
        send_parts(out_ref, out_span_ref, 5, outs, dims)


def shape(*sizes):
    return jax.ShapeDtypeStruct(sizes, F32)


def exchange(sent):
    core, chip, wake, span_near, span_far = sent
    n, s = lax.axis_size("wrap"), lax.axis_size("span")
    cores = [(i, i ^ 1) for i in range(n)]
    chips = [pair for i in range(1, n, 2) for pair in ((i, (i + 1) % n), ((i + 1) % n, i))]
    mirror = [(i, n - 1 - i) for i in range(n)]
    near = [(i, i ^ 1) for i in range(s)]
    far = [pair for i in range(1, s, 2) for pair in ((i, (i + 1) % s), ((i + 1) % s, i))]
    return (lax.ppermute(core, "wrap", cores), lax.ppermute(chip, "wrap", chips), lax.ppermute(wake, "wrap", mirror),
            lax.ppermute(span_near, "span", near), lax.ppermute(span_far, "span", far))


def body(density, velocity, pressure, metrics, volume, wake_partner, iblank):
    rows_i, rows_j, lanes = density.shape
    total, height = rows_i * rows_j, lanes // 4
    dims = (rows_i, height)
    volume, blank = volume.reshape(total, lanes), iblank.reshape(total, lanes)
    whole = pl.BlockSpec(memory_space=pltpu.VMEM)
    far = pl.BlockSpec(memory_space=pltpu.HBM)
    wake_partner = pltpu.with_memory_space_constraint(wake_partner, pltpu.HBM)
    params = pltpu.CompilerParams(vmem_limit_bytes=16 * 2**20)

    def call(kernel, name, ins, outs, scratch, specs=None, cost=0, out_specs=None):
        return pl.pallas_call(
            kernel,
            out_shape=outs,
            in_specs=specs or [whole] * len(ins),
            out_specs=out_specs or [whole] * len(outs),
            scratch_shapes=scratch,
            compiler_params=params,
            cost_estimate=pl.CostEstimate(flops=cost, bytes_accessed=cost // 4, transcendentals=0),
            name=name,
        )(*ins)

    def parts(fields):
        edge = H * rows_j
        return [shape(fields, edge, lanes), shape(fields, edge, lanes), shape(rows_i * 16, lanes),
                shape(fields, 8, lanes), shape(fields, 8, lanes)]

    field, span_rows, halo = shape(5, total, lanes), height * 8, 2 * H * rows_i
    state, span, met, *sent = call(
        functools.partial(prepare_kernel, dims), "prepare",
        [pltpu.with_memory_space_constraint(one, pltpu.HBM) for one in (
            density.reshape(total, lanes), velocity.reshape(3, total, lanes), pressure.reshape(total, lanes),
            metrics.reshape(9, total, lanes))],
        [field, shape(8, total, lanes), shape(9, total, lanes)] + parts(8),
        [pltpu.VMEM((total, lanes), F32), pltpu.VMEM((3, total, lanes), F32), pltpu.VMEM((total, lanes), F32),
         pltpu.SemaphoreType.DMA((6,))],
        [far] * 4,
    )
    span_met = span

    def halo_scratch(rows):
        return [pltpu.VMEM((5, rows, lanes), F32), pltpu.VMEM((5, rows, lanes), F32), pltpu.VMEM((rows, lanes), F32),
                pltpu.VMEM((5, rows, lanes), F32)]

    metric_halo = None
    start = state
    for final in (False, True):
        kind = jnp.bfloat16 if final else F32
        core, chip, wake, span_near, span_far = exchange(sent)
        if metric_halo is None:
            metric_halo = core, chip, span_near, span_far
        line, span_line = shape(5, total, lanes), shape(5, span_rows, lanes)
        normal, *lines = call(
            functools.partial(early_kernel, dims, kind), "early", (state, span, span_met, met),
            [field, line, line, shape(total, lanes), line, line, shape(total, lanes), line,
             span_line, span_line, shape(span_rows, lanes), span_line],
            [], cost=10**8,
        )
        plus_i, minus_i, metric_i, plus_j, minus_j, metric_j, diffused = lines[:7]
        (plane,) = call(
            functools.partial(chord_kernel, dims, kind), "chord",
            (state, met, core, chip, metric_halo[0], metric_halo[1], normal, plus_i, minus_i, metric_i, diffused),
            [field], halo_scratch(halo), cost=10**8,
        )
        ins = (span, span_met, span_near, span_far, metric_halo[2], metric_halo[3], *lines[7:], wake_partner, state, met,
               volume, blank, wake, plane, plus_j, minus_j, metric_j, diffused)
        ins += (start,) if final else ()
        state, *rest = call(
            functools.partial(span_kernel, dims, kind, final), "span", ins,
            [field] if final else [field, field] + parts(5),
            [pltpu.VMEM((5, span_rows, lanes), F32)] + halo_scratch(2 * H * 8) + [pltpu.VMEM((8, 2 * H * 8, lanes), F32)]
            + [pltpu.VMEM((5, H * rows_i, lanes), F32), pltpu.VMEM((5, total, lanes), F32)] + halo_scratch(H * rows_i)
            + [pltpu.VMEM((rows_i * 16, lanes), F32), pltpu.SMEM((rows_i,), jnp.int32), pltpu.SemaphoreType.DMA]
            + ([pltpu.VMEM((5, total, lanes), F32), pltpu.SemaphoreType.DMA((5,))] if final else []),
            [whole] * 10 + [far] + [whole] * (len(ins) - 11),
            cost=10**8, out_specs=[far] if final else None,
        )
        if not final:
            span, *sent = rest
    return state.reshape(5, rows_i, rows_j, lanes)


def solution(mesh):
    placed = (
        P("wrap", None, "span"),
        P(None, "wrap", None, "span"),
        P("wrap", None, "span"),
        P(None, "wrap", None, "span"),
        P("wrap", None, "span"),
        P("wrap"),
        P("wrap", None, "span"),
    )
    return jax.shard_map(
        body, mesh=mesh, in_specs=placed, out_specs=P(None, "wrap", None, "span"), check_vma=False
    )
```

```python
import functools

import jax
import jax.numpy as jnp
from jax import lax
from jax.experimental import pallas as pl
from jax.experimental.pallas import tpu as pltpu
from jax.sharding import PartitionSpec as P

epsilon = 1e-06
viscosity = 0.8
conduction = 1.0
time_step = 0.05
metric_scale = 12.0 * viscosity * 0.5
H = 3
F32 = jnp.float32


def primitives(state):
    rho, m0, m1, m2, energy = state
    inverse = 1.0 / rho
    velocity = (m0 * inverse, m1 * inverse, m2 * inverse)
    speed_sq = velocity[0] * velocity[0] + velocity[1] * velocity[1] + velocity[2] * velocity[2]
    pressure = 0.4 * (energy - 0.5 * rho * speed_sq)
    ratio = pressure * inverse
    heat = 0.5 * speed_sq + conduction * ratio
    return velocity, pressure, energy + pressure, (1.4 / metric_scale) * ratio, heat


def point_fluxes(state, prims, row, metric=None):
    rho, m0, m1, m2, _ = state
    (u0, u1, u2), pressure, enthalpy, sound_sq, _ = prims
    x0, x1, x2 = row
    contra = x0 * u0 + x1 * u1 + x2 * u2
    if metric is None:
        metric = (x0 * x0 + x1 * x1 + x2 * x2) * metric_scale
    square = sound_sq * metric
    speed = jnp.abs(contra) + square * lax.rsqrt(jnp.maximum(square, 1e-30))
    fluxes = (
        rho * contra,
        m0 * contra + x0 * pressure,
        m1 * contra + x1 * pressure,
        m2 * contra + x2 * pressure,
        enthalpy * contra,
    )
    waves = [speed * one for one in state]
    plus = [a + b for a, b in zip(fluxes, waves)]
    minus = [a - b for a, b in zip(fluxes, waves)]
    return plus, minus, metric


def RCP(x):
    return pl.reciprocal(x, approx=True)


def add(a, b):
    if a is None or b is None:
        return b if a is None else a
    return a + b


def subtract(a, b):
    if b is None:
        return a
    return -b if a is None else a - b


def multiply(a, b):
    return None if a is None or b is None else a * b


class Split:
    def __init__(self, load, kind, flat=None):
        self.load, self.memo, self.kind, self.flat = load, {}, kind, flat

    def get(self, name, n):
        if (name, n) not in self.memo:
            self.memo[name, n] = getattr(self, "make_" + name)(n)
        return self.memo[name, n]

    def cast(self, value):
        return None if value is None else value.astype(self.kind)

    def make_v(self, n):
        return self.load(n)

    def make_d(self, n):
        if self.flat is not None and n >= self.flat:
            return None
        return self.get("v", n + 1) - self.get("v", n)

    def make_e(self, n):
        return subtract(self.get("d", n), self.get("d", n - 1))

    def make_t(self, n):
        return subtract(self.get("e", n + 1), self.get("e", n))

    def make_near(self, n):
        return self.cast(self.get("t", n))

    def make_near2(self, n):
        return add(self.get("near", n), self.get("near", n))

    def make_low(self, n):
        return self.cast(self.get("d", n))

    def make_smooth(self, n):
        high, low = self.get("low", n), self.get("low", n - 1)
        bend = self.cast(self.get("e", n))
        least = self.kind(16.0 * epsilon / 3.0)
        if bend is None:
            return (jnp.full(self.get("v", self.flat).shape, least, self.kind),) * 3
        twice = bend + bend
        a, b = multiply(high, twice), multiply(low, twice)
        centre = subtract(a, b) * self.kind(2.0 / 3.0) + add(multiply(high, low), least)
        return add(a, centre), centre, subtract(centre, b)

    def correction(self, outer, middle, inner, near, far):
        left = middle * RCP(outer)
        right = middle * RCP(inner)
        weight_left = left * left * self.kind(1.0 / 3.0)
        weight_right = right * right
        total = (weight_left + weight_right) + self.kind(2.0)
        return add(multiply(weight_left, near), multiply(weight_right, far)) * RCP(total)


def sweep(kind, load_plus, load_minus, load_diffused, load_metric, store, first, last, open_low=False, open_high=False,
          flat=None):
    plus, minus = Split(load_plus, kind, flat), Split(load_minus, kind, flat)
    central, diffused, metric = {}, {}, {}

    def tripled(n):
        n = n if flat is None else min(n, flat)
        if n not in central:
            central[n] = 3.0 * (plus.get("v", n) + minus.get("v", n))
        return central[n]

    def cached(table, load, n):
        if n not in table:
            table[n] = load(n)
        return table[n]

    before = None
    for n in range(first, last + 1):
        up = plus.correction(
            plus.get("smooth", n - 1)[0],
            plus.get("smooth", n)[1],
            plus.get("smooth", n + 1)[2],
            plus.get("near2", n - 1),
            plus.get("near", n),
        )
        down = minus.correction(
            minus.get("smooth", n + 2)[2],
            minus.get("smooth", n + 1)[1],
            minus.get("smooth", n)[0],
            minus.get("near2", n + 1),
            minus.get("near", n),
        )
        flux = (tripled(n) + tripled(n + 1)) - add(plus.get("e", n), minus.get("e", n + 1)) + (down - up).astype(F32)
        if flat is not None and n >= flat:
            net = -flux
        else:
            face_metric = cached(metric, load_metric, n) + cached(metric, load_metric, n + 1)
            jump = cached(diffused, load_diffused, n + 1) - cached(diffused, load_diffused, n)
            net = face_metric * jump - flux
        if before is not None:
            store(n, net - before)
        elif open_low:
            store(n, net)
        before = net
    if open_high:
        store(last + 1, -before)


def put(refs, rows, plus, minus, metric=None):
    plus_ref, minus_ref, metric_ref = refs
    for f in range(5):
        plus_ref[f, rows, :] = plus[f]
        minus_ref[f, rows, :] = minus[f]
    if metric is not None:
        metric_ref[rows, :] = metric


def put_diffused(ref, rows, prims):
    for m in range(3):
        ref[1 + m, rows, :] = prims[0][m]
    ref[4, rows, :] = prims[4]


def aligned(start, count):
    return pl.ds(pl.multiple_of(start, 8), count)


def unit(which, m, value):
    return value + 1.0 if which == m else value


def to_span(value, store, height):
    for half in range(2):
        turned = value[half * 128 : (half + 1) * 128].T
        for q in range(4):
            store(q * 2 + half, turned[q * height : (q + 1) * height])


def send_parts(state_ref, span_ref, fields, outs, dims):
    rows_i, height = dims
    total = rows_i * rows_i
    core_ref, chip_ref, wake_ref, span_near_ref, span_far_ref = outs
    even = lax.rem(lax.axis_index("wrap"), 2) == 0
    edge = H * rows_i
    to_core, to_chip = jnp.where(even, total - edge, 0), jnp.where(even, 0, total - edge)
    for f in range(5):
        core_ref[f] = state_ref[f, aligned(to_core, edge), :]
        chip_ref[f] = state_ref[f, aligned(to_chip, edge), :]
        for r in range(H):
            wake_ref[pl.ds(f * H + r, rows_i, stride=16), :] = state_ref[f, pl.ds(r + 1, rows_i, stride=rows_i), :]
    even = lax.rem(lax.axis_index("span"), 2) == 0
    for f in range(fields):
        for r in range(H):
            top = (height - H + r) * 8
            low, high = span_ref[f, r * 8 : r * 8 + 2, :], span_ref[f, top + 6 : top + 8, :]
            span_near_ref[f, 2 * r : 2 * r + 2, :] = jnp.where(even, high, low)
            span_far_ref[f, 2 * r : 2 * r + 2, :] = jnp.where(even, low, high)


def prepare_kernel(dims, rho_hbm, vel_hbm, pre_hbm, met_hbm, state_ref, span_ref, met_ref, *refs):
    outs, (rho_ref, vel_ref, pre_ref, sems) = refs[:5], refs[5:]
    rows_i, height = dims
    total = rows_i * rows_i
    pairs = [(rho_hbm, rho_ref), (vel_hbm, vel_ref), (pre_hbm, pre_ref)]
    pairs += [(met_hbm.at[pl.ds(3 * d, 3)], met_ref.at[pl.ds(3 * d, 3)]) for d in (2, 0, 1)]
    copies = [pltpu.make_async_copy(a, b, sems.at[n]) for n, (a, b) in enumerate(pairs)]
    for copy in copies:
        copy.start()
    for copy in copies[:3]:
        copy.wait()
    rho, pressure = rho_ref[...], pre_ref[...]
    u = [vel_ref[m] for m in range(3)]
    speed_sq = u[0] * u[0] + u[1] * u[1] + u[2] * u[2]
    state_ref[0] = rho
    for m in range(3):
        state_ref[1 + m] = rho * u[m]
    state_ref[4] = pressure * (1.0 / 0.4) + 0.5 * rho * speed_sq
    core_ref, chip_ref = outs[:2]
    for f in range(8):
        if f == 5:
            copies[3].wait()
        value = state_ref[f] if f < 5 else met_ref[6 + f - 5]

        def store(start, block, f=f):
            span_ref[f, pl.ds(start, height, stride=8), :] = block

        to_span(value, store, height)
    send_parts(state_ref, span_ref, 8, outs, dims)
    copies[4].wait()
    even = lax.rem(lax.axis_index("wrap"), 2) == 0
    edge = H * rows_i
    to_core, to_chip = jnp.where(even, total - edge, 0), jnp.where(even, 0, total - edge)
    for m in range(3):
        core_ref[5 + m] = met_ref[m, aligned(to_core, edge), :]
        chip_ref[5 + m] = met_ref[m, aligned(to_chip, edge), :]
    copies[5].wait()


def early_kernel(dims, kind, kept, state_ref, span_ref, span_met_ref, met_ref, *refs):
    rows_i, height = dims
    if kept:
        metric_i, metric_j, metric_k = refs[:3]
        refs = refs[3:]
    acc_ref, plus_i, minus_i, plus_j, minus_j, diffused_ref, plus_k, minus_k, diffused_k = refs[:9]
    if not kept:
        metric_i, metric_j, metric_k = refs[9:]
    diffused_ref[0] = jnp.zeros(diffused_ref.shape[1:], F32)
    diffused_k[0] = jnp.zeros(diffused_k.shape[1:], F32)

    def place(refs, metric_ref, rows, state, prims, row):
        plus, minus, metric = point_fluxes(state, prims, row, metric_ref[rows, :] if kept else None)
        put((*refs, metric_ref), rows, plus, minus, None if kept else metric)

    def planes(n, carry):
        rows = aligned(n * rows_i, rows_i)
        state = [state_ref[f, rows, :] for f in range(5)]
        prims = primitives(state)
        put_diffused(diffused_ref, rows, prims)
        place((plus_i, minus_i), metric_i, rows, state, prims, [unit(0, m, met_ref[m, rows, :]) for m in range(3)])
        place((plus_j, minus_j), metric_j, rows, state, prims, [unit(1, m, met_ref[3 + m, rows, :]) for m in range(3)])
        return carry

    lax.fori_loop(0, rows_i, planes, 0, unroll=4)

    def spans(n, carry):
        rows = aligned(n * 16, 16)
        state = [span_ref[f, rows, :] for f in range(5)]
        prims = primitives(state)
        put_diffused(diffused_k, rows, prims)
        place((plus_k, minus_k), metric_k, rows, state, prims, [unit(2, m, span_met_ref[5 + m, rows, :]) for m in range(3)])
        return carry

    lax.fori_loop(0, height // 2, spans, 0, unroll=4)

    def normal(f, carry):
        def rows(n):
            return pl.ds(min(n, rows_i - 1), rows_i, stride=rows_i)

        def store(n, value):
            acc_ref[f, rows(n), :] = value

        for n in range(2):
            store(n, jnp.zeros((rows_i, 128), F32))
        sweep(kind, lambda n: plus_j[f, rows(n), :], lambda n: minus_j[f, rows(n), :], lambda n: diffused_ref[f, rows(n), :],
              lambda n: metric_j[rows(n), :], store, 2, rows_i - 1, open_low=True,
              flat=rows_i - 1)
        return carry

    lax.fori_loop(0, 5, normal, 0)


def chord_kernel(dims, kind, state_ref, met_ref, core_ref, chip_ref, met_core_ref, met_chip_ref, normal_ref,
                 plus_i, minus_i, metric_i, diffused_ref, acc_ref, halo_plus, halo_minus, halo_metric, halo_diffused):
    rows_i, height = dims
    total = rows_i * rows_i
    position, count = lax.axis_index("wrap"), lax.axis_size("wrap")
    even = lax.rem(position, 2) == 0
    at_end = (position == 0) | (position == count - 1)
    halo_diffused[0] = jnp.zeros(halo_diffused.shape[1:], F32)

    core_rows, chip_rows = jnp.where(even, H, 0), jnp.where(even, 0, H)
    own = jnp.where(even, 0, total - rows_i)
    for r in range(H):
        rows = slice(r * rows_i, (r + 1) * rows_i)
        state = [core_ref[f, rows, :] for f in range(5)]
        prims = primitives(state)
        to = aligned((core_rows + r) * rows_i, rows_i)
        put_diffused(halo_diffused, to, prims)
        put((halo_plus, halo_minus, halo_metric), to,
            *point_fluxes(state, prims, [unit(0, m, met_core_ref[5 + m, rows, :]) for m in range(3)]))
        edge = aligned(own, rows_i)
        state = [jnp.where(at_end, state_ref[f, edge, :], chip_ref[f, rows, :]) for f in range(5)]
        row = [jnp.where(at_end, met_ref[m, edge, :], met_chip_ref[5 + m, rows, :]) for m in range(3)]
        prims = primitives(state)
        to = aligned((chip_rows + r) * rows_i, rows_i)
        put_diffused(halo_diffused, to, prims)
        put((halo_plus, halo_minus, halo_metric), to,
            *point_fluxes(state, prims, [unit(0, m, row[m]) for m in range(3)]))

    def chord(f, carry):
        def loader(ref, halo, lead):
            def load(n):
                if 0 <= n < rows_i:
                    return ref[lead + (aligned(n * rows_i, rows_i),)]
                r = n + H if n < 0 else n - rows_i + H
                return halo[lead + (aligned(r * rows_i, rows_i),)]

            return load

        def store(n, value):
            rows = aligned(n * rows_i, rows_i)
            acc_ref[f, rows, :] = value + normal_ref[f, rows, :]

        sweep(kind, loader(plus_i, halo_plus, (f,)), loader(minus_i, halo_minus, (f,)), loader(diffused_ref, halo_diffused, (f,)),
              loader(metric_i, halo_metric, ()), store, -1, rows_i - 1)
        return carry

    lax.fori_loop(0, 5, chord, 0)


def span_kernel(dims, kind, final, *refs):
    rows_i, height = dims
    (span_ref, span_met_ref, span_near_ref, span_far_ref, met_near_ref, met_far_ref, plus_k, minus_k, metric_k, diffused_k,
     partner_hbm, state_ref, met_ref, vol_ref, blank_ref, wake_ref, plane_ref, plus_j, minus_j, metric_j,
     diffused_ref) = refs[:21]
    refs = refs[21:]
    if final:
        start_ref, out_ref = refs[:2]
        refs = refs[2:]
    else:
        out_ref, out_span_ref = refs[:2]
        outs, refs = refs[2:7], refs[7:]
    (acc_ref, halo_plus, halo_minus, halo_metric, halo_diffused, pad_ref, wall_ref, sum_ref,
     ghost_plus, ghost_minus, ghost_metric, ghost_diffused, ghost_ref, partner_ref, sem) = refs[:15]
    if final:
        staged_ref, out_sems = refs[15:]
    fetch = pltpu.make_async_copy(partner_hbm, partner_ref, sem)
    fetch.start()
    position, count = lax.axis_index("wrap"), lax.axis_size("wrap")
    ghost_diffused[0] = jnp.zeros(ghost_diffused.shape[1:], F32)
    even = lax.rem(lax.axis_index("span"), 2) == 0
    sublane = lax.broadcasted_iota(jnp.int32, (8, 128), 0)
    halo_diffused[0] = jnp.zeros(halo_diffused.shape[1:], F32)
    for r in range(H):
        for f in range(8):
            near_ref, far_ref = (span_near_ref, span_far_ref) if f < 5 else (met_near_ref, met_far_ref)
            near, far = near_ref[f, 2 * r : 2 * r + 2, :], far_ref[f, 2 * r : 2 * r + 2, :]
            pad_ref[f, r * 8 : r * 8 + 2, :] = jnp.where(even, far, near)
            pad_ref[f, (H + r) * 8 + 6 : (H + r) * 8 + 8, :] = jnp.where(even, near, far)
    for r in range(2 * H):
        rows = slice(r * 8, r * 8 + 8)
        values = []
        for f in range(8):
            ref = span_ref if f < 5 else span_met_ref
            if r < H:
                own = pltpu.roll(ref[f, (height - H + r) * 8 : (height - H + r) * 8 + 8, :], 2, 0)
                values.append(jnp.where(sublane < 2, pad_ref[f, rows, :], own))
            else:
                own = pltpu.roll(ref[f, (r - H) * 8 : (r - H) * 8 + 8, :], 6, 0)
                values.append(jnp.where(sublane >= 6, pad_ref[f, rows, :], own))
        prims = primitives(values[:5])
        put_diffused(halo_diffused, rows, prims)
        put((halo_plus, halo_minus, halo_metric), rows,
            *point_fluxes(values[:5], prims, [unit(2, m, values[5 + m]) for m in range(3)]))

    def sweep_span(f, carry):
        def loader(ref, halo, lead):
            def one(n):
                if 0 <= n < height:
                    return ref[lead + (slice(n * 8, n * 8 + 8),)]
                r = n + H if n < 0 else n - height + H
                return halo[lead + (slice(r * 8, r * 8 + 8),)]

            return lambda n: jnp.concatenate([one(n), one(n + height // 2)], axis=0)

        def store(n, value):
            acc_ref[f, n * 8 : n * 8 + 8, :] = value[:8]
            m = n + height // 2
            acc_ref[f, m * 8 : m * 8 + 8, :] = value[8:]

        sweep(kind, loader(plus_k, halo_plus, (f,)), loader(minus_k, halo_minus, (f,)), loader(diffused_k, halo_diffused, (f,)),
              loader(metric_k, halo_metric, ()), store, -1, height // 2 - 1)
        return carry

    lax.fori_loop(0, 5, sweep_span, 0)

    fetch.wait()
    base = (count - 1 - position) * rows_i
    for i in range(rows_i):
        ghost_ref[i * 16 : i * 16 + 16, :] = wake_ref[aligned((partner_ref[i] - base) * 16, 16), :]
    wall = pl.ds(0, rows_i, stride=rows_i)
    for r in range(H):
        state = [ghost_ref[pl.ds(f * H + r, rows_i, stride=16), :] for f in range(5)]
        prims = primitives(state)
        to = slice(r * rows_i, (r + 1) * rows_i)
        put_diffused(ghost_diffused, to, prims)
        put((ghost_plus, ghost_minus, ghost_metric), to,
            *point_fluxes(state, prims, [unit(1, m, met_ref[3 + m, wall, :]) for m in range(3)]))

    def normal(f):
        def rows(n):
            return pl.ds(n, rows_i, stride=rows_i)

        def loader(ref, halo, lead):
            def load(n):
                if n >= 0:
                    return ref[lead + (rows(n),)]
                return halo[lead + (aligned((-1 - n) * rows_i, rows_i),)]

            return load

        def store(n, value):
            wall_ref[f, n * rows_i : (n + 1) * rows_i, :] = value

        sweep(kind, loader(plus_j, ghost_plus, (f,)), loader(minus_j, ghost_minus, (f,)), loader(diffused_ref, ghost_diffused, (f,)),
              lambda n: metric_j[rows(max(n, 0)), :], store, -1, 1, open_high=True)


    scale = (time_step / 12.0) * blank_ref[...].astype(F32) / vol_ref[...]
    for f in range(5):
        normal(f)
        for half in range(2):
            parts = [acc_ref[f, pl.ds(q * 2 + half, height, stride=8), :] for q in range(4)]
            rows = slice(half * 128, (half + 1) * 128)
            sum_ref[f, rows, :] = plane_ref[f, rows, :] + jnp.concatenate(parts, axis=0).T
        for n in range(H):
            rows = pl.ds(n, rows_i, stride=rows_i)
            sum_ref[f, rows, :] = sum_ref[f, rows, :] + wall_ref[f, n * rows_i : (n + 1) * rows_i, :]
        moved = state_ref[f] + scale * sum_ref[f]
        if final:
            staged_ref[f] = 0.5 * start_ref[f] + 0.5 * moved
            pltpu.make_async_copy(staged_ref.at[f], out_ref.at[f], out_sems.at[f]).start()
        else:
            out_ref[f] = moved
    if final:
        for f in range(5):
            pltpu.make_async_copy(staged_ref.at[f], out_ref.at[f], out_sems.at[f]).wait()
    if not final:
        for f in range(5):
            def store(start, block, f=f):
                out_span_ref[f, pl.ds(start, height, stride=8), :] = block

            to_span(out_ref[f], store, height)
        send_parts(out_ref, out_span_ref, 5, outs, dims)


def shape(*sizes):
    return jax.ShapeDtypeStruct(sizes, F32)


def exchange(sent):
    core, chip, wake, span_near, span_far = sent
    n, s = lax.axis_size("wrap"), lax.axis_size("span")
    cores = [(i, i ^ 1) for i in range(n)]
    chips = [pair for i in range(1, n, 2) for pair in ((i, (i + 1) % n), ((i + 1) % n, i))]
    mirror = [(i, n - 1 - i) for i in range(n)]
    near = [(i, i ^ 1) for i in range(s)]
    far = [pair for i in range(1, s, 2) for pair in ((i, (i + 1) % s), ((i + 1) % s, i))]
    return (lax.ppermute(core, "wrap", cores), lax.ppermute(chip, "wrap", chips), lax.ppermute(wake, "wrap", mirror),
            lax.ppermute(span_near, "span", near), lax.ppermute(span_far, "span", far))


def body(density, velocity, pressure, metrics, volume, wake_partner, iblank):
    rows_i, rows_j, lanes = density.shape
    total, height = rows_i * rows_j, lanes // 4
    dims = (rows_i, height)
    volume, blank = volume.reshape(total, lanes), iblank.reshape(total, lanes)
    whole = pl.BlockSpec(memory_space=pltpu.VMEM)
    far = pl.BlockSpec(memory_space=pltpu.HBM)
    wake_partner = pltpu.with_memory_space_constraint(wake_partner, pltpu.HBM)
    params = pltpu.CompilerParams(vmem_limit_bytes=16 * 2**20)

    def call(kernel, name, ins, outs, scratch, specs=None, cost=0, out_specs=None):
        return pl.pallas_call(
            kernel,
            out_shape=outs,
            in_specs=specs or [whole] * len(ins),
            out_specs=out_specs or [whole] * len(outs),
            scratch_shapes=scratch,
            compiler_params=params,
            cost_estimate=pl.CostEstimate(flops=cost, bytes_accessed=cost // 4, transcendentals=0),
            name=name,
        )(*ins)

    def parts(fields):
        edge = H * rows_j
        return [shape(fields, edge, lanes), shape(fields, edge, lanes), shape(rows_i * 16, lanes),
                shape(fields, 8, lanes), shape(fields, 8, lanes)]

    field, span_rows, halo = shape(5, total, lanes), height * 8, 2 * H * rows_i
    state, span, met, *sent = call(
        functools.partial(prepare_kernel, dims), "prepare",
        [pltpu.with_memory_space_constraint(one, pltpu.HBM) for one in (
            density.reshape(total, lanes), velocity.reshape(3, total, lanes), pressure.reshape(total, lanes),
            metrics.reshape(9, total, lanes))],
        [field, shape(8, total, lanes), shape(9, total, lanes)] + parts(8),
        [pltpu.VMEM((total, lanes), F32), pltpu.VMEM((3, total, lanes), F32), pltpu.VMEM((total, lanes), F32),
         pltpu.SemaphoreType.DMA((6,))],
        [far] * 4,
    )
    span_met = span

    def halo_scratch(rows):
        return [pltpu.VMEM((5, rows, lanes), F32), pltpu.VMEM((5, rows, lanes), F32), pltpu.VMEM((rows, lanes), F32),
                pltpu.VMEM((5, rows, lanes), F32)]

    metric_halo, kept = None, ()
    start = state
    for final in (False, True):
        kind = jnp.bfloat16 if final else F32
        core, chip, wake, span_near, span_far = exchange(sent)
        if metric_halo is None:
            metric_halo = core, chip, span_near, span_far
        line, span_line = shape(5, total, lanes), shape(5, span_rows, lanes)
        normal, plus_i, minus_i, plus_j, minus_j, diffused, plus_k, minus_k, diffused_k, *squares = call(
            functools.partial(early_kernel, dims, kind, bool(kept)), "early", (state, span, span_met, met, *kept),
            [field, line, line, line, line, line, span_line, span_line, span_line]
            + ([] if kept else [shape(total, lanes), shape(total, lanes), shape(span_rows, lanes)]),
            [], cost=10**8,
        )
        kept = kept or tuple(squares)
        metric_i, metric_j, metric_k = kept
        (plane,) = call(
            functools.partial(chord_kernel, dims, kind), "chord",
            (state, met, core, chip, metric_halo[0], metric_halo[1], normal, plus_i, minus_i, metric_i, diffused),
            [field], halo_scratch(halo), cost=10**8,
        )
        ins = (span, span_met, span_near, span_far, metric_halo[2], metric_halo[3], plus_k, minus_k, metric_k, diffused_k, wake_partner, state, met,
               volume, blank, wake, plane, plus_j, minus_j, metric_j, diffused)
        ins += (start,) if final else ()
        state, *rest = call(
            functools.partial(span_kernel, dims, kind, final), "span", ins,
            [field] if final else [field, field] + parts(5),
            [pltpu.VMEM((5, span_rows, lanes), F32)] + halo_scratch(2 * H * 8) + [pltpu.VMEM((8, 2 * H * 8, lanes), F32)]
            + [pltpu.VMEM((5, H * rows_i, lanes), F32), pltpu.VMEM((5, total, lanes), F32)] + halo_scratch(H * rows_i)
            + [pltpu.VMEM((rows_i * 16, lanes), F32), pltpu.SMEM((rows_i,), jnp.int32), pltpu.SemaphoreType.DMA]
            + ([pltpu.VMEM((5, total, lanes), F32), pltpu.SemaphoreType.DMA((5,))] if final else []),
            [whole] * 10 + [far] + [whole] * (len(ins) - 11),
            cost=10**8, out_specs=[far] if final else None,
        )
        if not final:
            span, *sent = rest
    return state.reshape(5, rows_i, rows_j, lanes)


def solution(mesh):
    placed = (
        P("wrap", None, "span"),
        P(None, "wrap", None, "span"),
        P("wrap", None, "span"),
        P(None, "wrap", None, "span"),
        P("wrap", None, "span"),
        P("wrap"),
        P("wrap", None, "span"),
    )
    return jax.shard_map(
        body, mesh=mesh, in_specs=placed, out_specs=P(None, "wrap", None, "span"), check_vma=False
    )
```

```python
import functools

import jax
import jax.numpy as jnp
from jax import lax
from jax.experimental import pallas as pl
from jax.experimental.pallas import tpu as pltpu
from jax.sharding import PartitionSpec as P

epsilon = 1e-06
viscosity = 0.8
conduction = 1.0
time_step = 0.05
metric_scale = 12.0 * viscosity * 0.5
H = 3
F32 = jnp.float32


def primitives(state):
    rho, m0, m1, m2, energy = state
    inverse = 1.0 / rho
    velocity = (m0 * inverse, m1 * inverse, m2 * inverse)
    speed_sq = velocity[0] * velocity[0] + velocity[1] * velocity[1] + velocity[2] * velocity[2]
    pressure = 0.4 * (energy - 0.5 * rho * speed_sq)
    ratio = pressure * inverse
    heat = 0.5 * speed_sq + conduction * ratio
    return velocity, pressure, energy + pressure, (1.4 / metric_scale) * ratio, heat


def point_fluxes(state, prims, row, metric=None):
    rho, m0, m1, m2, _ = state
    (u0, u1, u2), pressure, enthalpy, sound_sq, _ = prims
    x0, x1, x2 = row
    contra = x0 * u0 + x1 * u1 + x2 * u2
    if metric is None:
        metric = (x0 * x0 + x1 * x1 + x2 * x2) * metric_scale
    square = sound_sq * metric
    speed = jnp.abs(contra) + square * lax.rsqrt(jnp.maximum(square, 1e-30))
    fluxes = (
        rho * contra,
        m0 * contra + x0 * pressure,
        m1 * contra + x1 * pressure,
        m2 * contra + x2 * pressure,
        enthalpy * contra,
    )
    waves = [speed * one for one in state]
    plus = [a + b for a, b in zip(fluxes, waves)]
    minus = [a - b for a, b in zip(fluxes, waves)]
    return plus, minus, [6.0 * one for one in fluxes], metric


def RCP(x):
    return pl.reciprocal(x, approx=True)


def add(a, b):
    if a is None or b is None:
        return b if a is None else a
    return a + b


def subtract(a, b):
    if b is None:
        return a
    return -b if a is None else a - b


def multiply(a, b):
    return None if a is None or b is None else a * b


class Split:
    def __init__(self, load, kind, flat=None):
        self.load, self.memo, self.kind, self.flat = load, {}, kind, flat

    def get(self, name, n):
        if (name, n) not in self.memo:
            self.memo[name, n] = getattr(self, "make_" + name)(n)
        return self.memo[name, n]

    def cast(self, value):
        return None if value is None else value.astype(self.kind)

    def make_v(self, n):
        return self.load(n)

    def make_d(self, n):
        if self.flat is not None and n >= self.flat:
            return None
        return self.get("v", n + 1) - self.get("v", n)

    def make_e(self, n):
        return subtract(self.get("d", n), self.get("d", n - 1))

    def make_t(self, n):
        return subtract(self.get("e", n + 1), self.get("e", n))

    def make_near(self, n):
        return self.cast(self.get("t", n))

    def make_near2(self, n):
        return add(self.get("near", n), self.get("near", n))

    def make_low(self, n):
        return self.cast(self.get("d", n))

    def make_smooth(self, n):
        high, low = self.get("low", n), self.get("low", n - 1)
        bend = self.cast(self.get("e", n))
        least = self.kind(16.0 * epsilon / 3.0)
        if bend is None:
            return (jnp.full(self.get("v", self.flat).shape, least, self.kind),) * 3
        twice = bend + bend
        a, b = multiply(high, twice), multiply(low, twice)
        centre = subtract(a, b) * self.kind(2.0 / 3.0) + add(multiply(high, low), least)
        return add(a, centre), centre, subtract(centre, b)

    def correction(self, outer, middle, inner, near, far):
        left = middle * RCP(outer)
        right = middle * RCP(inner)
        weight_left = left * left * self.kind(1.0 / 3.0)
        weight_right = right * right
        total = (weight_left + weight_right) + self.kind(2.0)
        return add(multiply(weight_left, near), multiply(weight_right, far)) * RCP(total)


def sweep(kind, load_plus, load_minus, load_centre, load_diffused, load_face, store, first, last, open_low=False, open_high=False,
          flat=None):
    plus, minus = Split(load_plus, kind, flat), Split(load_minus, kind, flat)
    central, diffused = {}, {}

    def cached(table, load, n):
        if n not in table:
            table[n] = load(n)
        return table[n]

    before = None
    for n in range(first, last + 1):
        up = plus.correction(
            plus.get("smooth", n - 1)[0],
            plus.get("smooth", n)[1],
            plus.get("smooth", n + 1)[2],
            plus.get("near2", n - 1),
            plus.get("near", n),
        )
        down = minus.correction(
            minus.get("smooth", n + 2)[2],
            minus.get("smooth", n + 1)[1],
            minus.get("smooth", n)[0],
            minus.get("near2", n + 1),
            minus.get("near", n),
        )
        centres = [cached(central, load_centre, m if flat is None else min(m, flat)) for m in (n, n + 1)]
        flux = (centres[0] + centres[1]) - add(plus.get("e", n), minus.get("e", n + 1)) + (down - up).astype(F32)
        if flat is not None and n >= flat:
            net = -flux
        else:
            jump = cached(diffused, load_diffused, n + 1) - cached(diffused, load_diffused, n)
            net = load_face(n) * jump - flux
        if before is not None:
            store(n, net - before)
        elif open_low:
            store(n, net)
        before = net
    if open_high:
        store(last + 1, -before)


def put(refs, rows, plus, minus, centre, metric=None):
    plus_ref, minus_ref, centre_ref, metric_ref = refs
    for f in range(5):
        plus_ref[f, rows, :] = plus[f]
        minus_ref[f, rows, :] = minus[f]
        centre_ref[f, rows, :] = centre[f]
    if metric is not None:
        metric_ref[rows, :] = metric


def put_diffused(ref, rows, prims):
    for m in range(3):
        ref[1 + m, rows, :] = prims[0][m]
    ref[4, rows, :] = prims[4]


def aligned(start, count):
    return pl.ds(pl.multiple_of(start, 8), count)


def unit(which, m, value):
    return value + 1.0 if which == m else value


def to_span(value, store, height):
    for half in range(2):
        turned = value[half * 128 : (half + 1) * 128].T
        for q in range(4):
            store(q * 2 + half, turned[q * height : (q + 1) * height])


def send_parts(state_ref, span_ref, fields, outs, dims):
    rows_i, height = dims
    total = rows_i * rows_i
    core_ref, chip_ref, wake_ref, span_near_ref, span_far_ref = outs
    even = lax.rem(lax.axis_index("wrap"), 2) == 0
    edge = H * rows_i
    to_core, to_chip = jnp.where(even, total - edge, 0), jnp.where(even, 0, total - edge)
    for f in range(5):
        core_ref[f] = state_ref[f, aligned(to_core, edge), :]
        chip_ref[f] = state_ref[f, aligned(to_chip, edge), :]
        for r in range(H):
            wake_ref[pl.ds(f * H + r, rows_i, stride=16), :] = state_ref[f, pl.ds(r + 1, rows_i, stride=rows_i), :]
    even = lax.rem(lax.axis_index("span"), 2) == 0
    for f in range(fields):
        for r in range(H):
            top = (height - H + r) * 8
            low, high = span_ref[f, r * 8 : r * 8 + 2, :], span_ref[f, top + 6 : top + 8, :]
            span_near_ref[f, 2 * r : 2 * r + 2, :] = jnp.where(even, high, low)
            span_far_ref[f, 2 * r : 2 * r + 2, :] = jnp.where(even, low, high)


def prepare_kernel(dims, rho_hbm, vel_hbm, pre_hbm, met_hbm, state_ref, span_ref, met_ref, *refs):
    outs, (rho_ref, vel_ref, pre_ref, sems) = refs[:5], refs[5:]
    rows_i, height = dims
    total = rows_i * rows_i
    pairs = [(rho_hbm, rho_ref), (vel_hbm, vel_ref), (pre_hbm, pre_ref)]
    pairs += [(met_hbm.at[pl.ds(3 * d, 3)], met_ref.at[pl.ds(3 * d, 3)]) for d in (2, 0, 1)]
    copies = [pltpu.make_async_copy(a, b, sems.at[n]) for n, (a, b) in enumerate(pairs)]
    for copy in copies:
        copy.start()
    for copy in copies[:3]:
        copy.wait()
    rho, pressure = rho_ref[...], pre_ref[...]
    u = [vel_ref[m] for m in range(3)]
    speed_sq = u[0] * u[0] + u[1] * u[1] + u[2] * u[2]
    state_ref[0] = rho
    for m in range(3):
        state_ref[1 + m] = rho * u[m]
    state_ref[4] = pressure * (1.0 / 0.4) + 0.5 * rho * speed_sq
    core_ref, chip_ref = outs[:2]
    for f in range(8):
        if f == 5:
            copies[3].wait()
        value = state_ref[f] if f < 5 else met_ref[6 + f - 5]

        def store(start, block, f=f):
            span_ref[f, pl.ds(start, height, stride=8), :] = block

        to_span(value, store, height)
    send_parts(state_ref, span_ref, 8, outs, dims)
    copies[4].wait()
    even = lax.rem(lax.axis_index("wrap"), 2) == 0
    edge = H * rows_i
    to_core, to_chip = jnp.where(even, total - edge, 0), jnp.where(even, 0, total - edge)
    for m in range(3):
        core_ref[5 + m] = met_ref[m, aligned(to_core, edge), :]
        chip_ref[5 + m] = met_ref[m, aligned(to_chip, edge), :]
    copies[5].wait()


def early_kernel(dims, kind, kept, state_ref, span_ref, span_met_ref, met_ref, *refs):
    rows_i, height = dims
    if kept:
        metric_i, metric_j, metric_k = refs[:3]
        refs = refs[3:]
    acc_ref, plus_i, minus_i, centre_i, plus_j, minus_j, centre_j, diffused_ref, plus_k, minus_k, centre_k, diffused_k = refs[:12]
    if not kept:
        metric_i, metric_j, metric_k = refs[12:15]
    face_ref = refs[-1]
    diffused_ref[0] = jnp.zeros(diffused_ref.shape[1:], F32)
    diffused_k[0] = jnp.zeros(diffused_k.shape[1:], F32)

    def place(refs, metric_ref, rows, state, prims, row):
        *fluxes, metric = point_fluxes(state, prims, row, metric_ref[rows, :] if kept else None)
        put((*refs, metric_ref), rows, *fluxes, None if kept else metric)

    def planes(n, carry):
        rows = aligned(n * rows_i, rows_i)
        state = [state_ref[f, rows, :] for f in range(5)]
        prims = primitives(state)
        put_diffused(diffused_ref, rows, prims)
        place((plus_i, minus_i, centre_i), metric_i, rows, state, prims, [unit(0, m, met_ref[m, rows, :]) for m in range(3)])
        place((plus_j, minus_j, centre_j), metric_j, rows, state, prims, [unit(1, m, met_ref[3 + m, rows, :]) for m in range(3)])
        return carry

    lax.fori_loop(0, rows_i, planes, 0, unroll=4)

    def spans(n, carry):
        rows = aligned(n * 16, 16)
        state = [span_ref[f, rows, :] for f in range(5)]
        prims = primitives(state)
        put_diffused(diffused_k, rows, prims)
        place((plus_k, minus_k, centre_k), metric_k, rows, state, prims, [unit(2, m, span_met_ref[5 + m, rows, :]) for m in range(3)])
        return carry

    lax.fori_loop(0, height // 2, spans, 0, unroll=4)

    for n in range(2, rows_i - 1):
        low, high = (metric_j[pl.ds(m, rows_i, stride=rows_i), :] for m in (n, n + 1))
        face_ref[n * rows_i : (n + 1) * rows_i, :] = low + high

    def normal(f, carry):
        def rows(n):
            return pl.ds(min(n, rows_i - 1), rows_i, stride=rows_i)

        def store(n, value):
            acc_ref[f, rows(n), :] = value

        for n in range(2):
            store(n, jnp.zeros((rows_i, 128), F32))
        sweep(kind, lambda n: plus_j[f, rows(n), :], lambda n: minus_j[f, rows(n), :], lambda n: centre_j[f, rows(n), :],
              lambda n: diffused_ref[f, rows(n), :], lambda n: face_ref[n * rows_i : (n + 1) * rows_i, :],
              store, 2, rows_i - 1, open_low=True,
              flat=rows_i - 1)
        return carry

    lax.fori_loop(0, 5, normal, 0)


def chord_kernel(dims, kind, state_ref, met_ref, core_ref, chip_ref, met_core_ref, met_chip_ref, normal_ref,
                 plus_i, minus_i, centre_i, metric_i, diffused_ref, acc_ref,
                 halo_plus, halo_minus, halo_centre, halo_metric, halo_diffused, face_ref):
    rows_i, height = dims
    total = rows_i * rows_i
    position, count = lax.axis_index("wrap"), lax.axis_size("wrap")
    even = lax.rem(position, 2) == 0
    at_end = (position == 0) | (position == count - 1)
    halo_diffused[0] = jnp.zeros(halo_diffused.shape[1:], F32)

    core_rows, chip_rows = jnp.where(even, H, 0), jnp.where(even, 0, H)
    own = jnp.where(even, 0, total - rows_i)
    for r in range(H):
        rows = slice(r * rows_i, (r + 1) * rows_i)
        state = [core_ref[f, rows, :] for f in range(5)]
        prims = primitives(state)
        to = aligned((core_rows + r) * rows_i, rows_i)
        put_diffused(halo_diffused, to, prims)
        put((halo_plus, halo_minus, halo_centre, halo_metric), to,
            *point_fluxes(state, prims, [unit(0, m, met_core_ref[5 + m, rows, :]) for m in range(3)]))
        edge = aligned(own, rows_i)
        state = [jnp.where(at_end, state_ref[f, edge, :], chip_ref[f, rows, :]) for f in range(5)]
        row = [jnp.where(at_end, met_ref[m, edge, :], met_chip_ref[5 + m, rows, :]) for m in range(3)]
        prims = primitives(state)
        to = aligned((chip_rows + r) * rows_i, rows_i)
        put_diffused(halo_diffused, to, prims)
        put((halo_plus, halo_minus, halo_centre, halo_metric), to,
            *point_fluxes(state, prims, [unit(0, m, row[m]) for m in range(3)]))

    def loader(ref, halo, lead):
        def load(n):
            if 0 <= n < rows_i:
                return ref[lead + (aligned(n * rows_i, rows_i),)]
            r = n + H if n < 0 else n - rows_i + H
            return halo[lead + (aligned(r * rows_i, rows_i),)]

        return load

    metric = loader(metric_i, halo_metric, ())
    for n in range(-1, rows_i):
        face_ref[(n + 1) * rows_i : (n + 2) * rows_i, :] = metric(n) + metric(n + 1)

    def chord(f, carry):
        def store(n, value):
            rows = aligned(n * rows_i, rows_i)
            acc_ref[f, rows, :] = value + normal_ref[f, rows, :]

        sweep(kind, loader(plus_i, halo_plus, (f,)), loader(minus_i, halo_minus, (f,)), loader(centre_i, halo_centre, (f,)),
              loader(diffused_ref, halo_diffused, (f,)), lambda n: face_ref[(n + 1) * rows_i : (n + 2) * rows_i, :],
              store, -1, rows_i - 1)
        return carry

    lax.fori_loop(0, 5, chord, 0)


def span_kernel(dims, kind, final, *refs):
    rows_i, height = dims
    (span_ref, span_met_ref, span_near_ref, span_far_ref, met_near_ref, met_far_ref, plus_k, minus_k, centre_k, metric_k,
     diffused_k,     partner_hbm, state_ref, met_ref, vol_ref, blank_ref, wake_ref, plane_ref, plus_j, minus_j, centre_j, metric_j,
     diffused_ref) = refs[:23]
    refs = refs[23:]
    if final:
        start_ref, out_ref = refs[:2]
        refs = refs[2:]
    else:
        out_ref, out_span_ref = refs[:2]
        outs, refs = refs[2:7], refs[7:]
    (acc_ref, halo_plus, halo_minus, halo_centre, halo_metric, halo_diffused, pad_ref, wall_ref, sum_ref,
     ghost_plus, ghost_minus, ghost_centre, ghost_metric, ghost_diffused, ghost_ref, partner_ref, sem, face_ref) = refs[:18]
    if final:
        staged_ref, out_sems = refs[18:]
    fetch = pltpu.make_async_copy(partner_hbm, partner_ref, sem)
    fetch.start()
    position, count = lax.axis_index("wrap"), lax.axis_size("wrap")
    ghost_diffused[0] = jnp.zeros(ghost_diffused.shape[1:], F32)
    even = lax.rem(lax.axis_index("span"), 2) == 0
    sublane = lax.broadcasted_iota(jnp.int32, (8, 128), 0)
    halo_diffused[0] = jnp.zeros(halo_diffused.shape[1:], F32)
    for r in range(H):
        for f in range(8):
            near_ref, far_ref = (span_near_ref, span_far_ref) if f < 5 else (met_near_ref, met_far_ref)
            near, far = near_ref[f, 2 * r : 2 * r + 2, :], far_ref[f, 2 * r : 2 * r + 2, :]
            pad_ref[f, r * 8 : r * 8 + 2, :] = jnp.where(even, far, near)
            pad_ref[f, (H + r) * 8 + 6 : (H + r) * 8 + 8, :] = jnp.where(even, near, far)
    for r in range(2 * H):
        rows = slice(r * 8, r * 8 + 8)
        values = []
        for f in range(8):
            ref = span_ref if f < 5 else span_met_ref
            if r < H:
                own = pltpu.roll(ref[f, (height - H + r) * 8 : (height - H + r) * 8 + 8, :], 2, 0)
                values.append(jnp.where(sublane < 2, pad_ref[f, rows, :], own))
            else:
                own = pltpu.roll(ref[f, (r - H) * 8 : (r - H) * 8 + 8, :], 6, 0)
                values.append(jnp.where(sublane >= 6, pad_ref[f, rows, :], own))
        prims = primitives(values[:5])
        put_diffused(halo_diffused, rows, prims)
        put((halo_plus, halo_minus, halo_centre, halo_metric), rows,
            *point_fluxes(values[:5], prims, [unit(2, m, values[5 + m]) for m in range(3)]))

    def loader(ref, halo, lead):
        def one(n):
            if 0 <= n < height:
                return ref[lead + (slice(n * 8, n * 8 + 8),)]
            r = n + H if n < 0 else n - height + H
            return halo[lead + (slice(r * 8, r * 8 + 8),)]

        return lambda n: jnp.concatenate([one(n), one(n + height // 2)], axis=0)

    metric = loader(metric_k, halo_metric, ())
    for n in range(-1, height // 2):
        face_ref[(n + 1) * 16 : (n + 2) * 16, :] = metric(n) + metric(n + 1)

    def sweep_span(f, carry):
        def store(n, value):
            acc_ref[f, n * 8 : n * 8 + 8, :] = value[:8]
            m = n + height // 2
            acc_ref[f, m * 8 : m * 8 + 8, :] = value[8:]

        sweep(kind, loader(plus_k, halo_plus, (f,)), loader(minus_k, halo_minus, (f,)), loader(centre_k, halo_centre, (f,)),
              loader(diffused_k, halo_diffused, (f,)), lambda n: face_ref[(n + 1) * 16 : (n + 2) * 16, :],
              store, -1, height // 2 - 1)
        return carry

    lax.fori_loop(0, 5, sweep_span, 0)

    fetch.wait()
    base = (count - 1 - position) * rows_i
    for i in range(rows_i):
        ghost_ref[i * 16 : i * 16 + 16, :] = wake_ref[aligned((partner_ref[i] - base) * 16, 16), :]
    wall = pl.ds(0, rows_i, stride=rows_i)
    for r in range(H):
        state = [ghost_ref[pl.ds(f * H + r, rows_i, stride=16), :] for f in range(5)]
        prims = primitives(state)
        to = slice(r * rows_i, (r + 1) * rows_i)
        put_diffused(ghost_diffused, to, prims)
        put((ghost_plus, ghost_minus, ghost_centre, ghost_metric), to,
            *point_fluxes(state, prims, [unit(1, m, met_ref[3 + m, wall, :]) for m in range(3)]))

    def normal(f):
        def rows(n):
            return pl.ds(n, rows_i, stride=rows_i)

        def loader(ref, halo, lead):
            def load(n):
                if n >= 0:
                    return ref[lead + (rows(n),)]
                return halo[lead + (aligned((-1 - n) * rows_i, rows_i),)]

            return load

        def store(n, value):
            wall_ref[f, n * rows_i : (n + 1) * rows_i, :] = value

        sweep(kind, loader(plus_j, ghost_plus, (f,)), loader(minus_j, ghost_minus, (f,)),
              loader(centre_j, ghost_centre, (f,)), loader(diffused_ref, ghost_diffused, (f,)),
              lambda n: metric_j[rows(max(n, 0)), :] + metric_j[rows(n + 1), :], store, -1, 1, open_high=True)


    scale = (time_step / 12.0) * blank_ref[...].astype(F32) / vol_ref[...]
    for f in range(5):
        normal(f)
        for half in range(2):
            parts = [acc_ref[f, pl.ds(q * 2 + half, height, stride=8), :] for q in range(4)]
            rows = slice(half * 128, (half + 1) * 128)
            sum_ref[f, rows, :] = plane_ref[f, rows, :] + jnp.concatenate(parts, axis=0).T
        for n in range(H):
            rows = pl.ds(n, rows_i, stride=rows_i)
            sum_ref[f, rows, :] = sum_ref[f, rows, :] + wall_ref[f, n * rows_i : (n + 1) * rows_i, :]
        moved = state_ref[f] + scale * sum_ref[f]
        if final:
            staged_ref[f] = 0.5 * start_ref[f] + 0.5 * moved
            pltpu.make_async_copy(staged_ref.at[f], out_ref.at[f], out_sems.at[f]).start()
        else:
            out_ref[f] = moved
    if final:
        for f in range(5):
            pltpu.make_async_copy(staged_ref.at[f], out_ref.at[f], out_sems.at[f]).wait()
    if not final:
        for f in range(5):
            def store(start, block, f=f):
                out_span_ref[f, pl.ds(start, height, stride=8), :] = block

            to_span(out_ref[f], store, height)
        send_parts(out_ref, out_span_ref, 5, outs, dims)


def shape(*sizes):
    return jax.ShapeDtypeStruct(sizes, F32)


def exchange(sent):
    core, chip, wake, span_near, span_far = sent
    n, s = lax.axis_size("wrap"), lax.axis_size("span")
    cores = [(i, i ^ 1) for i in range(n)]
    chips = [pair for i in range(1, n, 2) for pair in ((i, (i + 1) % n), ((i + 1) % n, i))]
    mirror = [(i, n - 1 - i) for i in range(n)]
    near = [(i, i ^ 1) for i in range(s)]
    far = [pair for i in range(1, s, 2) for pair in ((i, (i + 1) % s), ((i + 1) % s, i))]
    return (lax.ppermute(core, "wrap", cores), lax.ppermute(chip, "wrap", chips), lax.ppermute(wake, "wrap", mirror),
            lax.ppermute(span_near, "span", near), lax.ppermute(span_far, "span", far))


def body(density, velocity, pressure, metrics, volume, wake_partner, iblank):
    rows_i, rows_j, lanes = density.shape
    total, height = rows_i * rows_j, lanes // 4
    dims = (rows_i, height)
    volume, blank = volume.reshape(total, lanes), iblank.reshape(total, lanes)
    whole = pl.BlockSpec(memory_space=pltpu.VMEM)
    far = pl.BlockSpec(memory_space=pltpu.HBM)
    wake_partner = pltpu.with_memory_space_constraint(wake_partner, pltpu.HBM)
    params = pltpu.CompilerParams(vmem_limit_bytes=16 * 2**20)

    def call(kernel, name, ins, outs, scratch, specs=None, cost=0, out_specs=None):
        return pl.pallas_call(
            kernel,
            out_shape=outs,
            in_specs=specs or [whole] * len(ins),
            out_specs=out_specs or [whole] * len(outs),
            scratch_shapes=scratch,
            compiler_params=params,
            cost_estimate=pl.CostEstimate(flops=cost, bytes_accessed=cost // 4, transcendentals=0),
            name=name,
        )(*ins)

    def parts(fields):
        edge = H * rows_j
        return [shape(fields, edge, lanes), shape(fields, edge, lanes), shape(rows_i * 16, lanes),
                shape(fields, 8, lanes), shape(fields, 8, lanes)]

    field, span_rows, halo = shape(5, total, lanes), height * 8, 2 * H * rows_i
    state, span, met, *sent = call(
        functools.partial(prepare_kernel, dims), "prepare",
        [pltpu.with_memory_space_constraint(one, pltpu.HBM) for one in (
            density.reshape(total, lanes), velocity.reshape(3, total, lanes), pressure.reshape(total, lanes),
            metrics.reshape(9, total, lanes))],
        [field, shape(8, total, lanes), shape(9, total, lanes)] + parts(8),
        [pltpu.VMEM((total, lanes), F32), pltpu.VMEM((3, total, lanes), F32), pltpu.VMEM((total, lanes), F32),
         pltpu.SemaphoreType.DMA((6,))],
        [far] * 4,
    )
    span_met = span

    def halo_scratch(rows):
        return [pltpu.VMEM((5, rows, lanes), F32)] * 3 + [pltpu.VMEM((rows, lanes), F32), pltpu.VMEM((5, rows, lanes), F32)]

    faces = [pltpu.VMEM(((rows_i + 1) * rows_i, lanes), F32)]

    metric_halo, kept = None, ()
    start = state
    for final in (False, True):
        kind = jnp.bfloat16 if final else F32
        core, chip, wake, span_near, span_far = exchange(sent)
        if metric_halo is None:
            metric_halo = core, chip, span_near, span_far
        line, span_line = shape(5, total, lanes), shape(5, span_rows, lanes)
        (normal, plus_i, minus_i, centre_i, plus_j, minus_j, centre_j, diffused, plus_k, minus_k, centre_k, diffused_k,
         *squares) = call(
            functools.partial(early_kernel, dims, kind, bool(kept)), "early", (state, span, span_met, met, *kept),
            [field] + [line] * 7 + [span_line] * 4
            + ([] if kept else [shape(total, lanes), shape(total, lanes), shape(span_rows, lanes)]),
            faces, cost=10**8,
        )
        kept = kept or tuple(squares)
        metric_i, metric_j, metric_k = kept
        (plane,) = call(
            functools.partial(chord_kernel, dims, kind), "chord",
            (state, met, core, chip, metric_halo[0], metric_halo[1], normal, plus_i, minus_i, centre_i, metric_i,
             diffused),
            [field], halo_scratch(halo) + faces, cost=10**8,
        )
        ins = (span, span_met, span_near, span_far, metric_halo[2], metric_halo[3], plus_k, minus_k, centre_k, metric_k,
               diffused_k, wake_partner, state, met, volume, blank, wake, plane, plus_j, minus_j, centre_j, metric_j, diffused)
        ins += (start,) if final else ()
        state, *rest = call(
            functools.partial(span_kernel, dims, kind, final), "span", ins,
            [field] if final else [field, field] + parts(5),
            [pltpu.VMEM((5, span_rows, lanes), F32)] + halo_scratch(2 * H * 8) + [pltpu.VMEM((8, 2 * H * 8, lanes), F32)]
            + [pltpu.VMEM((5, H * rows_i, lanes), F32), pltpu.VMEM((5, total, lanes), F32)] + halo_scratch(H * rows_i)
            + [pltpu.VMEM((rows_i * 16, lanes), F32), pltpu.SMEM((rows_i,), jnp.int32), pltpu.SemaphoreType.DMA] + faces
            + ([pltpu.VMEM((5, total, lanes), F32), pltpu.SemaphoreType.DMA((5,))] if final else []),
            [whole] * 11 + [far] + [whole] * (len(ins) - 12),
            cost=10**8, out_specs=[far] if final else None,
        )
        if not final:
            span, *sent = rest
    return state.reshape(5, rows_i, rows_j, lanes)


def solution(mesh):
    placed = (
        P("wrap", None, "span"),
        P(None, "wrap", None, "span"),
        P("wrap", None, "span"),
        P(None, "wrap", None, "span"),
        P("wrap", None, "span"),
        P("wrap"),
        P("wrap", None, "span"),
    )
    return jax.shard_map(
        body, mesh=mesh, in_specs=placed, out_specs=P(None, "wrap", None, "span"), check_vma=False
    )
```

```python
import functools

import jax
import jax.numpy as jnp
from jax import lax
from jax.experimental import pallas as pl
from jax.experimental.pallas import tpu as pltpu
from jax.sharding import PartitionSpec as P

epsilon = 1e-06
viscosity = 0.8
conduction = 1.0
time_step = 0.05
metric_scale = 12.0 * viscosity * 0.5
H = 3
F32 = jnp.float32


def primitives(state):
    rho, m0, m1, m2, energy = state
    inverse = 1.0 / rho
    velocity = (m0 * inverse, m1 * inverse, m2 * inverse)
    speed_sq = velocity[0] * velocity[0] + velocity[1] * velocity[1] + velocity[2] * velocity[2]
    pressure = 0.4 * (energy - 0.5 * rho * speed_sq)
    ratio = pressure * inverse
    heat = 0.5 * speed_sq + conduction * ratio
    return velocity, pressure, energy + pressure, (1.4 / metric_scale) * ratio, heat


def point_fluxes(state, prims, row, metric=None):
    rho, m0, m1, m2, _ = state
    (u0, u1, u2), pressure, enthalpy, sound_sq, _ = prims
    x0, x1, x2 = row
    contra = x0 * u0 + x1 * u1 + x2 * u2
    if metric is None:
        metric = (x0 * x0 + x1 * x1 + x2 * x2) * metric_scale
    square = sound_sq * metric
    speed = jnp.abs(contra) + square * lax.rsqrt(jnp.maximum(square, 1e-30))
    fluxes = (
        rho * contra,
        m0 * contra + x0 * pressure,
        m1 * contra + x1 * pressure,
        m2 * contra + x2 * pressure,
        enthalpy * contra,
    )
    waves = [speed * one for one in state]
    plus = [a + b for a, b in zip(fluxes, waves)]
    minus = [a - b for a, b in zip(fluxes, waves)]
    return plus, minus, [6.0 * one for one in fluxes], metric


def RCP(x):
    return pl.reciprocal(x, approx=True)


def add(a, b):
    if a is None or b is None:
        return b if a is None else a
    return a + b


def subtract(a, b):
    if b is None:
        return a
    return -b if a is None else a - b


def multiply(a, b):
    return None if a is None or b is None else a * b


class Split:
    def __init__(self, load, kind, flat=None):
        self.load, self.memo, self.kind, self.flat = load, {}, kind, flat

    def get(self, name, n):
        if (name, n) not in self.memo:
            self.memo[name, n] = getattr(self, "make_" + name)(n)
        return self.memo[name, n]

    def cast(self, value):
        return None if value is None else value.astype(self.kind)

    def make_v(self, n):
        return self.load(n)

    def make_d(self, n):
        if self.flat is not None and n >= self.flat:
            return None
        return self.get("v", n + 1) - self.get("v", n)

    def make_e(self, n):
        return subtract(self.get("d", n), self.get("d", n - 1))

    def make_t(self, n):
        return subtract(self.get("e", n + 1), self.get("e", n))

    def make_near(self, n):
        return self.cast(self.get("t", n))

    def make_near2(self, n):
        return add(self.get("near", n), self.get("near", n))

    def make_low(self, n):
        return self.cast(self.get("d", n))

    def make_smooth(self, n):
        high, low = self.get("low", n), self.get("low", n - 1)
        bend = self.cast(self.get("e", n))
        least = self.kind(16.0 * epsilon / 3.0)
        if bend is None:
            return (jnp.full(self.get("v", self.flat).shape, least, self.kind),) * 3
        twice = bend + bend
        a, b = multiply(high, twice), multiply(low, twice)
        centre = subtract(a, b) * self.kind(2.0 / 3.0) + add(multiply(high, low), least)
        return add(a, centre), centre, subtract(centre, b)

    def correction(self, outer, middle, inner, near, far):
        left = middle * RCP(outer)
        right = middle * RCP(inner)
        weight_left = left * left * self.kind(1.0 / 3.0)
        weight_right = right * right
        total = (weight_left + weight_right) + self.kind(2.0)
        return add(multiply(weight_left, near), multiply(weight_right, far)) * RCP(total)


def sweep(kind, load_plus, load_minus, load_centre, load_diffused, load_face, store, first, last, open_low=False, open_high=False,
          flat=None):
    plus, minus = Split(load_plus, kind, flat), Split(load_minus, kind, flat)
    central, diffused = {}, {}

    def cached(table, load, n):
        if n not in table:
            table[n] = load(n)
        return table[n]

    before = None
    for n in range(first, last + 1):
        up = plus.correction(
            plus.get("smooth", n - 1)[0],
            plus.get("smooth", n)[1],
            plus.get("smooth", n + 1)[2],
            plus.get("near2", n - 1),
            plus.get("near", n),
        )
        down = minus.correction(
            minus.get("smooth", n + 2)[2],
            minus.get("smooth", n + 1)[1],
            minus.get("smooth", n)[0],
            minus.get("near2", n + 1),
            minus.get("near", n),
        )
        centres = [cached(central, load_centre, m if flat is None else min(m, flat)) for m in (n, n + 1)]
        flux = (centres[0] + centres[1]) - add(plus.get("e", n), minus.get("e", n + 1)) + (down - up).astype(F32)
        if flat is not None and n >= flat:
            net = -flux
        else:
            jump = cached(diffused, load_diffused, n + 1) - cached(diffused, load_diffused, n)
            net = load_face(n) * jump - flux
        if before is not None:
            store(n, net - before)
        elif open_low:
            store(n, net)
        before = net
    if open_high:
        store(last + 1, -before)


def put(refs, rows, plus, minus, centre, metric=None):
    plus_ref, minus_ref, centre_ref, metric_ref = refs
    for f in range(5):
        plus_ref[f, rows, :] = plus[f]
        minus_ref[f, rows, :] = minus[f]
        centre_ref[f, rows, :] = centre[f]
    if metric is not None:
        metric_ref[rows, :] = metric


def put_diffused(ref, rows, prims):
    for m in range(3):
        ref[1 + m, rows, :] = prims[0][m]
    ref[4, rows, :] = prims[4]


def aligned(start, count):
    return pl.ds(pl.multiple_of(start, 8), count)


def unit(which, m, value):
    return value + 1.0 if which == m else value


def to_span(value, store, height):
    for half in range(2):
        turned = value[half * 128 : (half + 1) * 128].T
        for q in range(4):
            store(q * 2 + half, turned[q * height : (q + 1) * height])


def send_parts(state_ref, span_ref, fields, outs, dims):
    rows_i, height = dims
    total = rows_i * rows_i
    core_ref, chip_ref, wake_ref, span_near_ref, span_far_ref = outs
    even = lax.rem(lax.axis_index("wrap"), 2) == 0
    edge = H * rows_i
    to_core, to_chip = jnp.where(even, total - edge, 0), jnp.where(even, 0, total - edge)
    for f in range(5):
        core_ref[f] = state_ref[f, aligned(to_core, edge), :]
        chip_ref[f] = state_ref[f, aligned(to_chip, edge), :]
        for r in range(H):
            wake_ref[pl.ds(f * H + r, rows_i, stride=16), :] = state_ref[f, pl.ds(r + 1, rows_i, stride=rows_i), :]
    even = lax.rem(lax.axis_index("span"), 2) == 0
    for f in range(fields):
        for r in range(H):
            top = (height - H + r) * 8
            low, high = span_ref[f, r * 8 : r * 8 + 2, :], span_ref[f, top + 6 : top + 8, :]
            span_near_ref[f, 2 * r : 2 * r + 2, :] = jnp.where(even, high, low)
            span_far_ref[f, 2 * r : 2 * r + 2, :] = jnp.where(even, low, high)


def prepare_kernel(dims, rho_hbm, vel_hbm, pre_hbm, met_hbm, state_ref, span_ref, met_ref, *refs):
    outs, (rho_ref, vel_ref, pre_ref, sems) = refs[:5], refs[5:]
    rows_i, height = dims
    total = rows_i * rows_i
    pairs = [(rho_hbm, rho_ref), (vel_hbm, vel_ref), (pre_hbm, pre_ref)]
    pairs += [(met_hbm.at[pl.ds(3 * d, 3)], met_ref.at[pl.ds(3 * d, 3)]) for d in (2, 0, 1)]
    copies = [pltpu.make_async_copy(a, b, sems.at[n]) for n, (a, b) in enumerate(pairs)]
    for copy in copies:
        copy.start()
    for copy in copies[:3]:
        copy.wait()
    rho, pressure = rho_ref[...], pre_ref[...]
    u = [vel_ref[m] for m in range(3)]
    speed_sq = u[0] * u[0] + u[1] * u[1] + u[2] * u[2]
    state_ref[0] = rho
    for m in range(3):
        state_ref[1 + m] = rho * u[m]
    state_ref[4] = pressure * (1.0 / 0.4) + 0.5 * rho * speed_sq
    core_ref, chip_ref = outs[:2]
    for f in range(8):
        if f == 5:
            copies[3].wait()
        value = state_ref[f] if f < 5 else met_ref[6 + f - 5]

        def store(start, block, f=f):
            span_ref[f, pl.ds(start, height, stride=8), :] = block

        to_span(value, store, height)
    send_parts(state_ref, span_ref, 8, outs, dims)
    copies[4].wait()
    even = lax.rem(lax.axis_index("wrap"), 2) == 0
    edge = H * rows_i
    to_core, to_chip = jnp.where(even, total - edge, 0), jnp.where(even, 0, total - edge)
    for m in range(3):
        core_ref[5 + m] = met_ref[m, aligned(to_core, edge), :]
        chip_ref[5 + m] = met_ref[m, aligned(to_chip, edge), :]
    copies[5].wait()


def early_kernel(dims, kind, kept, state_ref, span_ref, span_met_ref, met_ref, *refs):
    rows_i, height = dims
    if kept:
        metric_i, metric_j, metric_k = refs[:3]
        refs = refs[3:]
    acc_ref, plus_i, minus_i, centre_i, plus_j, minus_j, centre_j, diffused_ref, plus_k, minus_k, centre_k, diffused_k = refs[:12]
    if not kept:
        metric_i, metric_j, metric_k = refs[12:15]
    face_ref = refs[-1]
    diffused_ref[0] = jnp.zeros(diffused_ref.shape[1:], F32)
    diffused_k[0] = jnp.zeros(diffused_k.shape[1:], F32)

    def place(refs, metric_ref, rows, state, prims, row):
        *fluxes, metric = point_fluxes(state, prims, row, metric_ref[rows, :] if kept else None)
        put((*refs, metric_ref), rows, *fluxes, None if kept else metric)

    def planes(n, carry):
        rows = aligned(n * rows_i, rows_i)
        state = [state_ref[f, rows, :] for f in range(5)]
        prims = primitives(state)
        put_diffused(diffused_ref, rows, prims)
        place((plus_i, minus_i, centre_i), metric_i, rows, state, prims, [unit(0, m, met_ref[m, rows, :]) for m in range(3)])
        place((plus_j, minus_j, centre_j), metric_j, rows, state, prims, [unit(1, m, met_ref[3 + m, rows, :]) for m in range(3)])
        return carry

    lax.fori_loop(0, rows_i, planes, 0, unroll=4)

    def spans(n, carry):
        rows = aligned(n * 16, 16)
        state = [span_ref[f, rows, :] for f in range(5)]
        prims = primitives(state)
        put_diffused(diffused_k, rows, prims)
        place((plus_k, minus_k, centre_k), metric_k, rows, state, prims, [unit(2, m, span_met_ref[5 + m, rows, :]) for m in range(3)])
        return carry

    lax.fori_loop(0, height // 2, spans, 0, unroll=4)

    for n in range(2, rows_i - 1):
        low, high = (metric_j[pl.ds(m, rows_i, stride=rows_i), :] for m in (n, n + 1))
        face_ref[n * rows_i : (n + 1) * rows_i, :] = low + high

    def normal(f, carry):
        def rows(n):
            return pl.ds(min(n, rows_i - 1), rows_i, stride=rows_i)

        def store(n, value):
            acc_ref[f, rows(n), :] = value

        for n in range(2):
            store(n, jnp.zeros((rows_i, 128), F32))
        sweep(kind, lambda n: plus_j[f, rows(n), :], lambda n: minus_j[f, rows(n), :], lambda n: centre_j[f, rows(n), :],
              lambda n: diffused_ref[f, rows(n), :], lambda n: face_ref[n * rows_i : (n + 1) * rows_i, :],
              store, 2, rows_i - 1, open_low=True,
              flat=rows_i - 1)
        return carry

    lax.fori_loop(0, 5, normal, 0, unroll=5)


def chord_kernel(dims, kind, state_ref, met_ref, core_ref, chip_ref, met_core_ref, met_chip_ref, normal_ref,
                 plus_i, minus_i, centre_i, metric_i, diffused_ref, acc_ref,
                 halo_plus, halo_minus, halo_centre, halo_metric, halo_diffused, face_ref):
    rows_i, height = dims
    total = rows_i * rows_i
    position, count = lax.axis_index("wrap"), lax.axis_size("wrap")
    even = lax.rem(position, 2) == 0
    at_end = (position == 0) | (position == count - 1)
    halo_diffused[0] = jnp.zeros(halo_diffused.shape[1:], F32)

    core_rows, chip_rows = jnp.where(even, H, 0), jnp.where(even, 0, H)
    own = jnp.where(even, 0, total - rows_i)
    for r in range(H):
        rows = slice(r * rows_i, (r + 1) * rows_i)
        state = [core_ref[f, rows, :] for f in range(5)]
        prims = primitives(state)
        to = aligned((core_rows + r) * rows_i, rows_i)
        put_diffused(halo_diffused, to, prims)
        put((halo_plus, halo_minus, halo_centre, halo_metric), to,
            *point_fluxes(state, prims, [unit(0, m, met_core_ref[5 + m, rows, :]) for m in range(3)]))
        edge = aligned(own, rows_i)
        state = [jnp.where(at_end, state_ref[f, edge, :], chip_ref[f, rows, :]) for f in range(5)]
        row = [jnp.where(at_end, met_ref[m, edge, :], met_chip_ref[5 + m, rows, :]) for m in range(3)]
        prims = primitives(state)
        to = aligned((chip_rows + r) * rows_i, rows_i)
        put_diffused(halo_diffused, to, prims)
        put((halo_plus, halo_minus, halo_centre, halo_metric), to,
            *point_fluxes(state, prims, [unit(0, m, row[m]) for m in range(3)]))

    def loader(ref, halo, lead):
        def load(n):
            if 0 <= n < rows_i:
                return ref[lead + (aligned(n * rows_i, rows_i),)]
            r = n + H if n < 0 else n - rows_i + H
            return halo[lead + (aligned(r * rows_i, rows_i),)]

        return load

    metric = loader(metric_i, halo_metric, ())
    for n in range(-1, rows_i):
        face_ref[(n + 1) * rows_i : (n + 2) * rows_i, :] = metric(n) + metric(n + 1)

    def chord(f, carry):
        def store(n, value):
            rows = aligned(n * rows_i, rows_i)
            acc_ref[f, rows, :] = value + normal_ref[f, rows, :]

        sweep(kind, loader(plus_i, halo_plus, (f,)), loader(minus_i, halo_minus, (f,)), loader(centre_i, halo_centre, (f,)),
              loader(diffused_ref, halo_diffused, (f,)), lambda n: face_ref[(n + 1) * rows_i : (n + 2) * rows_i, :],
              store, -1, rows_i - 1)
        return carry

    lax.fori_loop(0, 5, chord, 0, unroll=5)


def span_kernel(dims, kind, final, *refs):
    rows_i, height = dims
    (span_ref, span_met_ref, span_near_ref, span_far_ref, met_near_ref, met_far_ref, plus_k, minus_k, centre_k, metric_k,
     diffused_k,     partner_hbm, state_ref, met_ref, vol_ref, blank_ref, wake_ref, plane_ref, plus_j, minus_j, centre_j, metric_j,
     diffused_ref) = refs[:23]
    refs = refs[23:]
    if final:
        start_ref, out_ref = refs[:2]
        refs = refs[2:]
    else:
        out_ref, out_span_ref = refs[:2]
        outs, refs = refs[2:7], refs[7:]
    (acc_ref, halo_plus, halo_minus, halo_centre, halo_metric, halo_diffused, pad_ref, wall_ref, sum_ref,
     ghost_plus, ghost_minus, ghost_centre, ghost_metric, ghost_diffused, ghost_ref, partner_ref, sem, face_ref) = refs[:18]
    if final:
        staged_ref, out_sems = refs[18:]
    fetch = pltpu.make_async_copy(partner_hbm, partner_ref, sem)
    fetch.start()
    position, count = lax.axis_index("wrap"), lax.axis_size("wrap")
    ghost_diffused[0] = jnp.zeros(ghost_diffused.shape[1:], F32)
    even = lax.rem(lax.axis_index("span"), 2) == 0
    sublane = lax.broadcasted_iota(jnp.int32, (8, 128), 0)
    halo_diffused[0] = jnp.zeros(halo_diffused.shape[1:], F32)
    for r in range(H):
        for f in range(8):
            near_ref, far_ref = (span_near_ref, span_far_ref) if f < 5 else (met_near_ref, met_far_ref)
            near, far = near_ref[f, 2 * r : 2 * r + 2, :], far_ref[f, 2 * r : 2 * r + 2, :]
            pad_ref[f, r * 8 : r * 8 + 2, :] = jnp.where(even, far, near)
            pad_ref[f, (H + r) * 8 + 6 : (H + r) * 8 + 8, :] = jnp.where(even, near, far)
    for r in range(2 * H):
        rows = slice(r * 8, r * 8 + 8)
        values = []
        for f in range(8):
            ref = span_ref if f < 5 else span_met_ref
            if r < H:
                own = pltpu.roll(ref[f, (height - H + r) * 8 : (height - H + r) * 8 + 8, :], 2, 0)
                values.append(jnp.where(sublane < 2, pad_ref[f, rows, :], own))
            else:
                own = pltpu.roll(ref[f, (r - H) * 8 : (r - H) * 8 + 8, :], 6, 0)
                values.append(jnp.where(sublane >= 6, pad_ref[f, rows, :], own))
        prims = primitives(values[:5])
        put_diffused(halo_diffused, rows, prims)
        put((halo_plus, halo_minus, halo_centre, halo_metric), rows,
            *point_fluxes(values[:5], prims, [unit(2, m, values[5 + m]) for m in range(3)]))

    def loader(ref, halo, lead):
        def one(n):
            if 0 <= n < height:
                return ref[lead + (slice(n * 8, n * 8 + 8),)]
            r = n + H if n < 0 else n - height + H
            return halo[lead + (slice(r * 8, r * 8 + 8),)]

        return lambda n: jnp.concatenate([one(n), one(n + height // 2)], axis=0)

    metric = loader(metric_k, halo_metric, ())
    for n in range(-1, height // 2):
        face_ref[(n + 1) * 16 : (n + 2) * 16, :] = metric(n) + metric(n + 1)

    def sweep_span(f, carry):
        def store(n, value):
            acc_ref[f, n * 8 : n * 8 + 8, :] = value[:8]
            m = n + height // 2
            acc_ref[f, m * 8 : m * 8 + 8, :] = value[8:]

        sweep(kind, loader(plus_k, halo_plus, (f,)), loader(minus_k, halo_minus, (f,)), loader(centre_k, halo_centre, (f,)),
              loader(diffused_k, halo_diffused, (f,)), lambda n: face_ref[(n + 1) * 16 : (n + 2) * 16, :],
              store, -1, height // 2 - 1)
        return carry

    lax.fori_loop(0, 5, sweep_span, 0, unroll=5)

    fetch.wait()
    base = (count - 1 - position) * rows_i
    for i in range(rows_i):
        ghost_ref[i * 16 : i * 16 + 16, :] = wake_ref[aligned((partner_ref[i] - base) * 16, 16), :]
    wall = pl.ds(0, rows_i, stride=rows_i)
    for r in range(H):
        state = [ghost_ref[pl.ds(f * H + r, rows_i, stride=16), :] for f in range(5)]
        prims = primitives(state)
        to = slice(r * rows_i, (r + 1) * rows_i)
        put_diffused(ghost_diffused, to, prims)
        put((ghost_plus, ghost_minus, ghost_centre, ghost_metric), to,
            *point_fluxes(state, prims, [unit(1, m, met_ref[3 + m, wall, :]) for m in range(3)]))

    def normal(f):
        def rows(n):
            return pl.ds(n, rows_i, stride=rows_i)

        def loader(ref, halo, lead):
            def load(n):
                if n >= 0:
                    return ref[lead + (rows(n),)]
                return halo[lead + (aligned((-1 - n) * rows_i, rows_i),)]

            return load

        def store(n, value):
            wall_ref[f, n * rows_i : (n + 1) * rows_i, :] = value

        sweep(kind, loader(plus_j, ghost_plus, (f,)), loader(minus_j, ghost_minus, (f,)),
              loader(centre_j, ghost_centre, (f,)), loader(diffused_ref, ghost_diffused, (f,)),
              lambda n: metric_j[rows(max(n, 0)), :] + metric_j[rows(n + 1), :], store, -1, 1, open_high=True)


    scale = (time_step / 12.0) * blank_ref[...].astype(F32) / vol_ref[...]
    for f in range(5):
        normal(f)
        for half in range(2):
            parts = [acc_ref[f, pl.ds(q * 2 + half, height, stride=8), :] for q in range(4)]
            rows = slice(half * 128, (half + 1) * 128)
            sum_ref[f, rows, :] = plane_ref[f, rows, :] + jnp.concatenate(parts, axis=0).T
        for n in range(H):
            rows = pl.ds(n, rows_i, stride=rows_i)
            sum_ref[f, rows, :] = sum_ref[f, rows, :] + wall_ref[f, n * rows_i : (n + 1) * rows_i, :]
        moved = state_ref[f] + scale * sum_ref[f]
        if final:
            staged_ref[f] = 0.5 * start_ref[f] + 0.5 * moved
            pltpu.make_async_copy(staged_ref.at[f], out_ref.at[f], out_sems.at[f]).start()
        else:
            out_ref[f] = moved
    if final:
        for f in range(5):
            pltpu.make_async_copy(staged_ref.at[f], out_ref.at[f], out_sems.at[f]).wait()
    if not final:
        for f in range(5):
            def store(start, block, f=f):
                out_span_ref[f, pl.ds(start, height, stride=8), :] = block

            to_span(out_ref[f], store, height)
        send_parts(out_ref, out_span_ref, 5, outs, dims)


def shape(*sizes):
    return jax.ShapeDtypeStruct(sizes, F32)


def exchange(sent):
    core, chip, wake, span_near, span_far = sent
    n, s = lax.axis_size("wrap"), lax.axis_size("span")
    cores = [(i, i ^ 1) for i in range(n)]
    chips = [pair for i in range(1, n, 2) for pair in ((i, (i + 1) % n), ((i + 1) % n, i))]
    mirror = [(i, n - 1 - i) for i in range(n)]
    near = [(i, i ^ 1) for i in range(s)]
    far = [pair for i in range(1, s, 2) for pair in ((i, (i + 1) % s), ((i + 1) % s, i))]
    return (lax.ppermute(core, "wrap", cores), lax.ppermute(chip, "wrap", chips), lax.ppermute(wake, "wrap", mirror),
            lax.ppermute(span_near, "span", near), lax.ppermute(span_far, "span", far))


def body(density, velocity, pressure, metrics, volume, wake_partner, iblank):
    rows_i, rows_j, lanes = density.shape
    total, height = rows_i * rows_j, lanes // 4
    dims = (rows_i, height)
    volume, blank = volume.reshape(total, lanes), iblank.reshape(total, lanes)
    whole = pl.BlockSpec(memory_space=pltpu.VMEM)
    far = pl.BlockSpec(memory_space=pltpu.HBM)
    wake_partner = pltpu.with_memory_space_constraint(wake_partner, pltpu.HBM)
    params = pltpu.CompilerParams(vmem_limit_bytes=16 * 2**20)

    def call(kernel, name, ins, outs, scratch, specs=None, cost=0, out_specs=None):
        return pl.pallas_call(
            kernel,
            out_shape=outs,
            in_specs=specs or [whole] * len(ins),
            out_specs=out_specs or [whole] * len(outs),
            scratch_shapes=scratch,
            compiler_params=params,
            cost_estimate=pl.CostEstimate(flops=cost, bytes_accessed=cost // 4, transcendentals=0),
            name=name,
        )(*ins)

    def parts(fields):
        edge = H * rows_j
        return [shape(fields, edge, lanes), shape(fields, edge, lanes), shape(rows_i * 16, lanes),
                shape(fields, 8, lanes), shape(fields, 8, lanes)]

    field, span_rows, halo = shape(5, total, lanes), height * 8, 2 * H * rows_i
    state, span, met, *sent = call(
        functools.partial(prepare_kernel, dims), "prepare",
        [pltpu.with_memory_space_constraint(one, pltpu.HBM) for one in (
            density.reshape(total, lanes), velocity.reshape(3, total, lanes), pressure.reshape(total, lanes),
            metrics.reshape(9, total, lanes))],
        [field, shape(8, total, lanes), shape(9, total, lanes)] + parts(8),
        [pltpu.VMEM((total, lanes), F32), pltpu.VMEM((3, total, lanes), F32), pltpu.VMEM((total, lanes), F32),
         pltpu.SemaphoreType.DMA((6,))],
        [far] * 4,
    )
    span_met = span

    def halo_scratch(rows):
        return [pltpu.VMEM((5, rows, lanes), F32)] * 3 + [pltpu.VMEM((rows, lanes), F32), pltpu.VMEM((5, rows, lanes), F32)]

    faces = [pltpu.VMEM(((rows_i + 1) * rows_i, lanes), F32)]

    metric_halo, kept = None, ()
    start = state
    for final in (False, True):
        kind = jnp.bfloat16 if final else F32
        core, chip, wake, span_near, span_far = exchange(sent)
        if metric_halo is None:
            metric_halo = core, chip, span_near, span_far
        line, span_line = shape(5, total, lanes), shape(5, span_rows, lanes)
        (normal, plus_i, minus_i, centre_i, plus_j, minus_j, centre_j, diffused, plus_k, minus_k, centre_k, diffused_k,
         *squares) = call(
            functools.partial(early_kernel, dims, kind, bool(kept)), "early", (state, span, span_met, met, *kept),
            [field] + [line] * 7 + [span_line] * 4
            + ([] if kept else [shape(total, lanes), shape(total, lanes), shape(span_rows, lanes)]),
            faces, cost=10**8,
        )
        kept = kept or tuple(squares)
        metric_i, metric_j, metric_k = kept
        (plane,) = call(
            functools.partial(chord_kernel, dims, kind), "chord",
            (state, met, core, chip, metric_halo[0], metric_halo[1], normal, plus_i, minus_i, centre_i, metric_i,
             diffused),
            [field], halo_scratch(halo) + faces, cost=10**8,
        )
        ins = (span, span_met, span_near, span_far, metric_halo[2], metric_halo[3], plus_k, minus_k, centre_k, metric_k,
               diffused_k, wake_partner, state, met, volume, blank, wake, plane, plus_j, minus_j, centre_j, metric_j, diffused)
        ins += (start,) if final else ()
        state, *rest = call(
            functools.partial(span_kernel, dims, kind, final), "span", ins,
            [field] if final else [field, field] + parts(5),
            [pltpu.VMEM((5, span_rows, lanes), F32)] + halo_scratch(2 * H * 8) + [pltpu.VMEM((8, 2 * H * 8, lanes), F32)]
            + [pltpu.VMEM((5, H * rows_i, lanes), F32), pltpu.VMEM((5, total, lanes), F32)] + halo_scratch(H * rows_i)
            + [pltpu.VMEM((rows_i * 16, lanes), F32), pltpu.SMEM((rows_i,), jnp.int32), pltpu.SemaphoreType.DMA] + faces
            + ([pltpu.VMEM((5, total, lanes), F32), pltpu.SemaphoreType.DMA((5,))] if final else []),
            [whole] * 11 + [far] + [whole] * (len(ins) - 12),
            cost=10**8, out_specs=[far] if final else None,
        )
        if not final:
            span, *sent = rest
    return state.reshape(5, rows_i, rows_j, lanes)


def solution(mesh):
    placed = (
        P("wrap", None, "span"),
        P(None, "wrap", None, "span"),
        P("wrap", None, "span"),
        P(None, "wrap", None, "span"),
        P("wrap", None, "span"),
        P("wrap"),
        P("wrap", None, "span"),
    )
    return jax.shard_map(
        body, mesh=mesh, in_specs=placed, out_specs=P(None, "wrap", None, "span"), check_vma=False
    )
```

```python
import functools

import jax
import jax.numpy as jnp
from jax import lax
from jax.experimental import pallas as pl
from jax.experimental.pallas import tpu as pltpu
from jax.sharding import PartitionSpec as P

epsilon = 1e-06
viscosity = 0.8
conduction = 1.0
time_step = 0.05
metric_scale = 12.0 * viscosity * 0.5
H = 3
F32 = jnp.float32


def primitives(state):
    rho, m0, m1, m2, energy = state
    inverse = 1.0 / rho
    velocity = (m0 * inverse, m1 * inverse, m2 * inverse)
    speed_sq = velocity[0] * velocity[0] + velocity[1] * velocity[1] + velocity[2] * velocity[2]
    pressure = 0.4 * (energy - 0.5 * rho * speed_sq)
    ratio = pressure * inverse
    heat = 0.5 * speed_sq + conduction * ratio
    return velocity, pressure, energy + pressure, (1.4 / metric_scale) * ratio, heat


def point_fluxes(state, prims, row, metric=None):
    rho, m0, m1, m2, _ = state
    (u0, u1, u2), pressure, enthalpy, sound_sq, _ = prims
    x0, x1, x2 = row
    contra = x0 * u0 + x1 * u1 + x2 * u2
    if metric is None:
        metric = (x0 * x0 + x1 * x1 + x2 * x2) * metric_scale
    square = sound_sq * metric
    speed = jnp.abs(contra) + square * lax.rsqrt(jnp.maximum(square, 1e-30))
    fluxes = (
        rho * contra,
        m0 * contra + x0 * pressure,
        m1 * contra + x1 * pressure,
        m2 * contra + x2 * pressure,
        enthalpy * contra,
    )
    waves = [speed * one for one in state]
    plus = [a + b for a, b in zip(fluxes, waves)]
    minus = [a - b for a, b in zip(fluxes, waves)]
    return plus, minus, [6.0 * one for one in fluxes], metric


def RCP(x):
    return pl.reciprocal(x, approx=True)


def add(a, b):
    if a is None or b is None:
        return b if a is None else a
    return a + b


def subtract(a, b):
    if b is None:
        return a
    return -b if a is None else a - b


def multiply(a, b):
    return None if a is None or b is None else a * b


class Split:
    def __init__(self, load, kind, flat=None):
        self.load, self.memo, self.kind, self.flat = load, {}, kind, flat

    def get(self, name, n):
        if (name, n) not in self.memo:
            self.memo[name, n] = getattr(self, "make_" + name)(n)
        return self.memo[name, n]

    def cast(self, value):
        return None if value is None else value.astype(self.kind)

    def make_v(self, n):
        return self.load(n)

    def make_d(self, n):
        if self.flat is not None and n >= self.flat:
            return None
        return self.get("v", n + 1) - self.get("v", n)

    def make_e(self, n):
        return subtract(self.get("d", n), self.get("d", n - 1))

    def make_t(self, n):
        return subtract(self.get("e", n + 1), self.get("e", n))

    def make_near(self, n):
        return self.cast(self.get("t", n))

    def make_near2(self, n):
        return add(self.get("near", n), self.get("near", n))

    def make_low(self, n):
        return self.cast(self.get("d", n))

    def make_smooth(self, n):
        high, low = self.get("low", n), self.get("low", n - 1)
        bend = self.cast(self.get("e", n))
        least = self.kind(16.0 * epsilon / 3.0)
        if bend is None:
            return (jnp.full(self.get("v", self.flat).shape, least, self.kind),) * 3
        twice = bend + bend
        a, b = multiply(high, twice), multiply(low, twice)
        centre = subtract(a, b) * self.kind(2.0 / 3.0) + add(multiply(high, low), least)
        return add(a, centre), centre, subtract(centre, b)

    def correction(self, outer, middle, inner, near, far):
        left = middle * RCP(outer)
        right = middle * RCP(inner)
        weight_left = left * left * self.kind(1.0 / 3.0)
        weight_right = right * right
        total = (weight_left + weight_right) + self.kind(2.0)
        return add(multiply(weight_left, near), multiply(weight_right, far)) * RCP(total)


def sweep(kind, load_plus, load_minus, load_centre, load_diffused, load_face, store, first, last, open_low=False, open_high=False,
          flat=None):
    plus, minus = Split(load_plus, kind, flat), Split(load_minus, kind, flat)
    central, diffused = {}, {}

    def cached(table, load, n):
        if n not in table:
            table[n] = load(n)
        return table[n]

    before = None
    for n in range(first, last + 1):
        up = plus.correction(
            plus.get("smooth", n - 1)[0],
            plus.get("smooth", n)[1],
            plus.get("smooth", n + 1)[2],
            plus.get("near2", n - 1),
            plus.get("near", n),
        )
        down = minus.correction(
            minus.get("smooth", n + 2)[2],
            minus.get("smooth", n + 1)[1],
            minus.get("smooth", n)[0],
            minus.get("near2", n + 1),
            minus.get("near", n),
        )
        centres = [cached(central, load_centre, m if flat is None else min(m, flat)) for m in (n, n + 1)]
        flux = (centres[0] + centres[1]) - add(plus.get("e", n), minus.get("e", n + 1)) + (down - up).astype(F32)
        if flat is not None and n >= flat:
            net = -flux
        else:
            jump = cached(diffused, load_diffused, n + 1) - cached(diffused, load_diffused, n)
            net = load_face(n) * jump - flux
        if before is not None:
            store(n, net - before)
        elif open_low:
            store(n, net)
        before = net
    if open_high:
        store(last + 1, -before)


def put(refs, rows, plus, minus, centre, metric=None):
    plus_ref, minus_ref, centre_ref, metric_ref = refs
    for f in range(5):
        plus_ref[f, rows, :] = plus[f]
        minus_ref[f, rows, :] = minus[f]
        centre_ref[f, rows, :] = centre[f]
    if metric is not None:
        metric_ref[rows, :] = metric


def put_diffused(ref, rows, prims):
    for m in range(3):
        ref[1 + m, rows, :] = prims[0][m]
    ref[4, rows, :] = prims[4]


def aligned(start, count):
    return pl.ds(pl.multiple_of(start, 8), count)


def unit(which, m, value):
    return value + 1.0 if which == m else value


def to_span(value, store, height):
    for half in range(2):
        turned = value[half * 128 : (half + 1) * 128].T
        for q in range(4):
            store(q * 2 + half, turned[q * height : (q + 1) * height])


def send_parts(state_ref, span_ref, fields, outs, dims):
    rows_i, height = dims
    total = rows_i * rows_i
    core_ref, chip_ref, wake_ref, span_near_ref, span_far_ref = outs
    even = lax.rem(lax.axis_index("wrap"), 2) == 0
    edge = H * rows_i
    to_core, to_chip = jnp.where(even, total - edge, 0), jnp.where(even, 0, total - edge)
    for f in range(5):
        core_ref[f] = state_ref[f, aligned(to_core, edge), :]
        chip_ref[f] = state_ref[f, aligned(to_chip, edge), :]
        for r in range(H):
            wake_ref[pl.ds(f * H + r, rows_i, stride=16), :] = state_ref[f, pl.ds(r + 1, rows_i, stride=rows_i), :]
    even = lax.rem(lax.axis_index("span"), 2) == 0
    for f in range(fields):
        for r in range(H):
            top = (height - H + r) * 8
            low, high = span_ref[f, r * 8 : r * 8 + 2, :], span_ref[f, top + 6 : top + 8, :]
            span_near_ref[f, 2 * r : 2 * r + 2, :] = jnp.where(even, high, low)
            span_far_ref[f, 2 * r : 2 * r + 2, :] = jnp.where(even, low, high)


def prepare_kernel(dims, rho_hbm, vel_hbm, pre_hbm, met_hbm, state_ref, span_ref, met_ref, *refs):
    outs, (rho_ref, vel_ref, pre_ref, sems) = refs[:5], refs[5:]
    rows_i, height = dims
    total = rows_i * rows_i
    pairs = [(rho_hbm, rho_ref), (vel_hbm, vel_ref), (pre_hbm, pre_ref)]
    pairs += [(met_hbm.at[pl.ds(3 * d, 3)], met_ref.at[pl.ds(3 * d, 3)]) for d in (2, 0, 1)]
    copies = [pltpu.make_async_copy(a, b, sems.at[n]) for n, (a, b) in enumerate(pairs)]
    for copy in copies:
        copy.start()
    for copy in copies[:3]:
        copy.wait()
    rho, pressure = rho_ref[...], pre_ref[...]
    u = [vel_ref[m] for m in range(3)]
    speed_sq = u[0] * u[0] + u[1] * u[1] + u[2] * u[2]
    state_ref[0] = rho
    for m in range(3):
        state_ref[1 + m] = rho * u[m]
    state_ref[4] = pressure * (1.0 / 0.4) + 0.5 * rho * speed_sq
    core_ref, chip_ref = outs[:2]
    for f in range(8):
        if f == 5:
            copies[3].wait()
        value = state_ref[f] if f < 5 else met_ref[6 + f - 5]

        def store(start, block, f=f):
            span_ref[f, pl.ds(start, height, stride=8), :] = block

        to_span(value, store, height)
    send_parts(state_ref, span_ref, 8, outs, dims)
    copies[4].wait()
    even = lax.rem(lax.axis_index("wrap"), 2) == 0
    edge = H * rows_i
    to_core, to_chip = jnp.where(even, total - edge, 0), jnp.where(even, 0, total - edge)
    for m in range(3):
        core_ref[5 + m] = met_ref[m, aligned(to_core, edge), :]
        chip_ref[5 + m] = met_ref[m, aligned(to_chip, edge), :]
    copies[5].wait()


def early_kernel(dims, kind, kept, state_ref, span_ref, span_met_ref, met_ref, *refs):
    rows_i, height = dims
    if kept:
        metric_i, metric_j, metric_k = refs[:3]
        refs = refs[3:]
    acc_ref, plus_i, minus_i, centre_i, plus_j, minus_j, centre_j, diffused_ref, plus_k, minus_k, centre_k, diffused_k = refs[:12]
    if not kept:
        metric_i, metric_j, metric_k = refs[12:15]
    face_ref = refs[-1]
    diffused_ref[0] = jnp.zeros(diffused_ref.shape[1:], F32)
    diffused_k[0] = jnp.zeros(diffused_k.shape[1:], F32)

    def place(refs, metric_ref, rows, state, prims, row):
        *fluxes, metric = point_fluxes(state, prims, row, metric_ref[rows, :] if kept else None)
        put((*refs, metric_ref), rows, *fluxes, None if kept else metric)

    def planes(n, carry):
        rows = aligned(n * rows_i, rows_i)
        state = [state_ref[f, rows, :] for f in range(5)]
        prims = primitives(state)
        put_diffused(diffused_ref, rows, prims)
        place((plus_i, minus_i, centre_i), metric_i, rows, state, prims, [unit(0, m, met_ref[m, rows, :]) for m in range(3)])
        place((plus_j, minus_j, centre_j), metric_j, rows, state, prims, [unit(1, m, met_ref[3 + m, rows, :]) for m in range(3)])
        return carry

    lax.fori_loop(0, rows_i, planes, 0, unroll=8)

    def spans(n, carry):
        rows = aligned(n * 16, 16)
        state = [span_ref[f, rows, :] for f in range(5)]
        prims = primitives(state)
        put_diffused(diffused_k, rows, prims)
        place((plus_k, minus_k, centre_k), metric_k, rows, state, prims, [unit(2, m, span_met_ref[5 + m, rows, :]) for m in range(3)])
        return carry

    lax.fori_loop(0, height // 2, spans, 0, unroll=8)

    for n in range(2, rows_i - 1):
        low, high = (metric_j[pl.ds(m, rows_i, stride=rows_i), :] for m in (n, n + 1))
        face_ref[n * rows_i : (n + 1) * rows_i, :] = low + high

    def normal(f, carry):
        def rows(n):
            return pl.ds(min(n, rows_i - 1), rows_i, stride=rows_i)

        def store(n, value):
            acc_ref[f, rows(n), :] = value

        for n in range(2):
            store(n, jnp.zeros((rows_i, 128), F32))
        sweep(kind, lambda n: plus_j[f, rows(n), :], lambda n: minus_j[f, rows(n), :], lambda n: centre_j[f, rows(n), :],
              lambda n: diffused_ref[f, rows(n), :], lambda n: face_ref[n * rows_i : (n + 1) * rows_i, :],
              store, 2, rows_i - 1, open_low=True,
              flat=rows_i - 1)
        return carry

    lax.fori_loop(0, 5, normal, 0, unroll=5)


def chord_kernel(dims, kind, state_ref, met_ref, core_ref, chip_ref, met_core_ref, met_chip_ref, normal_ref,
                 plus_i, minus_i, centre_i, metric_i, diffused_ref, acc_ref,
                 halo_plus, halo_minus, halo_centre, halo_metric, halo_diffused, face_ref):
    rows_i, height = dims
    total = rows_i * rows_i
    position, count = lax.axis_index("wrap"), lax.axis_size("wrap")
    even = lax.rem(position, 2) == 0
    at_end = (position == 0) | (position == count - 1)
    halo_diffused[0] = jnp.zeros(halo_diffused.shape[1:], F32)

    core_rows, chip_rows = jnp.where(even, H, 0), jnp.where(even, 0, H)
    own = jnp.where(even, 0, total - rows_i)
    for r in range(H):
        rows = slice(r * rows_i, (r + 1) * rows_i)
        state = [core_ref[f, rows, :] for f in range(5)]
        prims = primitives(state)
        to = aligned((core_rows + r) * rows_i, rows_i)
        put_diffused(halo_diffused, to, prims)
        put((halo_plus, halo_minus, halo_centre, halo_metric), to,
            *point_fluxes(state, prims, [unit(0, m, met_core_ref[5 + m, rows, :]) for m in range(3)]))
        edge = aligned(own, rows_i)
        state = [jnp.where(at_end, state_ref[f, edge, :], chip_ref[f, rows, :]) for f in range(5)]
        row = [jnp.where(at_end, met_ref[m, edge, :], met_chip_ref[5 + m, rows, :]) for m in range(3)]
        prims = primitives(state)
        to = aligned((chip_rows + r) * rows_i, rows_i)
        put_diffused(halo_diffused, to, prims)
        put((halo_plus, halo_minus, halo_centre, halo_metric), to,
            *point_fluxes(state, prims, [unit(0, m, row[m]) for m in range(3)]))

    def loader(ref, halo, lead):
        def load(n):
            if 0 <= n < rows_i:
                return ref[lead + (aligned(n * rows_i, rows_i),)]
            r = n + H if n < 0 else n - rows_i + H
            return halo[lead + (aligned(r * rows_i, rows_i),)]

        return load

    metric = loader(metric_i, halo_metric, ())
    for n in range(-1, rows_i):
        face_ref[(n + 1) * rows_i : (n + 2) * rows_i, :] = metric(n) + metric(n + 1)

    def chord(f, carry):
        def store(n, value):
            rows = aligned(n * rows_i, rows_i)
            acc_ref[f, rows, :] = value + normal_ref[f, rows, :]

        sweep(kind, loader(plus_i, halo_plus, (f,)), loader(minus_i, halo_minus, (f,)), loader(centre_i, halo_centre, (f,)),
              loader(diffused_ref, halo_diffused, (f,)), lambda n: face_ref[(n + 1) * rows_i : (n + 2) * rows_i, :],
              store, -1, rows_i - 1)
        return carry

    lax.fori_loop(0, 5, chord, 0, unroll=5)


def span_kernel(dims, kind, final, *refs):
    rows_i, height = dims
    (span_ref, span_met_ref, span_near_ref, span_far_ref, met_near_ref, met_far_ref, plus_k, minus_k, centre_k, metric_k,
     diffused_k,     partner_hbm, state_ref, met_ref, vol_ref, blank_ref, wake_ref, plane_ref, plus_j, minus_j, centre_j, metric_j,
     diffused_ref) = refs[:23]
    refs = refs[23:]
    if final:
        start_ref, out_ref = refs[:2]
        refs = refs[2:]
    else:
        out_ref, out_span_ref = refs[:2]
        outs, refs = refs[2:7], refs[7:]
    (acc_ref, halo_plus, halo_minus, halo_centre, halo_metric, halo_diffused, pad_ref, wall_ref, sum_ref,
     ghost_plus, ghost_minus, ghost_centre, ghost_metric, ghost_diffused, ghost_ref, partner_ref, sem, face_ref) = refs[:18]
    if final:
        staged_ref, out_sems = refs[18:]
    fetch = pltpu.make_async_copy(partner_hbm, partner_ref, sem)
    fetch.start()
    position, count = lax.axis_index("wrap"), lax.axis_size("wrap")
    ghost_diffused[0] = jnp.zeros(ghost_diffused.shape[1:], F32)
    even = lax.rem(lax.axis_index("span"), 2) == 0
    sublane = lax.broadcasted_iota(jnp.int32, (8, 128), 0)
    halo_diffused[0] = jnp.zeros(halo_diffused.shape[1:], F32)
    for r in range(H):
        for f in range(8):
            near_ref, far_ref = (span_near_ref, span_far_ref) if f < 5 else (met_near_ref, met_far_ref)
            near, far = near_ref[f, 2 * r : 2 * r + 2, :], far_ref[f, 2 * r : 2 * r + 2, :]
            pad_ref[f, r * 8 : r * 8 + 2, :] = jnp.where(even, far, near)
            pad_ref[f, (H + r) * 8 + 6 : (H + r) * 8 + 8, :] = jnp.where(even, near, far)
    for r in range(2 * H):
        rows = slice(r * 8, r * 8 + 8)
        values = []
        for f in range(8):
            ref = span_ref if f < 5 else span_met_ref
            if r < H:
                own = pltpu.roll(ref[f, (height - H + r) * 8 : (height - H + r) * 8 + 8, :], 2, 0)
                values.append(jnp.where(sublane < 2, pad_ref[f, rows, :], own))
            else:
                own = pltpu.roll(ref[f, (r - H) * 8 : (r - H) * 8 + 8, :], 6, 0)
                values.append(jnp.where(sublane >= 6, pad_ref[f, rows, :], own))
        prims = primitives(values[:5])
        put_diffused(halo_diffused, rows, prims)
        put((halo_plus, halo_minus, halo_centre, halo_metric), rows,
            *point_fluxes(values[:5], prims, [unit(2, m, values[5 + m]) for m in range(3)]))

    def loader(ref, halo, lead):
        def one(n):
            if 0 <= n < height:
                return ref[lead + (slice(n * 8, n * 8 + 8),)]
            r = n + H if n < 0 else n - height + H
            return halo[lead + (slice(r * 8, r * 8 + 8),)]

        return lambda n: jnp.concatenate([one(n), one(n + height // 2)], axis=0)

    metric = loader(metric_k, halo_metric, ())
    for n in range(-1, height // 2):
        face_ref[(n + 1) * 16 : (n + 2) * 16, :] = metric(n) + metric(n + 1)

    def sweep_span(f, carry):
        def store(n, value):
            acc_ref[f, n * 8 : n * 8 + 8, :] = value[:8]
            m = n + height // 2
            acc_ref[f, m * 8 : m * 8 + 8, :] = value[8:]

        sweep(kind, loader(plus_k, halo_plus, (f,)), loader(minus_k, halo_minus, (f,)), loader(centre_k, halo_centre, (f,)),
              loader(diffused_k, halo_diffused, (f,)), lambda n: face_ref[(n + 1) * 16 : (n + 2) * 16, :],
              store, -1, height // 2 - 1)
        return carry

    lax.fori_loop(0, 5, sweep_span, 0, unroll=5)

    fetch.wait()
    base = (count - 1 - position) * rows_i
    for i in range(rows_i):
        ghost_ref[i * 16 : i * 16 + 16, :] = wake_ref[aligned((partner_ref[i] - base) * 16, 16), :]
    wall = pl.ds(0, rows_i, stride=rows_i)
    for r in range(H):
        state = [ghost_ref[pl.ds(f * H + r, rows_i, stride=16), :] for f in range(5)]
        prims = primitives(state)
        to = slice(r * rows_i, (r + 1) * rows_i)
        put_diffused(ghost_diffused, to, prims)
        put((ghost_plus, ghost_minus, ghost_centre, ghost_metric), to,
            *point_fluxes(state, prims, [unit(1, m, met_ref[3 + m, wall, :]) for m in range(3)]))

    def normal(f):
        def rows(n):
            return pl.ds(n, rows_i, stride=rows_i)

        def loader(ref, halo, lead):
            def load(n):
                if n >= 0:
                    return ref[lead + (rows(n),)]
                return halo[lead + (aligned((-1 - n) * rows_i, rows_i),)]

            return load

        def store(n, value):
            wall_ref[f, n * rows_i : (n + 1) * rows_i, :] = value

        sweep(kind, loader(plus_j, ghost_plus, (f,)), loader(minus_j, ghost_minus, (f,)),
              loader(centre_j, ghost_centre, (f,)), loader(diffused_ref, ghost_diffused, (f,)),
              lambda n: metric_j[rows(max(n, 0)), :] + metric_j[rows(n + 1), :], store, -1, 1, open_high=True)


    scale = (time_step / 12.0) * blank_ref[...].astype(F32) / vol_ref[...]
    for f in range(5):
        normal(f)
        for half in range(2):
            parts = [acc_ref[f, pl.ds(q * 2 + half, height, stride=8), :] for q in range(4)]
            rows = slice(half * 128, (half + 1) * 128)
            sum_ref[f, rows, :] = plane_ref[f, rows, :] + jnp.concatenate(parts, axis=0).T
        for n in range(H):
            rows = pl.ds(n, rows_i, stride=rows_i)
            sum_ref[f, rows, :] = sum_ref[f, rows, :] + wall_ref[f, n * rows_i : (n + 1) * rows_i, :]
        moved = state_ref[f] + scale * sum_ref[f]
        if final:
            staged_ref[f] = 0.5 * start_ref[f] + 0.5 * moved
            pltpu.make_async_copy(staged_ref.at[f], out_ref.at[f], out_sems.at[f]).start()
        else:
            out_ref[f] = moved
    if final:
        for f in range(5):
            pltpu.make_async_copy(staged_ref.at[f], out_ref.at[f], out_sems.at[f]).wait()
    if not final:
        for f in range(5):
            def store(start, block, f=f):
                out_span_ref[f, pl.ds(start, height, stride=8), :] = block

            to_span(out_ref[f], store, height)
        send_parts(out_ref, out_span_ref, 5, outs, dims)


def shape(*sizes):
    return jax.ShapeDtypeStruct(sizes, F32)


def exchange(sent):
    core, chip, wake, span_near, span_far = sent
    n, s = lax.axis_size("wrap"), lax.axis_size("span")
    cores = [(i, i ^ 1) for i in range(n)]
    chips = [pair for i in range(1, n, 2) for pair in ((i, (i + 1) % n), ((i + 1) % n, i))]
    mirror = [(i, n - 1 - i) for i in range(n)]
    near = [(i, i ^ 1) for i in range(s)]
    far = [pair for i in range(1, s, 2) for pair in ((i, (i + 1) % s), ((i + 1) % s, i))]
    return (lax.ppermute(core, "wrap", cores), lax.ppermute(chip, "wrap", chips), lax.ppermute(wake, "wrap", mirror),
            lax.ppermute(span_near, "span", near), lax.ppermute(span_far, "span", far))


def body(density, velocity, pressure, metrics, volume, wake_partner, iblank):
    rows_i, rows_j, lanes = density.shape
    total, height = rows_i * rows_j, lanes // 4
    dims = (rows_i, height)
    volume, blank = volume.reshape(total, lanes), iblank.reshape(total, lanes)
    whole = pl.BlockSpec(memory_space=pltpu.VMEM)
    far = pl.BlockSpec(memory_space=pltpu.HBM)
    wake_partner = pltpu.with_memory_space_constraint(wake_partner, pltpu.HBM)
    params = pltpu.CompilerParams(vmem_limit_bytes=16 * 2**20)

    def call(kernel, name, ins, outs, scratch, specs=None, cost=0, out_specs=None):
        return pl.pallas_call(
            kernel,
            out_shape=outs,
            in_specs=specs or [whole] * len(ins),
            out_specs=out_specs or [whole] * len(outs),
            scratch_shapes=scratch,
            compiler_params=params,
            cost_estimate=pl.CostEstimate(flops=cost, bytes_accessed=cost // 4, transcendentals=0),
            name=name,
        )(*ins)

    def parts(fields):
        edge = H * rows_j
        return [shape(fields, edge, lanes), shape(fields, edge, lanes), shape(rows_i * 16, lanes),
                shape(fields, 8, lanes), shape(fields, 8, lanes)]

    field, span_rows, halo = shape(5, total, lanes), height * 8, 2 * H * rows_i
    state, span, met, *sent = call(
        functools.partial(prepare_kernel, dims), "prepare",
        [pltpu.with_memory_space_constraint(one, pltpu.HBM) for one in (
            density.reshape(total, lanes), velocity.reshape(3, total, lanes), pressure.reshape(total, lanes),
            metrics.reshape(9, total, lanes))],
        [field, shape(8, total, lanes), shape(9, total, lanes)] + parts(8),
        [pltpu.VMEM((total, lanes), F32), pltpu.VMEM((3, total, lanes), F32), pltpu.VMEM((total, lanes), F32),
         pltpu.SemaphoreType.DMA((6,))],
        [far] * 4,
    )
    span_met = span

    def halo_scratch(rows):
        return [pltpu.VMEM((5, rows, lanes), F32)] * 3 + [pltpu.VMEM((rows, lanes), F32), pltpu.VMEM((5, rows, lanes), F32)]

    faces = [pltpu.VMEM(((rows_i + 1) * rows_i, lanes), F32)]

    metric_halo, kept = None, ()
    start = state
    for final in (False, True):
        kind = jnp.bfloat16 if final else F32
        core, chip, wake, span_near, span_far = exchange(sent)
        if metric_halo is None:
            metric_halo = core, chip, span_near, span_far
        line, span_line = shape(5, total, lanes), shape(5, span_rows, lanes)
        (normal, plus_i, minus_i, centre_i, plus_j, minus_j, centre_j, diffused, plus_k, minus_k, centre_k, diffused_k,
         *squares) = call(
            functools.partial(early_kernel, dims, kind, bool(kept)), "early", (state, span, span_met, met, *kept),
            [field] + [line] * 7 + [span_line] * 4
            + ([] if kept else [shape(total, lanes), shape(total, lanes), shape(span_rows, lanes)]),
            faces, cost=10**8,
        )
        kept = kept or tuple(squares)
        metric_i, metric_j, metric_k = kept
        (plane,) = call(
            functools.partial(chord_kernel, dims, kind), "chord",
            (state, met, core, chip, metric_halo[0], metric_halo[1], normal, plus_i, minus_i, centre_i, metric_i,
             diffused),
            [field], halo_scratch(halo) + faces, cost=10**8,
        )
        ins = (span, span_met, span_near, span_far, metric_halo[2], metric_halo[3], plus_k, minus_k, centre_k, metric_k,
               diffused_k, wake_partner, state, met, volume, blank, wake, plane, plus_j, minus_j, centre_j, metric_j, diffused)
        ins += (start,) if final else ()
        state, *rest = call(
            functools.partial(span_kernel, dims, kind, final), "span", ins,
            [field] if final else [field, field] + parts(5),
            [pltpu.VMEM((5, span_rows, lanes), F32)] + halo_scratch(2 * H * 8) + [pltpu.VMEM((8, 2 * H * 8, lanes), F32)]
            + [pltpu.VMEM((5, H * rows_i, lanes), F32), pltpu.VMEM((5, total, lanes), F32)] + halo_scratch(H * rows_i)
            + [pltpu.VMEM((rows_i * 16, lanes), F32), pltpu.SMEM((rows_i,), jnp.int32), pltpu.SemaphoreType.DMA] + faces
            + ([pltpu.VMEM((5, total, lanes), F32), pltpu.SemaphoreType.DMA((5,))] if final else []),
            [whole] * 11 + [far] + [whole] * (len(ins) - 12),
            cost=10**8, out_specs=[far] if final else None,
        )
        if not final:
            span, *sent = rest
    return state.reshape(5, rows_i, rows_j, lanes)


def solution(mesh):
    placed = (
        P("wrap", None, "span"),
        P(None, "wrap", None, "span"),
        P("wrap", None, "span"),
        P(None, "wrap", None, "span"),
        P("wrap", None, "span"),
        P("wrap"),
        P("wrap", None, "span"),
    )
    return jax.shard_map(
        body, mesh=mesh, in_specs=placed, out_specs=P(None, "wrap", None, "span"), check_vma=False
    )
```
